128 devices in a mesh: ctx: 32 (over x_hi, z, y), wt: 4 (over x_lo, core).
Axes of the slice: x: 4 (x_hi: 2, x_lo: 2; x = x_hi * 2 + x_lo), y: 4, z: 4, core: 2. Of those that a mesh axis runs over, the one named last changes fastest.
Arguments:
- inputs: float32 [8, 4096, 768], P('wt', 'ctx'), may hold values from -6 to 6
- lengths: int32 [8], P('wt'), may hold values from 512 to 4096, as said below
- attend_weight: float32 [768, 2304], P('wt'), may hold values from -0.21875 to 0.21875
- query_bias: float32 [768], P('wt'), may hold values from -3 to 3
- value_bias: float32 [768], P('wt'), may hold values from -0.13258252 to 0.13258252
- output_weight: float32 [768, 768], P('wt'), may hold values from -9.797959 to 9.797959
- output_bias: float32 [768], P('wt'), may hold values from -3 to 3
- norm_gain: float32 [768], P('wt'), may hold values from 0.25 to 1.75
- norm_shift: float32 [768], P('wt'), may hold values from -3 to 3
- expand_weight: float32 [768, 3072], P('wt'), may hold values from -0.21875 to 0.21875
- expand_bias: float32 [3072], P('wt'), may hold values from -3 to 3
- shrink_weight: float32 [3072, 768], P('wt'), may hold values from -0.21875 to 0.21875
- shrink_bias: float32 [768], P('wt'), may hold values from -3 to 3
- final_gain: float32 [768], P('wt'), may hold values from 0.25 to 1.75
- final_shift: float32 [768], P('wt'), may hold values from -3 to 3
- cotangent: float32 [8, 4096, 768], P('wt', 'ctx'), may hold values from -6 to 6
Outputs:
- result: float32 [8, 4096, 768], P('wt', 'ctx')
- input_grad: float32 [8, 4096, 768], P('wt', 'ctx')
- attend_grad: float32 [768, 2304], P('wt')
- query_bias_grad: float32 [768], P('wt')
- value_bias_grad: float32 [768], P('wt')
- output_grad: float32 [768, 768], P('wt')
- output_bias_grad: float32 [768], P('wt')
- norm_gain_grad: float32 [768], P('wt')
- norm_shift_grad: float32 [768], P('wt')
- expand_grad: float32 [768, 3072], P('wt')
- expand_bias_grad: float32 [3072], P('wt')
- shrink_grad: float32 [3072, 768], P('wt')
- shrink_bias_grad: float32 [768], P('wt')
- final_gain_grad: float32 [768], P('wt')
- final_shift_grad: float32 [768], P('wt')
The draws below stay inside these ranges and needn't reach their ends.
Inputs may be any that keep to these rules, and one draw needn't show every extreme that they name: `lengths`: among the 2 sequences held by each index of wt, one, drawn from the seed, is valid at all 4096 positions; among the other sequences, one of the whole batch, drawn from the seed, is valid at exactly one eighth of 4096 positions.
All inputs are finite; a program needn't handle non-finite values.
Results may differ from the reference program's by a relative error of at most 0.03.
Values may be sent and summed in bfloat16 or wider, within the bound.
A program may use at most 320 MiB of HBM per device.

```python
import jax
import jax.numpy as jnp
from jax import lax

D = 768
HEADS = 12
HEAD_DIM = 64
FF = 3072
SEQ_WT = 2
LEN = 4096
SEQS = 8
N_WT = 4


def draw_lengths(key, part):
    key = jax.random.fold_in(key, 7)
    draw_key, pick_key, group_key, slot_key = jax.random.split(key, 4)
    drawn = jax.random.randint(draw_key, (SEQS,), LEN // 8, LEN + 1)
    chosen = jax.random.randint(pick_key, (N_WT,), 0, SEQ_WT)
    indices = jnp.arange(SEQS, dtype=jnp.int32)
    full_slot = jnp.repeat(chosen, SEQ_WT)
    short_group = jax.random.randint(group_key, (), 0, N_WT)
    short_step = jax.random.randint(slot_key, (), 1, SEQ_WT)
    short_slot = (chosen[short_group] + short_step) % SEQ_WT
    short_index = short_group * SEQ_WT + short_slot
    partial_lengths = jnp.where(indices == short_index, LEN // 8, drawn)
    return jnp.where(indices % SEQ_WT == full_slot, LEN, partial_lengths).astype(jnp.int32)


def block_scale(stream_key, dims, pieces, low, high):
    def one(dim, parts):
        draws = jax.random.uniform(jax.random.fold_in(jax.random.fold_in(stream_key, 6), dim), (parts,), jnp.float32, low / len(pieces), high / len(pieces))
        return jnp.repeat(jnp.exp(draws), dims[dim] // parts).reshape((-1,) + (1,) * (len(dims) - dim - 1))

    level = one(*pieces[0])
    for cut in pieces[1:]:
        level = level * one(*cut)
    return level


def gaussian(own_key, dims, width, limit, shards=(), kind=jnp.bfloat16):
    factor_of = block_scale(own_key, dims, shards, -0.22, 0.18) if shards else 1.0
    values = jax.random.normal(own_key, dims, jnp.float32) * width * factor_of
    return jnp.minimum(jnp.maximum(values, -limit), limit).astype(kind)


def setup_inputs(seed: int = 0) -> dict:
    splits = jax.random.split(jax.random.key(seed), 17)
    inputs = gaussian(splits[0], (SEQS, LEN, D), 1.0, 6.0, ((0, 4), (1, 32)), jnp.float32)
    lengths = draw_lengths(jax.random.fold_in(splits[16], 71), 0)
    attend_weight = gaussian(splits[2], (D, 3 * D), D ** -0.5, 0.21875, ((0, 4),), jnp.float32)
    query_bias = gaussian(splits[3], (D,), 0.5, 3.0, ((0, 4),), jnp.float32)
    value_bias = gaussian(splits[4], (D,), ((LEN // 2) ** -0.5), 0.13258252, ((0, 4),), jnp.float32)
    output_weight = gaussian(splits[5], (D, D), ((LEN // 2) ** 0.5 * D ** -0.5), 9.797959, ((0, 4),), jnp.float32)
    output_bias = gaussian(splits[6], (D,), 0.5, 3.0, ((0, 4),), jnp.float32)
    norm_gain = jnp.clip(1.0 + 0.15 * jax.random.normal(splits[7], (D,), jnp.float32), 0.25, 1.75)
    norm_shift = gaussian(splits[8], (D,), 0.5, 3.0, ((0, 4),), jnp.float32)
    expand_weight = gaussian(splits[9], (D, FF), D ** -0.5, 0.21875, ((0, 4),), jnp.float32)
    expand_bias = gaussian(splits[10], (FF,), 0.5, 3.0, ((0, 4),), jnp.float32)
    shrink_weight = gaussian(splits[11], (FF, D), (FF // 4) ** -0.5, 0.21875, ((0, 4),), jnp.float32)
    shrink_bias = gaussian(splits[12], (D,), 0.5, 3.0, ((0, 4),), jnp.float32)
    final_gain = jnp.clip(1.0 + 0.15 * jax.random.normal(splits[13], (D,), jnp.float32), 0.25, 1.75)
    final_shift = gaussian(splits[14], (D,), 0.5, 3.0, ((0, 4),), jnp.float32)
    cotangent = gaussian(splits[15], (SEQS, LEN, D), 1.0, 6.0, ((0, 4), (1, 32)), jnp.float32)
    return {"inputs": inputs, "lengths": lengths, "attend_weight": attend_weight, "query_bias": query_bias, "value_bias": value_bias, "output_weight": output_weight, "output_bias": output_bias, "norm_gain": norm_gain, "norm_shift": norm_shift, "expand_weight": expand_weight, "expand_bias": expand_bias, "shrink_weight": shrink_weight, "shrink_bias": shrink_bias, "final_gain": final_gain, "final_shift": final_shift, "cotangent": cotangent}


norm_eps = 1e-06
masked_score = -1e+30
highest = lax.Precision.HIGHEST

@jax.custom_vjp
def low(v):
    return lax.optimization_barrier(v.astype(jnp.bfloat16)).astype(jnp.float32)

@jax.custom_vjp
def low_back(v):
    return v

def low_keep(v):
    return (low(v), None)

def low_pass(kept, grad):
    return (grad,)

def back_keep(v):
    return (v, None)

def back_low(kept, grad):
    return (low(grad),)
low.defvjp(low_keep, low_pass)
low_back.defvjp(back_keep, back_low)

def layer_norm(values, gain_row, shift_row):
    centered = values - lax.optimization_barrier(jnp.mean(values, axis=-1, keepdims=True))
    variance = lax.optimization_barrier(jnp.mean(centered * centered, axis=-1, keepdims=True))
    return centered * lax.rsqrt(variance + norm_eps) * gain_row + shift_row

def matmul(left_side, right_side):
    return jnp.dot(left_side, right_side, precision=highest)

def sequence_forward(tokens, length, params):
    attend, query_add, value_add, output, output_add, gain_one, shift_one, expand, expand_add, shrink, shrink_add, gain_two, shift_two = params
    model_width = tokens.shape[1]
    query_scale = HEAD_DIM ** (-0.5)
    column_scale = jnp.concatenate([jnp.full((model_width,), query_scale, jnp.float32), jnp.ones((2 * model_width,), jnp.float32)])
    bias_row = jnp.concatenate([query_add, jnp.zeros_like(query_add), value_add])
    packed = low(low_back((matmul(low(tokens), attend) + bias_row) * column_scale))
    query_rows = packed[:, :model_width].reshape(LEN, HEADS, HEAD_DIM)
    key_rows = packed[:, model_width:2 * model_width].reshape(LEN, HEADS, HEAD_DIM)
    value_rows = packed[:, 2 * model_width:].reshape(LEN, HEADS, HEAD_DIM)
    key_mask = jnp.arange(LEN, dtype=jnp.int32) < length
    block_rows = min(512, LEN)

    def attend_block(query_block):
        scores = low_back(jnp.einsum('qhd,khd->hqk', query_block, key_rows, precision=highest))
        scores = jnp.where(key_mask[None, None, :], scores, masked_score)
        soft_weights = low(jax.nn.softmax(scores, axis=-1))
        return jnp.einsum('hqk,khd->qhd', soft_weights, value_rows, precision=highest)
    mixed = lax.map(jax.checkpoint(attend_block), query_rows.reshape(LEN // block_rows, block_rows, HEADS, HEAD_DIM))
    mixed = low(low_back(mixed.reshape(LEN, model_width)))
    attended = low_back(matmul(mixed, output) + output_add)
    normed_one = layer_norm(tokens + attended, gain_one, shift_one)
    raised = low_back(matmul(low(normed_one), expand) + expand_add)
    activated = low(jax.nn.gelu(raised, approximate=False))
    branch = low_back(matmul(activated, shrink) + shrink_add)
    return layer_norm(normed_one + branch, gain_two, shift_two)

def reference(inputs, lengths, attend_weight, query_bias, value_bias, output_weight, output_bias, norm_gain, norm_shift, expand_weight, expand_bias, shrink_weight, shrink_bias, final_gain, final_shift, cotangent):
    weights = (attend_weight, query_bias, value_bias, output_weight, output_bias, norm_gain, norm_shift, expand_weight, expand_bias, shrink_weight, shrink_bias, final_gain, final_shift)

    def forward(tokens_all, params):
        rounded = tuple((low(member) for member in params))
        return lax.map(lambda member: sequence_forward(member[0], member[1], rounded), (tokens_all, lengths))
    result, pullback = jax.vjp(forward, inputs, weights)
    input_grad, weight_grads = pullback(cotangent)
    return (result, input_grad, weight_grads[0], weight_grads[1], weight_grads[2], weight_grads[3], weight_grads[4], weight_grads[5], weight_grads[6], weight_grads[7], weight_grads[8], weight_grads[9], weight_grads[10], weight_grads[11], weight_grads[12])
```

```python
import functools

import jax
import jax.numpy as jnp
from jax import lax
from jax.experimental import pallas as pl
from jax.experimental.pallas import tpu as pltpu
from jax.sharding import PartitionSpec as P

HEADS = 12
HEAD_DIM = 64
LEN = 4096
WIDTH = 768
OWNERS = 32
PAIRS = 24
SPAN = 128
MASKED = -1e30
norm_eps = 1e-06
f32 = jnp.float32
bf16 = jnp.bfloat16
MESH = pl.DeviceIdType.MESH


def layer_norm(values, gain_row, shift_row):
    centered = values - jnp.mean(values, axis=-1, keepdims=True)
    variance = jnp.mean(centered * centered, axis=-1, keepdims=True)
    return centered * lax.rsqrt(variance + norm_eps) * gain_row + shift_row


def norm_pullback(values, gain_row, upstream):
    _, pulled = jax.vjp(lambda inside, scaled: layer_norm(inside, scaled, 0.0), values, gain_row)
    grad_values, grad_gain = pulled(upstream)
    return (grad_values, grad_gain, jnp.sum(upstream, axis=0))


def exact_gelu(values):
    return jax.nn.gelu(values, approximate=False)


def dot(left, right):
    return jnp.dot(left, right, preferred_element_type=f32)


def contract(left, right, left_dim, right_dim):
    return lax.dot_general(
        left, right, (((left_dim,), (right_dim,)), ((), ())), preferred_element_type=f32
    )


def attend_kernel(len_ref, x_ref, o_ref, low_ref, lse_ref, qn, kt, vn, *, q_rows, k_rows):
    valid = len_ref[0]
    lane = lax.broadcasted_iota(jnp.int32, (64, 128), 1)
    first = lax.broadcasted_iota(jnp.int32, (64, 128), 0) == 0
    zero = jnp.zeros((64, 128), f32)
    one_row = jnp.where(first, 1.0, zero)

    @pl.when(valid > 0)
    def _():
        def prepare(c, _):
            here = pl.ds(pl.multiple_of(c * SPAN, SPAN), SPAN)
            qn[here, :] = jnp.concatenate([x_ref[c, 0].astype(f32), one_row], 0).T.astype(bf16)
            vn[here, :] = jnp.concatenate([x_ref[c, 2].astype(f32), one_row], 0).T.astype(bf16)
            kt[0:64, here] = x_ref[c, 1]
            mask = jnp.where(lane + c * SPAN < valid, 0.0, MASKED)
            kt[64:128, here] = jnp.where(first, mask, zero).astype(bf16)
            return 0

        lax.fori_loop(0, OWNERS, prepare, 0)
        k_steps = lax.div(valid + (k_rows - 1), k_rows)

        def q_block(i, _):
            q = qn[pl.ds(pl.multiple_of(i * q_rows, q_rows), q_rows), :]

            def k_block(j, carry):
                peak, acc = carry
                here = pl.ds(pl.multiple_of(j * k_rows, k_rows), k_rows)
                scores = dot(q, kt[:, here])
                folded = scores[:, 0:128]
                for t in range(1, k_rows // 128):
                    folded = jnp.maximum(folded, scores[:, t * 128 : (t + 1) * 128])
                peak_new = jnp.maximum(peak, jnp.max(folded, axis=1, keepdims=True))
                weights = jnp.exp(scores - peak_new).astype(bf16)
                return peak_new, acc * jnp.exp(peak - peak_new) + dot(weights, vn[here, :])

            start = (jnp.full((q_rows, 1), -3e38, f32), jnp.zeros((q_rows, 128), f32))
            peak, acc = lax.fori_loop(0, k_steps, k_block, start)
            total = acc[:, 64:65]
            column = lax.broadcasted_iota(jnp.int32, (q_rows, 128), 1)
            full = jnp.where(column == 64, peak + jnp.log(total), acc / total).T
            for t in range(q_rows // SPAN):
                c = i * (q_rows // SPAN) + t
                cols = slice(t * SPAN, (t + 1) * SPAN)
                o_ref[c] = full[0:64, cols]
                low_ref[c] = full[0:64, cols].astype(bf16)
                lse_ref[c] = full[64:72, cols]
            return 0

        lax.fori_loop(0, LEN // q_rows, q_block, 0)


def attend(valid, packed):
    vmem = pl.BlockSpec(memory_space=pltpu.VMEM)
    return pl.pallas_call(
        functools.partial(attend_kernel, q_rows=512, k_rows=1024),
        out_shape=(
            jax.ShapeDtypeStruct((OWNERS, 64, SPAN), f32),
            jax.ShapeDtypeStruct((OWNERS, 64, SPAN), bf16),
            jax.ShapeDtypeStruct((OWNERS, 8, SPAN), f32),
        ),
        in_specs=[pl.BlockSpec(memory_space=pltpu.SMEM), vmem],
        out_specs=[vmem] * 3,
        scratch_shapes=[
            pltpu.VMEM((LEN, 128), bf16),
            pltpu.VMEM((128, LEN), bf16),
            pltpu.VMEM((LEN, 128), bf16),
        ],
        compiler_params=pltpu.CompilerParams(vmem_limit_bytes=50 << 20),
        name="attend",
    )(valid, packed)


def split_terms(values):
    high = values.astype(bf16).astype(f32)
    rest = values - high
    middle = rest.astype(bf16).astype(f32)
    return high, middle, rest - middle


def attend_back_kernel(
    len_ref, x_ref, o_ref, lse_ref, d_ref, g_ref, qt, qn, kn, kt, vn, dt, dn, dq, *, q_rows, k_rows, streams
):
    valid = len_ref[0]

    @pl.when(valid > 0)
    def _():
        lane = lax.broadcasted_iota(jnp.int32, (64, 128), 1)
        row = lax.broadcasted_iota(jnp.int32, (64, 128), 0)
        zero = jnp.zeros((64, 128), f32)

        def prepare(c, _):
            here = pl.ds(pl.multiple_of(c * SPAN, SPAN), SPAN)
            q = x_ref[c, 0].astype(f32)
            k = x_ref[c, 1].astype(f32)
            v = x_ref[c, 2].astype(f32)
            do = d_ref[c].astype(f32)
            high, middle, rest = split_terms(-lse_ref[c][0:1])
            q_extra = jnp.where(
                row == 0, 1.0, jnp.where(row == 1, high, jnp.where(row == 2, middle, jnp.where(row == 3, rest, 0.0)))
            )
            mask = jnp.where(lane + c * SPAN < valid, 0.0, MASKED)
            k_extra = jnp.where(row == 0, mask, jnp.where(row < 4, 1.0, 0.0))
            qt[:, here] = jnp.concatenate([q, q_extra], 0).astype(bf16)
            qn[here, :] = jnp.concatenate([q, zero], 0).T.astype(bf16)
            kn[here, :] = jnp.concatenate([k, k_extra], 0).T.astype(bf16)
            kt[:, here] = k.astype(bf16)
            delta = jnp.sum(do * o_ref[c], axis=0, keepdims=True)
            high, middle, rest = split_terms(-delta)
            d_extra = jnp.where(row == 0, high, jnp.where(row == 1, middle, jnp.where(row == 2, rest, 0.0)))
            v_extra = jnp.where(row < 3, 1.0, zero)
            dt[:, here] = jnp.concatenate([do, d_extra], 0).astype(bf16)
            dn[here, :] = jnp.concatenate([do, zero], 0).T.astype(bf16)
            vn[here, :] = jnp.concatenate([v, v_extra], 0).T.astype(bf16)
            return 0

        lax.fori_loop(0, OWNERS, prepare, 0)
        dq[...] = jnp.zeros_like(dq)
        k_steps = lax.div(valid + (k_rows - 1), k_rows)
        pieces = k_rows // SPAN

        def k_block(j, _):
            here = pl.ds(pl.multiple_of(j * k_rows, k_rows), k_rows)
            k, v, k_flat = kn[here, :], vn[here, :], kt[:, here]

            def q_block(i, carry):
                dk, dv = carry
                for s in range(streams):
                    cols = pl.ds(pl.multiple_of(i * (q_rows * streams) + s * q_rows, q_rows), q_rows)
                    weights = jnp.exp(dot(k, qt[:, cols]))
                    ds = (weights * dot(v, dt[:, cols])).astype(bf16)
                    dv = dv + dot(weights.astype(bf16), dn[cols, :])
                    dk = dk + dot(ds, qn[cols, :])
                    dq[:, cols] += dot(k_flat, ds)
                return dk, dv

            start = jnp.zeros((k_rows, 128), f32)
            dk, dv = lax.fori_loop(0, LEN // (q_rows * streams), q_block, (start, start))
            for t in range(pieces):
                rows = slice(t * SPAN, (t + 1) * SPAN)
                g_ref[j * pieces + t, 1] = dk[rows].T[0:64].astype(bf16)
                g_ref[j * pieces + t, 2] = dv[rows].T[0:64].astype(bf16)
            return 0

        lax.fori_loop(0, k_steps, k_block, 0)

        def blank(j, _):
            for t in range(pieces):
                g_ref[j * pieces + t, 1] = jnp.zeros((64, 128), bf16)
                g_ref[j * pieces + t, 2] = jnp.zeros((64, 128), bf16)
            return 0

        lax.fori_loop(k_steps, LEN // k_rows, blank, 0)

        def finish(c, _):
            rounded = dq[:, pl.ds(pl.multiple_of(c * SPAN, SPAN), SPAN)].astype(bf16)
            g_ref[c, 0] = (rounded.astype(f32) * HEAD_DIM ** (-0.5)).astype(bf16)
            return 0

        lax.fori_loop(0, OWNERS, finish, 0)


def attend_back(valid, packed, mixed, lse, grad_mixed):
    vmem = pl.BlockSpec(memory_space=pltpu.VMEM)
    return pl.pallas_call(
        functools.partial(attend_back_kernel, q_rows=512, k_rows=512, streams=2),
        out_shape=jax.ShapeDtypeStruct((OWNERS, 3, 64, SPAN), bf16),
        in_specs=[pl.BlockSpec(memory_space=pltpu.SMEM)] + [vmem] * 4,
        out_specs=vmem,
        scratch_shapes=[
            pltpu.VMEM((128, LEN), bf16),
            pltpu.VMEM((LEN, 128), bf16),
            pltpu.VMEM((LEN, 128), bf16),
            pltpu.VMEM((64, LEN), bf16),
            pltpu.VMEM((LEN, 128), bf16),
            pltpu.VMEM((128, LEN), bf16),
            pltpu.VMEM((LEN, 128), bf16),
            pltpu.VMEM((64, LEN), f32),
        ],
        compiler_params=pltpu.CompilerParams(vmem_limit_bytes=50 << 20),
        name="attend_back",
    )(valid, packed, mixed, lse, grad_mixed)


def greet_owners(me):
    barrier = pltpu.get_barrier_semaphore()

    def greet(s, _):
        pl.semaphore_signal(barrier, 1, device_id={"ctx": lax.rem(me + s, OWNERS)}, device_id_type=MESH)
        return 0

    lax.fori_loop(1, OWNERS, greet, 0)
    pl.semaphore_wait(barrier, OWNERS - 1)


def token_slice(ref, pair):
    lanes = pl.ds(pl.multiple_of((pair // HEADS) * SPAN, SPAN), SPAN)
    if len(ref.shape) == 4:
        return ref.at[:, pair % HEADS, :, lanes]
    return ref.at[pair % HEADS, :, lanes]


def to_heads_kernel(src, dst, send_sem, recv_sem, local_sem):
    me = lax.axis_index("ctx")
    greet_owners(me)

    def copy(s):
        peer = lax.rem(me + s, OWNERS)
        pair = jnp.minimum(peer, PAIRS - 1)
        return peer, pltpu.make_async_remote_copy(
            token_slice(src, pair), dst.at[me], send_sem.at[s], recv_sem.at[s],
            device_id={"ctx": peer}, device_id_type=MESH,
        )

    def start(s, _):
        peer, moved = copy(s)

        @pl.when(peer < PAIRS)
        def _():
            moved.start()

        return 0

    lax.fori_loop(1, OWNERS, start, 0)

    @pl.when(me < PAIRS)
    def _():
        own = pltpu.make_async_copy(token_slice(src, jnp.minimum(me, PAIRS - 1)), dst.at[me], local_sem)
        own.start()
        own.wait()

    def finish(s, _):
        peer, moved = copy(s)

        @pl.when(peer < PAIRS)
        def _():
            moved.wait_send()

        @pl.when(me < PAIRS)
        def _():
            moved.wait_recv()

        return 0

    lax.fori_loop(1, OWNERS, finish, 0)


def to_tokens_kernel(src, dst, send_sem, recv_sem, local_sem):
    me = lax.axis_index("ctx")
    greet_owners(me)
    pair = jnp.minimum(me, PAIRS - 1)

    def copy(s):
        peer = lax.rem(me + s, OWNERS)
        return pltpu.make_async_remote_copy(
            src.at[peer], token_slice(dst, pair), send_sem.at[s], recv_sem.at[s],
            device_id={"ctx": peer}, device_id_type=MESH,
        )

    @pl.when(me < PAIRS)
    def _():
        def start(s, _):
            copy(s).start()
            return 0

        lax.fori_loop(1, OWNERS, start, 0)
        own = pltpu.make_async_copy(src.at[me], token_slice(dst, pair), local_sem)
        own.start()
        own.wait()

    def finish(s, _):
        @pl.when(me < PAIRS)
        def _():
            copy(s).wait_send()

        @pl.when(lax.rem(me + OWNERS - s, OWNERS) < PAIRS)
        def _():
            copy(s).wait_recv()

        return 0

    lax.fori_loop(1, OWNERS, finish, 0)


def exchange(kernel, values, out_shape, collective_id, name):
    anywhere = pl.BlockSpec(memory_space=pl.ANY)
    return pl.pallas_call(
        kernel,
        out_shape=jax.ShapeDtypeStruct(out_shape, bf16),
        in_specs=[anywhere],
        out_specs=anywhere,
        scratch_shapes=[
            pltpu.SemaphoreType.DMA((OWNERS,)),
            pltpu.SemaphoreType.DMA((OWNERS,)),
            pltpu.SemaphoreType.DMA(()),
        ],
        compiler_params=pltpu.CompilerParams(collective_id=collective_id, has_side_effects=True),
        name=name,
    )(values)


def place():
    ctx, wt = lax.axis_index("ctx"), lax.axis_index("wt")
    return dict(
        x_hi=ctx // 16, z=(ctx // 4) % 4, y=ctx % 4, x_lo=wt // 2, core=wt % 2, x=(ctx // 16) * 2 + wt // 2
    )


def device_at(here, **change):
    at = dict(here)
    if "x" in change:
        at["x_hi"], at["x_lo"] = change["x"] // 2, change["x"] % 2
        change = {k: v for k, v in change.items() if k != "x"}
    at.update(change)
    return (at["x_hi"] * 16 + at["z"] * 4 + at["y"], at["x_lo"] * 2 + at["core"])


def greet_all(devices):
    barrier = pltpu.get_barrier_semaphore()
    for device in devices:
        pl.semaphore_signal(barrier, 1, device_id=device, device_id_type=MESH)
    pl.semaphore_wait(barrier, len(devices))


def weights_kernel(count, *refs):
    shards, fulls = refs[:count], refs[count : 2 * count]
    send_sem, recv_sem, local_sem = refs[2 * count :]
    here = place()
    partner = device_at(here, core=1 - here["core"])
    ahead = device_at(here, x=(here["x"] + 1) % 4)
    behind = device_at(here, x=(here["x"] + 3) % 4)
    greet_all([partner, ahead, behind])
    mine = here["x_lo"] * 2 + here["core"]
    far = (1 - here["x_lo"]) * 2 + here["core"]

    def remote(src, dst, slot, n, device):
        return pltpu.make_async_remote_copy(
            src, dst, send_sem.at[slot, n], recv_sem.at[slot, n], device_id=device, device_id_type=MESH
        )

    sent, forwarded, local = [], [], []
    for n in range(count):
        rows = shards[n].shape[0]
        half = rows // 2

        def part(ref, owner, h, half=half, rows=rows):
            return ref.at[pl.ds(pl.multiple_of(owner * rows + h * half, 16), half), :]

        first = remote(shards[n].at[pl.ds(0, half), :], part(fulls[n], mine, 0), 0, n, ahead)
        second = remote(shards[n].at[pl.ds(half, half), :], part(fulls[n], mine, 1), 1, n, behind)
        whole = fulls[n].at[pl.ds(pl.multiple_of(mine * rows, 16), rows), :]
        across = remote(shards[n], whole, 2, n, partner)
        for copy in (first, second, across):
            copy.start()
        own = pltpu.make_async_copy(shards[n], whole, local_sem.at[n])
        own.start()
        local.append(own)
        sent.append((first, second, across))
        forwarded.append([remote(part(fulls[n], far, h), part(fulls[n], far, h), 3 + h, n, partner) for h in (0, 1)])
    for n in range(count):
        for h in (0, 1):
            sent[n][h].wait_recv()
            forwarded[n][h].start()
    for n in range(count):
        local[n].wait()
        for copy in sent[n]:
            copy.wait_send()
        sent[n][2].wait_recv()
        for copy in forwarded[n]:
            copy.wait()


def gather_weights(shards, collective_id):
    anywhere = pl.BlockSpec(memory_space=pl.ANY)
    count = len(shards)
    return pl.pallas_call(
        functools.partial(weights_kernel, count),
        out_shape=tuple(jax.ShapeDtypeStruct((4 * s.shape[0], s.shape[1]), s.dtype) for s in shards),
        in_specs=[anywhere] * count,
        out_specs=[anywhere] * count,
        scratch_shapes=[
            pltpu.SemaphoreType.DMA((5, count)),
            pltpu.SemaphoreType.DMA((5, count)),
            pltpu.SemaphoreType.DMA((count,)),
        ],
        compiler_params=pltpu.CompilerParams(collective_id=collective_id, has_side_effects=True),
        name="gather_weights",
    )(*shards)


ORDERS = (("y", "z", "x"), ("z", "x", "y"), ("x", "y", "z"))


def reduce_kernel(
    rows, src, out, own, other, s1, s2, s3, r1, r2, r3,
    core_send, core_recv, own_sem, send_sem, recv_sem, gather_send, gather_recv,
):
    here = place()
    partner = device_at(here, core=1 - here["core"])
    peers = {
        axis: [device_at(here, **{axis: (here[axis] + d) % 4}) for d in (1, 2, 3)] for axis in ("x", "y", "z")
    }
    opposite = 1 - here["x_hi"]
    greet_all([partner] + peers["x"] + peers["y"] + peers["z"])
    core = here["core"]

    def band(p):
        return pl.ds(p * rows, rows)

    core_copies, own_copies = [], []
    for p in range(3):
        for lo in range(2):
            moved = pltpu.make_async_remote_copy(
                src.at[lo, 1 - core, :, :, :, band(p), :], other.at[p, lo], core_send.at[p, lo], core_recv.at[p, lo],
                device_id=partner, device_id_type=MESH,
            )
            kept = pltpu.make_async_copy(src.at[lo, core, :, :, :, band(p), :], own.at[p, lo], own_sem.at[p, lo])
            moved.start()
            kept.start()
            core_copies.append(moved)
            own_copies.append(kept)

    def slot(p, stage, d):
        return (p * 3 + stage) * 3 + d

    def chunk_index(axis_list, axis, value):
        index = []
        for name in axis_list:
            if name == "x":
                index += [value % 2, value // 2] if axis == "x" else [slice(None), slice(None)]
            else:
                index.append(value if axis == name else slice(None))
        return tuple(index)

    def scatter(p, stage, source, axes, landing):
        axis = ORDERS[p][stage]
        copies = []
        for d in (1, 2, 3):
            target = (here[axis] + d) % 4
            moved = pltpu.make_async_remote_copy(
                source.at[chunk_index(axes, axis, target)], landing.at[d - 1],
                send_sem.at[slot(p, stage, d - 1)], recv_sem.at[slot(p, stage, d - 1)],
                device_id=peers[axis][d - 1], device_id_type=MESH,
            )
            moved.start()
            copies.append(moved)
        return copies

    def sums(p, stage, source, axes, landing, target):
        axis = ORDERS[p][stage]
        kept = source.at[chunk_index(axes, axis, here[axis])]
        lead = target.shape[:-2]
        total = 1
        for size in lead:
            total *= size

        def step(n, _):
            index, left = [], n
            for size in reversed(lead):
                index.insert(0, left % size)
                left = left // size
            index = tuple(index)
            value = kept[index].astype(f32)
            for d in range(3):
                value = value + landing[(d,) + index].astype(f32)
            target[index] = value.astype(bf16)
            return 0

        if lead:
            lax.fori_loop(0, total, step, 0)
        else:
            value = kept[...].astype(f32)
            for d in range(3):
                value = value + landing[d].astype(f32)
            target[...] = value.astype(bf16)

    left_axes = []
    for p in range(3):
        axes = ["x", "z", "y"]
        left = [list(axes)]
        for axis in ORDERS[p]:
            axes.remove(axis)
            left.append(list(axes))
        left_axes.append(left)

    in_flight = [None] * 3
    for p in range(3):
        for lo in range(2):
            own_copies[2 * p + lo].wait()
            core_copies[2 * p + lo].wait_recv()

        def add(n, _, p=p):
            lo, hi, z, y = n // 32, (n // 16) % 2, (n // 4) % 4, n % 4
            index = (p, lo, hi, z, y)
            own[index] = (own[index].astype(f32) + other[index].astype(f32)).astype(bf16)
            return 0

        lax.fori_loop(0, 64, add, 0)
        in_flight[p] = scatter(p, 0, own.at[p], left_axes[p][0], r1[p])
    waits = []
    stages = ((own, r1, s1), (None, r2, s2), (None, r3, s3))
    for stage in range(3):
        for p in range(3):
            source = own.at[p] if stage == 0 else (s1[p] if stage == 1 else s2[p])
            landing = (r1, r2, r3)[stage][p]
            target = (s1, s2, s3)[stage][p]
            for moved in in_flight[p]:
                moved.wait_recv()
            waits += in_flight[p]
            if stage < 2:
                sums(p, stage, source, left_axes[p][stage], landing, target)
                in_flight[p] = scatter(p, stage + 1, target, left_axes[p][stage + 1], (r1, r2, r3)[stage + 1][p])
            else:
                final = out.at[here["x_hi"], here["z"], here["y"], band(p), :]
                sums(p, stage, source, left_axes[p][stage], landing, final)

    def spread(p, stage):
        axis = ORDERS[p][2 - stage]
        done = [ORDERS[p][2 - k] for k in range(stage)]
        index = tuple(
            slice(None) if name in done else here["x_hi" if name == "x" else name] for name in ("x", "z", "y")
        )
        piece = out.at[index + (band(p), slice(None))]
        if axis == "x":
            targets = [device_at(here, x_hi=opposite)]
        else:
            targets = peers[axis]
        copies = []
        for d, device in enumerate(targets):
            moved = pltpu.make_async_remote_copy(
                piece, piece, gather_send.at[slot(p, stage, d)], gather_recv.at[slot(p, stage, d)],
                device_id=device, device_id_type=MESH,
            )
            moved.start()
            copies.append(moved)
        return copies

    for stage in range(3):
        for p in range(3):
            if stage:
                for moved in in_flight[p]:
                    moved.wait_recv()
                waits += in_flight[p]
            in_flight[p] = spread(p, stage)
    for p in range(3):
        for moved in in_flight[p]:
            moved.wait_recv()
        waits += in_flight[p]
    for moved in waits + core_copies:
        moved.wait_send()


def reduce_gradients(values, rows, collective_id):
    def stage_shapes(lead):
        out = []
        for p in range(3):
            axes = ["x", "z", "y"]
            for axis in ORDERS[p][:lead]:
                axes.remove(axis)
            shape = []
            for name in axes:
                shape += [2, 2] if name == "x" else [4]
            out.append(tuple(shape) + (rows, 128))
        return out

    after = [stage_shapes(n) for n in (1, 2, 3)]
    scratch = [pltpu.VMEM((3, 2, 2, 4, 4, rows, 128), bf16), pltpu.VMEM((3, 2, 2, 4, 4, rows, 128), bf16)]
    for shapes in after[:2]:
        scratch += [pltpu.VMEM(shape, bf16) for shape in shapes]
    for shapes in after:
        scratch += [pltpu.VMEM((3,) + shape, bf16) for shape in shapes]
    scratch += [
        pltpu.SemaphoreType.DMA((3, 2)), pltpu.SemaphoreType.DMA((3, 2)), pltpu.SemaphoreType.DMA((3, 2)),
        pltpu.SemaphoreType.DMA((27,)), pltpu.SemaphoreType.DMA((27,)),
        pltpu.SemaphoreType.DMA((27,)), pltpu.SemaphoreType.DMA((27,)),
    ]

    def kernel(src, out, own, other, a0, a1, a2, b0, b1, b2, c0, c1, c2, d0, d1, d2, e0, e1, e2, *sems):
        reduce_kernel(
            rows, src, out, own, other, (a0, a1, a2), (b0, b1, b2), (None,) * 3,
            (c0, c1, c2), (d0, d1, d2), (e0, e1, e2), *sems,
        )

    return pl.pallas_call(
        kernel,
        out_shape=jax.ShapeDtypeStruct((2, 4, 4, 3 * rows, 128), bf16),
        in_specs=[pl.BlockSpec(memory_space=pl.ANY)],
        out_specs=pl.BlockSpec(memory_space=pltpu.VMEM),
        scratch_shapes=scratch,
        compiler_params=pltpu.CompilerParams(
            collective_id=collective_id, has_side_effects=True, vmem_limit_bytes=50 << 20
        ),
        name="reduce_gradients",
    )(values)


def columns_out(matrix):
    rows, width = matrix.shape
    blocks = matrix.astype(bf16).reshape(4, rows // 4, width // 128, 128)
    return jnp.transpose(blocks, (0, 2, 1, 3)).reshape(4, -1, 128)


def columns_in(flat, rows, width):
    blocks = flat.astype(f32).reshape(width // 128, rows, 128)
    return jnp.transpose(blocks, (1, 0, 2)).reshape(rows, width)


def per_device(
    inputs, lengths, attend_weight, query_bias, value_bias, output_weight, output_bias, norm_gain, norm_shift,
    expand_weight, expand_bias, shrink_weight, shrink_bias, final_gain, final_shift, cotangent,
):
    ctx, wt = lax.axis_index("ctx"), lax.axis_index("wt")
    vectors = (
        query_bias, value_bias, output_bias, norm_gain, norm_shift, expand_bias, shrink_bias, final_gain, final_shift,
    )
    small = jnp.concatenate([v.astype(bf16) for v in vectors] + [jnp.zeros((32 * 128 - 2304,), bf16)]).reshape(32, 128)
    attend_full, small_full, output_full, expand_full, shrink_full = gather_weights(
        (attend_weight.astype(bf16), small, output_weight.astype(bf16), expand_weight.astype(bf16),
         shrink_weight.astype(bf16)), 0,
    )
    small_full = small_full.reshape(4, 32 * 128).astype(f32)
    unpacked, offset = [], 0
    for v in vectors:
        unpacked.append(small_full[:, offset : offset + v.shape[0]].reshape(-1))
        offset += v.shape[0]
    query_add, value_add, output_add, gain_one, shift_one, expand_add, shrink_add, gain_two, shift_two = unpacked

    seq_count, tok_local, model_width = inputs.shape
    row_count = seq_count * tok_local
    tokens = inputs.reshape(row_count, model_width)
    tokens_low = tokens.astype(bf16)
    column_scale = jnp.concatenate(
        [jnp.full((model_width,), HEAD_DIM ** (-0.5), f32), jnp.ones((2 * model_width,), f32)]
    )
    bias = jnp.concatenate([query_add, jnp.zeros_like(query_add), value_add])
    packed = ((contract(attend_full, tokens_low, 0, 1) + bias[:, None]) * column_scale[:, None]).astype(bf16)
    held = exchange(to_heads_kernel, packed.reshape(3, HEADS, 64, row_count), (OWNERS, 3, 64, SPAN), 1, "to_heads")
    my_length = jnp.where(ctx < HEADS, lengths[0], lengths[1])
    my_length = jnp.where(ctx < PAIRS, my_length, 0).astype(jnp.int32).reshape(1)
    mixed_heads, mixed_heads_low, lse = attend(my_length, held)
    mixed_low = exchange(
        to_tokens_kernel, mixed_heads_low, (HEADS, 64, row_count), 2, "mixed_to_tokens"
    ).reshape(model_width, row_count)

    attended = contract(mixed_low, output_full, 0, 0) + output_add
    hidden_one = tokens + attended
    normed_one = layer_norm(hidden_one, gain_one, shift_one)
    normed_low = normed_one.astype(bf16)
    raised = dot(normed_low, expand_full) + expand_add
    activated = exact_gelu(raised).astype(bf16)
    branch = dot(activated, shrink_full) + shrink_add
    hidden_two = normed_one + branch
    result = layer_norm(hidden_two, gain_two, shift_two)

    upstream = cotangent.reshape(row_count, model_width)
    grad_two, final_gain_term, final_shift_term = norm_pullback(hidden_two, gain_two, upstream)
    branch_low = grad_two.astype(bf16)
    shrink_bias_term = jnp.sum(branch_low.astype(f32), axis=0)
    shrink_term = contract(activated, branch_low, 0, 0)
    grad_active = contract(branch_low, shrink_full, 1, 1)
    _, gelu_pull = jax.vjp(exact_gelu, raised)
    raised_low = gelu_pull(grad_active)[0].astype(bf16)
    expand_bias_term = jnp.sum(raised_low.astype(f32), axis=0)
    expand_term = contract(normed_low, raised_low, 0, 0)
    grad_normed = grad_two + contract(raised_low, expand_full, 1, 1)
    grad_one, norm_gain_term, norm_shift_term = norm_pullback(hidden_one, gain_one, grad_normed)
    attended_low = grad_one.astype(bf16)
    output_bias_term = jnp.sum(attended_low.astype(f32), axis=0)
    output_term = dot(mixed_low, attended_low)
    grad_mixed = contract(output_full, attended_low, 1, 1).astype(bf16)

    grad_heads = exchange(
        to_heads_kernel, grad_mixed.reshape(HEADS, 64, row_count), (OWNERS, 64, SPAN), 3, "grad_to_heads"
    )
    grad_held = attend_back(my_length, held, mixed_heads, lse, grad_heads)
    grad_packed = exchange(
        to_tokens_kernel, grad_held, (3, HEADS, 64, row_count), 4, "grad_to_tokens"
    ).reshape(3 * model_width, row_count)
    attend_term = contract(tokens_low, grad_packed, 0, 1)
    input_grad = grad_one + contract(grad_packed, attend_full, 0, 1)
    query_bias_term = jnp.sum(grad_packed[:model_width].astype(f32), axis=1)
    value_bias_term = jnp.sum(grad_packed[2 * model_width :].astype(f32), axis=1)

    packed_terms = jnp.concatenate(
        [columns_out(m) for m in (output_term, expand_term, shrink_term, attend_term)], axis=1
    )
    total = packed_terms.shape[1]
    reduced = reduce_gradients(
        packed_terms.reshape(2, 2, 2, 4, 4, total // 32, 128), total // 96, 5
    ).reshape(total, 128)
    grads, offset = [], 0
    for rows, width in ((192, 768), (192, 3072), (768, 768), (192, 2304)):
        count = rows * width // 128
        grads.append(columns_in(reduced[offset : offset + count], rows, width))
        offset += count
    output_grad, expand_grad, shrink_grad, attend_grad = grads

    early = lax.psum(
        jnp.concatenate(
            [t.reshape(4, -1) for t in (
                output_bias_term, norm_gain_term, norm_shift_term, expand_bias_term, shrink_bias_term,
                final_gain_term, final_shift_term)], axis=1,
        ), ("ctx", "wt"),
    )
    late = lax.psum(
        jnp.concatenate([t.reshape(4, -1) for t in (query_bias_term, value_bias_term)], axis=1), ("ctx", "wt")
    )
    early = lax.dynamic_index_in_dim(early, wt, 0, keepdims=False)
    late = lax.dynamic_index_in_dim(late, wt, 0, keepdims=False)
    n = 192
    return (
        result.reshape(inputs.shape),
        input_grad.reshape(inputs.shape),
        attend_grad,
        late[:n],
        late[n:],
        output_grad,
        early[0:n],
        early[n : 2 * n],
        early[2 * n : 3 * n],
        expand_grad,
        early[3 * n : 7 * n],
        shrink_grad,
        early[7 * n : 8 * n],
        early[8 * n : 9 * n],
        early[9 * n : 10 * n],
    )


def solution(mesh):
    wide, rows, flat = P("wt", "ctx", None), P("wt", None), P("wt")
    return jax.shard_map(
        per_device,
        mesh=mesh,
        in_specs=(
            wide, flat, rows, flat, flat, rows, flat, flat, flat, rows, flat, rows, flat, flat, flat, wide,
        ),
        out_specs=(
            wide, wide, rows, flat, flat, rows, flat, flat, flat, rows, flat, rows, flat, flat, flat,
        ),
        check_vma=False,
    )
```

```python
import functools

import jax
import jax.numpy as jnp
from jax import lax
from jax.experimental import pallas as pl
from jax.experimental.pallas import tpu as pltpu
from jax.sharding import PartitionSpec as P

HEADS = 12
HEAD_DIM = 64
LEN = 4096
WIDTH = 768
OWNERS = 32
PAIRS = 24
VMEM_BYTES = 58 << 20
SPAN = 128
MASKED = -1e30
norm_eps = 1e-06
f32 = jnp.float32
bf16 = jnp.bfloat16
MESH = pl.DeviceIdType.MESH


def layer_norm(values, gain_row, shift_row):
    centered = values - jnp.mean(values, axis=-1, keepdims=True)
    variance = jnp.mean(centered * centered, axis=-1, keepdims=True)
    return centered * lax.rsqrt(variance + norm_eps) * gain_row + shift_row


def norm_pullback(values, gain_row, upstream):
    _, pulled = jax.vjp(lambda inside, scaled: layer_norm(inside, scaled, 0.0), values, gain_row)
    grad_values, grad_gain = pulled(upstream)
    return (grad_values, grad_gain, jnp.sum(upstream, axis=0))


def exact_gelu(values):
    return jax.nn.gelu(values, approximate=False)


def dot(left, right):
    return jnp.dot(left, right, preferred_element_type=f32)


def contract(left, right, left_dim, right_dim):
    return lax.dot_general(
        left, right, (((left_dim,), (right_dim,)), ((), ())), preferred_element_type=f32
    )


def head_of(ctx):
    z, y = (ctx // 4) % 4, ctx % 4
    turn = lax.rem(y + 7 - z, 4)
    return ctx // 16, 3 * z + jnp.minimum(turn, 2), turn < 3


def greet_owners(me):
    barrier = pltpu.get_barrier_semaphore()

    def greet(s, _):
        pl.semaphore_signal(barrier, 1, device_id={"ctx": lax.rem(me + s, OWNERS)}, device_id_type=MESH)
        return 0

    lax.fori_loop(1, OWNERS, greet, 0)
    pl.semaphore_wait(barrier, OWNERS - 1)


def token_slice(ref, ctx):
    seq, head, _ = head_of(ctx)
    lanes = pl.ds(pl.multiple_of(seq * SPAN, SPAN), SPAN)
    if len(ref.shape) == 4:
        return ref.at[:, head, :, lanes]
    return ref.at[head, :, lanes]


def to_heads_kernel(src, dst, send_sem, recv_sem, local_sem):
    me = lax.axis_index("ctx")
    greet_owners(me)
    holds = head_of(me)[2]

    def copy(s):
        peer = lax.rem(me + s, OWNERS)
        return head_of(peer)[2], pltpu.make_async_remote_copy(
            token_slice(src, peer), dst.at[me], send_sem.at[s], recv_sem.at[s],
            device_id={"ctx": peer}, device_id_type=MESH,
        )

    def start(s, _):
        wanted, moved = copy(s)

        @pl.when(wanted)
        def _():
            moved.start()

        return 0

    lax.fori_loop(1, OWNERS, start, 0)

    @pl.when(holds)
    def _():
        own = pltpu.make_async_copy(token_slice(src, me), dst.at[me], local_sem)
        own.start()
        own.wait()

    def finish(s, _):
        wanted, moved = copy(s)

        @pl.when(wanted)
        def _():
            moved.wait_send()

        @pl.when(holds)
        def _():
            moved.wait_recv()

        return 0

    lax.fori_loop(1, OWNERS, finish, 0)


def to_tokens_kernel(src, dst, send_sem, recv_sem, local_sem):
    me = lax.axis_index("ctx")
    greet_owners(me)
    holds = head_of(me)[2]

    def copy(s):
        peer = lax.rem(me + s, OWNERS)
        return pltpu.make_async_remote_copy(
            src.at[peer], token_slice(dst, me), send_sem.at[s], recv_sem.at[s],
            device_id={"ctx": peer}, device_id_type=MESH,
        )

    @pl.when(holds)
    def _():
        def start(s, _):
            copy(s).start()
            return 0

        lax.fori_loop(1, OWNERS, start, 0)
        own = pltpu.make_async_copy(src.at[me], token_slice(dst, me), local_sem)
        own.start()
        own.wait()

    def finish(s, _):
        @pl.when(holds)
        def _():
            copy(s).wait_send()

        @pl.when(head_of(lax.rem(me + OWNERS - s, OWNERS))[2])
        def _():
            copy(s).wait_recv()

        return 0

    lax.fori_loop(1, OWNERS, finish, 0)


def exchange(kernel, values, out_shape, collective_id, name):
    anywhere = pl.BlockSpec(memory_space=pl.ANY)
    return pl.pallas_call(
        kernel,
        out_shape=jax.ShapeDtypeStruct(out_shape, bf16),
        in_specs=[anywhere],
        out_specs=anywhere,
        scratch_shapes=[
            pltpu.SemaphoreType.DMA((OWNERS,)),
            pltpu.SemaphoreType.DMA((OWNERS,)),
            pltpu.SemaphoreType.DMA(()),
        ],
        compiler_params=pltpu.CompilerParams(collective_id=collective_id, has_side_effects=True),
        name=name,
    )(values)


def place():
    ctx, wt = lax.axis_index("ctx"), lax.axis_index("wt")
    return dict(
        x_hi=ctx // 16, z=(ctx // 4) % 4, y=ctx % 4, x_lo=wt // 2, core=wt % 2, x=(ctx // 16) * 2 + wt // 2
    )


def device_at(here, **change):
    at = dict(here)
    if "x" in change:
        at["x_hi"], at["x_lo"] = change["x"] // 2, change["x"] % 2
        change = {k: v for k, v in change.items() if k != "x"}
    at.update(change)
    return (at["x_hi"] * 16 + at["z"] * 4 + at["y"], at["x_lo"] * 2 + at["core"])


def greet_all(devices):
    barrier = pltpu.get_barrier_semaphore()
    for device in devices:
        pl.semaphore_signal(barrier, 1, device_id=device, device_id_type=MESH)
    pl.semaphore_wait(barrier, len(devices))


class WeightGather:
    def __init__(self, here, shards, fulls, send_sem, recv_sem, local_sem):
        self.partner = device_at(here, core=1 - here["core"])
        self.ahead = device_at(here, x=(here["x"] + 1) % 4)
        self.behind = device_at(here, x=(here["x"] + 3) % 4)
        self.mine = here["x_lo"] * 2 + here["core"]
        self.far = (1 - here["x_lo"]) * 2 + here["core"]
        self.shards, self.fulls = shards, fulls
        self.sems = send_sem, recv_sem, local_sem

    def neighbours(self):
        return [self.partner, self.ahead, self.behind]

    def remote(self, src, dst, slot, n, device):
        return pltpu.make_async_remote_copy(
            src, dst, self.sems[0].at[slot, n], self.sems[1].at[slot, n], device_id=device, device_id_type=MESH
        )

    def start(self):
        self.sent, self.local, self.handed = [], [], []
        for n, (shard, full) in enumerate(zip(self.shards, self.fulls)):
            rows = shard.shape[0]
            half = rows // 2

            def part(owner, h, full=full, rows=rows, half=half):
                return full.at[pl.ds(pl.multiple_of(owner * rows + h * half, 16), half), :]

            whole = full.at[pl.ds(pl.multiple_of(self.mine * rows, 16), rows), :]
            copies = [
                self.remote(shard.at[pl.ds(0, half), :], part(self.mine, 0), 0, n, self.ahead),
                self.remote(shard.at[pl.ds(half, half), :], part(self.mine, 1), 1, n, self.behind),
                self.remote(shard, whole, 2, n, self.partner),
            ]
            own = pltpu.make_async_copy(shard, whole, self.sems[2].at[n])
            for copy in copies + [own]:
                copy.start()
            self.sent.append(copies)
            self.local.append(own)
            self.handed.append(
                [self.remote(part(self.far, h), part(self.far, h), 3 + h, n, self.partner) for h in (0, 1)]
            )

    def hand_on(self, n):
        for h in (0, 1):
            self.sent[n][h].wait_recv()
            self.handed[n][h].start()

    def finish(self):
        for copies, own, handed in zip(self.sent, self.local, self.handed):
            own.wait()
            for copy in copies:
                copy.wait_send()
            copies[2].wait_recv()
            for copy in handed:
                copy.wait()


def first_weights_kernel(weight, *refs):
    vectors, (full, small_full, low, small, small_low, send_sem, recv_sem, local_sem) = refs[:9], refs[9:]
    here = place()
    gather = WeightGather(here, (low, small_low), (full, small_full), send_sem, recv_sem, local_sem)
    low[...] = weight[...].astype(bf16)
    small[...] = jnp.zeros_like(small)
    for n, vector in enumerate(vectors):
        small[n : n + 1, 0 : vector.shape[1]] = vector[...]
    small_low[...] = small[...].astype(bf16)
    greet_all(gather.neighbours())
    gather.start()
    gather.hand_on(0)
    gather.hand_on(1)
    gather.finish()


def first_weights(weight, vectors, collective_id):
    vmem, anywhere = pl.BlockSpec(memory_space=pltpu.VMEM), pl.BlockSpec(memory_space=pl.ANY)
    rows, width = weight.shape
    return pl.pallas_call(
        first_weights_kernel,
        out_shape=(jax.ShapeDtypeStruct((4 * rows, width), bf16), jax.ShapeDtypeStruct((128, 768), bf16)),
        in_specs=[vmem] * 10,
        out_specs=[anywhere] * 2,
        scratch_shapes=[
            pltpu.VMEM((rows, width), bf16), pltpu.VMEM((32, 768), f32), pltpu.VMEM((32, 768), bf16),
            pltpu.SemaphoreType.DMA((5, 2)), pltpu.SemaphoreType.DMA((5, 2)), pltpu.SemaphoreType.DMA((2,)),
        ],
        compiler_params=pltpu.CompilerParams(
            collective_id=collective_id, has_side_effects=True, vmem_limit_bytes=VMEM_BYTES
        ),
        name="first_weights",
    )(weight, *[v.reshape(1, -1) for v in vectors])


def attend_kernel(
    len_ref, x_ref, w0, w1, w2, o_ref, low_ref, lse_ref, f0, f1, f2, qn, kt, vn, b0, b1, b2,
    send_sem, recv_sem, local_sem, *, q_rows, k_rows,
):
    valid = len_ref[0]
    gather = WeightGather(place(), (b0, b1, b2), (f0, f1, f2), send_sem, recv_sem, local_sem)
    for low, wide in ((b0, w0), (b1, w1), (b2, w2)):
        low[...] = wide[...].astype(bf16)
    greet_all(gather.neighbours())
    gather.start()
    lane = lax.broadcasted_iota(jnp.int32, (64, 128), 1)
    first = lax.broadcasted_iota(jnp.int32, (64, 128), 0) == 0
    zero = jnp.zeros((64, 128), f32)
    one_row = jnp.where(first, 1.0, zero)

    def prepare(c, _):
        here = pl.ds(pl.multiple_of(c * SPAN, SPAN), SPAN)
        qn[here, :] = jnp.concatenate([x_ref[c, 0].astype(f32), one_row], 0).T.astype(bf16)
        vn[here, :] = jnp.concatenate([x_ref[c, 2].astype(f32), one_row], 0).T.astype(bf16)
        kt[0:64, here] = x_ref[c, 1]
        mask = jnp.where(lane + c * SPAN < valid, 0.0, MASKED)
        kt[64:128, here] = jnp.where(first, mask, zero).astype(bf16)
        return 0

    lax.fori_loop(0, OWNERS, prepare, 0)

    def q_block(i, _):
        q = qn[pl.ds(pl.multiple_of(i * q_rows, q_rows), q_rows), :]

        def k_block(j, carry):
            peak, acc = carry
            here = pl.ds(pl.multiple_of(j * k_rows, k_rows), k_rows)
            scores = dot(q, kt[:, here])
            folded = scores[:, 0:128]
            for t in range(1, k_rows // 128):
                folded = jnp.maximum(folded, scores[:, t * 128 : (t + 1) * 128])
            peak_new = jnp.maximum(peak, jnp.max(folded, axis=1, keepdims=True))
            weights = jnp.exp(scores - peak_new).astype(bf16)
            return peak_new, acc * jnp.exp(peak - peak_new) + dot(weights, vn[here, :])

        start = (jnp.full((q_rows, 1), -3e38, f32), jnp.zeros((q_rows, 128), f32))
        peak, acc = lax.fori_loop(0, LEN // k_rows, k_block, start)
        total = acc[:, 64:65]
        column = lax.broadcasted_iota(jnp.int32, (q_rows, 128), 1)
        full = jnp.where(column == 64, peak + jnp.log(total), acc / total).T
        for t in range(q_rows // SPAN):
            c = i * (q_rows // SPAN) + t
            cols = slice(t * SPAN, (t + 1) * SPAN)
            o_ref[c] = full[0:64, cols]
            low_ref[c] = full[0:64, cols].astype(bf16)
            lse_ref[c] = full[64:72, cols]
        return 0

    steps = LEN // q_rows
    cuts = (0, steps // 2, steps - 2, steps)
    for n in range(3):
        lax.fori_loop(cuts[n], cuts[n + 1], q_block, 0)
        gather.hand_on(n)
    gather.finish()


def attend(valid, packed, shards, collective_id):
    vmem, anywhere = pl.BlockSpec(memory_space=pltpu.VMEM), pl.BlockSpec(memory_space=pl.ANY)
    return pl.pallas_call(
        functools.partial(attend_kernel, q_rows=512, k_rows=1024),
        out_shape=(
            jax.ShapeDtypeStruct((OWNERS, 64, SPAN), f32),
            jax.ShapeDtypeStruct((OWNERS, 64, SPAN), bf16),
            jax.ShapeDtypeStruct((OWNERS, 8, SPAN), f32),
        ) + tuple(jax.ShapeDtypeStruct((4 * s.shape[0], s.shape[1]), bf16) for s in shards),
        in_specs=[pl.BlockSpec(memory_space=pltpu.SMEM)] + [vmem] * 4,
        out_specs=[vmem] * 3 + [anywhere] * 3,
        scratch_shapes=[
            pltpu.VMEM((LEN, 128), bf16),
            pltpu.VMEM((128, LEN), bf16),
            pltpu.VMEM((LEN, 128), bf16),
        ] + [pltpu.VMEM(s.shape, bf16) for s in shards] + [
            pltpu.SemaphoreType.DMA((5, 3)), pltpu.SemaphoreType.DMA((5, 3)), pltpu.SemaphoreType.DMA((3,)),
        ],
        compiler_params=pltpu.CompilerParams(
            collective_id=collective_id, has_side_effects=True, vmem_limit_bytes=VMEM_BYTES
        ),
        name="attend",
    )(valid, packed, *shards)


def split_terms(values):
    high = values.astype(bf16).astype(f32)
    rest = values - high
    middle = rest.astype(bf16).astype(f32)
    return high, middle, rest - middle


def attend_back_body(
    len_ref, x_ref, o_ref, lse_ref, d_ref, g_ref, qt, qn, kn, kt, vn, dt, dn, dq, *, q_rows, k_rows, streams, after
):
    valid = len_ref[0]
    lane = lax.broadcasted_iota(jnp.int32, (64, 128), 1)
    row = lax.broadcasted_iota(jnp.int32, (64, 128), 0)
    zero = jnp.zeros((64, 128), f32)

    def prepare(c, _):
        here = pl.ds(pl.multiple_of(c * SPAN, SPAN), SPAN)
        q = x_ref[c, 0].astype(f32)
        k = x_ref[c, 1].astype(f32)
        v = x_ref[c, 2].astype(f32)
        do = d_ref[c].astype(f32)
        high, middle, rest = split_terms(-lse_ref[c][0:1])
        q_extra = jnp.where(
            row == 0, 1.0, jnp.where(row == 1, high, jnp.where(row == 2, middle, jnp.where(row == 3, rest, 0.0)))
        )
        mask = jnp.where(lane + c * SPAN < valid, 0.0, MASKED)
        k_extra = jnp.where(row == 0, mask, jnp.where(row < 4, 1.0, 0.0))
        qt[:, here] = jnp.concatenate([q, q_extra], 0).astype(bf16)
        qn[here, :] = jnp.concatenate([q, zero], 0).T.astype(bf16)
        kn[here, :] = jnp.concatenate([k, k_extra], 0).T.astype(bf16)
        kt[:, here] = k.astype(bf16)
        delta = jnp.sum(do * o_ref[c], axis=0, keepdims=True)
        high, middle, rest = split_terms(-delta)
        d_extra = jnp.where(row == 0, high, jnp.where(row == 1, middle, jnp.where(row == 2, rest, 0.0)))
        v_extra = jnp.where(row < 3, 1.0, zero)
        dt[:, here] = jnp.concatenate([do, d_extra], 0).astype(bf16)
        dn[here, :] = jnp.concatenate([do, zero], 0).T.astype(bf16)
        vn[here, :] = jnp.concatenate([v, v_extra], 0).T.astype(bf16)
        return 0

    lax.fori_loop(0, OWNERS, prepare, 0)
    dq[...] = jnp.zeros_like(dq)
    pieces = k_rows // SPAN

    def k_block(j, _):
        here = pl.ds(pl.multiple_of(j * k_rows, k_rows), k_rows)
        k, v, k_flat = kn[here, :], vn[here, :], kt[:, here]

        def q_block(i, carry):
            dk, dv = carry
            for s in range(streams):
                cols = pl.ds(pl.multiple_of(i * (q_rows * streams) + s * q_rows, q_rows), q_rows)
                weights = jnp.exp(dot(k, qt[:, cols]))
                ds = (weights * dot(v, dt[:, cols])).astype(bf16)
                dv = dv + dot(weights.astype(bf16), dn[cols, :])
                dk = dk + dot(ds, qn[cols, :])
                dq[:, cols] += dot(k_flat, ds)
            return dk, dv

        start = jnp.zeros((k_rows, 128), f32)
        dk, dv = lax.fori_loop(0, LEN // (q_rows * streams), q_block, (start, start))
        for t in range(pieces):
            rows = slice(t * SPAN, (t + 1) * SPAN)
            g_ref[j * pieces + t, 1] = dk[rows].T[0:64].astype(bf16)
            g_ref[j * pieces + t, 2] = dv[rows].T[0:64].astype(bf16)
        return 0

    begin = 0
    for end, event in after:
        lax.fori_loop(begin, end, k_block, 0)
        event()
        begin = end

    def finish(c, _):
        rounded = dq[:, pl.ds(pl.multiple_of(c * SPAN, SPAN), SPAN)].astype(bf16)
        g_ref[c, 0] = (rounded.astype(f32) * HEAD_DIM ** (-0.5)).astype(bf16)
        return 0

    lax.fori_loop(0, OWNERS, finish, 0)


ORDERS = (("y", "z", "x"), ("z", "x", "y"), ("x", "y", "z"))
LEAD = ("x", "z", "y")
STAGES = ("y", "z", "x")


def axes_after(p, count):
    return [a for a in LEAD if a not in ORDERS[p][:count]]


def shape_after(p, count, width):
    shape = []
    for name in axes_after(p, count):
        shape += [2, 2] if name == "x" else [4]
    return tuple(shape) + (16, width)


def total_shape(width):
    return (2, 4, 4, 48, width)


class Reduce:
    def __init__(self, here, width, halves, merge, unpack, small, scratch):
        self.here, self.width, self.merge, self.unpack, self.small = here, width, merge, unpack, small
        self.halves = halves
        (self.acc, self.out, self.sums, self.landing, self.hall,
         self.core_send, self.core_recv, self.own_sem, self.send_sem, self.recv_sem,
         self.back_send, self.back_recv, self.small_send, self.small_recv) = scratch
        self.partner = device_at(here, core=1 - here["core"])
        self.peers = {
            axis: [device_at(here, **{axis: (here[axis] + d) % 4}) for d in (1, 2, 3)] for axis in STAGES
        }
        self.waits = []
        self.flying = [[], [], []]

    @staticmethod
    def scratch(width, halves, small_rows):
        shapes = []
        for shape in halves:
            shapes += [pltpu.VMEM((3, 2) + shape, bf16)] * 2
        shapes += [pltpu.VMEM(shape_after(p, 0, width), bf16) for p in range(3)]
        shapes.append(pltpu.VMEM(total_shape(width), bf16))
        for count in (1, 2):
            shapes += [pltpu.VMEM(shape_after(p, count, width), bf16) for p in range(3)]
        for count in (1, 2, 3):
            shapes += [pltpu.VMEM((3,) + shape_after(p, count, width), bf16) for p in range(3)]
        shapes.append(pltpu.VMEM((4, 4, small_rows, 128), f32))
        count = 3 * 2 * len(halves)
        shapes += [pltpu.SemaphoreType.DMA((count,))] * 3
        shapes += [pltpu.SemaphoreType.DMA((27,))] * 4
        shapes += [pltpu.SemaphoreType.DMA((12,))] * 2
        return shapes

    @staticmethod
    def unflatten(refs, tensors):
        refs = list(refs)
        pairs = [(refs[2 * n], refs[2 * n + 1]) for n in range(tensors)]
        refs = refs[2 * tensors :]
        acc, out, refs = refs[:3], refs[3], refs[4:]
        sums = [refs[0:3], refs[3:6]]
        landing = [refs[6:9], refs[9:12], refs[12:15]]
        return pairs, [acc, out, sums, landing] + refs[15:]

    def neighbours(self):
        return [self.partner] + [device for axis in STAGES for device in self.peers[axis]]

    def remote(self, src, dst, sems, slot, device):
        copy = pltpu.make_async_remote_copy(
            src, dst, sems[0].at[slot], sems[1].at[slot], device_id=device, device_id_type=MESH
        )
        copy.start()
        self.waits.append(copy)
        return copy

    def start(self):
        core = self.here["core"]
        self.core_copies = [[], [], []]
        slot = 0
        for p in range(3):
            for source, own, other in self.halves:
                for lo in range(2):
                    moved = self.remote(
                        source.at[lo, 1 - core, p], other.at[p, lo], (self.core_send, self.core_recv), slot,
                        self.partner,
                    )
                    kept = pltpu.make_async_copy(source.at[lo, core, p], own.at[p, lo], self.own_sem.at[slot])
                    kept.start()
                    self.core_copies[p].append((moved, kept))
                    slot += 1
        self.small_stage(0, self.small[...])

    def small_stage(self, stage, value):
        axis = STAGES[stage] if stage < 3 else "core"
        mine = self.hall.at[stage, self.here[axis]]
        mine[...] = value
        devices = self.peers[axis] if stage < 3 else [self.partner]
        self.small_flying = [
            self.remote(mine, mine, (self.small_send, self.small_recv), 3 * stage + d, device)
            for d, device in enumerate(devices)
        ]

    def small_sum(self, stage):
        for copy in self.small_flying:
            copy.wait_recv()
        value = self.hall[stage, 0]
        for n in range(1, 4 if stage < 3 else 2):
            value = value + self.hall[stage, n]
        return value

    def index(self, axes, axis, value):
        index = []
        for name in axes:
            if name == "x":
                index += [value % 2, value // 2] if axis == "x" else [slice(None), slice(None)]
            else:
                index.append(value if axis == name else slice(None))
        return tuple(index)

    def scatter(self, p, stage, source):
        axis, axes = ORDERS[p][stage], axes_after(p, stage)
        self.flying[p] = [
            self.remote(
                source.at[self.index(axes, axis, (self.here[axis] + d) % 4)], self.landing[stage][p].at[d - 1],
                (self.send_sem, self.recv_sem), (p * 3 + stage) * 3 + d - 1, self.peers[axis][d - 1],
            )
            for d in (1, 2, 3)
        ]

    def begin(self, p):
        for moved, kept in self.core_copies[p]:
            moved.wait_recv()
            kept.wait()
        self.merge(p, self.acc[p])
        self.scatter(p, 0, self.acc[p])

    def advance(self, p, stage):
        axis, axes = ORDERS[p][stage], axes_after(p, stage)
        source = self.acc[p] if stage == 0 else self.sums[stage - 1][p]
        kept = source.at[self.index(axes, axis, self.here[axis])]
        landing = self.landing[stage][p]
        for copy in self.flying[p]:
            copy.wait_recv()
        if stage < 2:
            target = self.sums[stage][p]
        else:
            target = self.out.at[self.here["x_hi"], self.here["z"], self.here["y"], pl.ds(16 * p, 16), :]
        lead = target.shape[:-2]
        total = 1
        for size in lead:
            total *= size

        def step(n, _):
            index, left = [], n
            for size in reversed(lead):
                index.insert(0, left % size)
                left = left // size
            index = tuple(index)
            value = kept[index].astype(f32)
            for d in range(3):
                value = value + landing[(d,) + index].astype(f32)
            target[index] = value.astype(bf16)
            return 0

        if lead:
            lax.fori_loop(0, total, step, 0)
            self.scatter(p, stage + 1, target)
        else:
            value = kept[...].astype(f32)
            for d in range(3):
                value = value + landing[d].astype(f32)
            target[...] = value.astype(bf16)
            self.spread(p, 0)

    def spread(self, p, stage):
        if stage:
            for copy in self.flying[p]:
                copy.wait_recv()
        if stage == 3:
            return
        axis = ORDERS[p][2 - stage]
        done = [ORDERS[p][2 - k] for k in range(stage)]
        index = tuple(
            slice(None) if name in done else self.here["x_hi" if name == "x" else name] for name in LEAD
        )
        piece = self.out.at[index + (pl.ds(16 * p, 16), slice(None))]
        devices = [device_at(self.here, x_hi=1 - self.here["x_hi"])] if axis == "x" else self.peers[axis]
        self.flying[p] = [
            self.remote(piece, piece, (self.back_send, self.back_recv), (p * 3 + stage) * 3 + d, device)
            for d, device in enumerate(devices)
        ]

    def step(self, number):
        for p in range(3):
            if number == 0:
                self.begin(p)
            elif number <= 3:
                self.advance(p, number - 1)
            else:
                self.spread(p, number - 3)
        if 1 <= number <= 3:
            self.small_stage(number, self.small_sum(number - 1))
        elif number == 4:
            self.small[...] = self.small_sum(3)

    def finish(self):
        self.unpack(self.out)
        for copy in self.waits:
            copy.wait_send()


def merge_blocks(p, pairs, acc, blocks):
    def step(n, _):
        lo, z = n // 4, n % 4

        def load(tensor, index):
            own, other = pairs[tensor]
            index = (p, lo, z) + index
            return own[index].astype(f32) + other[index].astype(f32)

        for (hi, y, left), value in blocks(load):
            acc[lo, hi, z, y, :, left : left + value.shape[1]] = value.astype(bf16)
        return 0

    lax.fori_loop(0, 8, step, 0)


def cut(value):
    return [value[:, n * 384 : (n + 1) * 384] for n in range(value.shape[1] // 384)]


def early_blocks(load):
    wide = cut(load(0, ()))
    found = [((n // 4, n % 4, 0), value) for n, value in enumerate(wide)]
    for y in range(4):
        found += [((hi, y, 384), value) for hi, value in enumerate(cut(load(1, (y,))))]
    return found


def late_blocks(load):
    pieces = cut(load(0, ())) + cut(load(1, ()))
    return [((n // 4, n % 4, 0), value) for n, value in enumerate(pieces)]


def early_unpack(expand_out, shrink_out):
    def unpack(out):
        def step(n, _):
            p, z = n // 4, n % 4
            band = pl.ds(pl.multiple_of(p * 16, 16), 16)
            rows = pl.ds(pl.multiple_of(n * 16, 16), 16)
            for hi in range(2):
                for y in range(4):
                    value = out[hi, z, y, band, :].astype(f32)
                    left = hi * 1536 + y * 384
                    expand_out[rows, left : left + 384] = value[:, 0:384]
                    below = pl.ds(pl.multiple_of(n * 64 + y * 16, 16), 16)
                    shrink_out[below, hi * 384 : hi * 384 + 384] = value[:, 384:768]
            return 0

        lax.fori_loop(0, 12, step, 0)

    return unpack


def late_unpack(output_out, attend_out):
    def unpack(out):
        def step(n, _):
            p, z = n // 4, n % 4
            band = pl.ds(pl.multiple_of(p * 16, 16), 16)
            rows = pl.ds(pl.multiple_of(n * 16, 16), 16)
            for m in range(8):
                value = out[m // 4, z, m % 4, band, :].astype(f32)
                if m < 2:
                    output_out[rows, m * 384 : m * 384 + 384] = value
                else:
                    attend_out[rows, (m - 2) * 384 : (m - 1) * 384] = value
            return 0

        lax.fori_loop(0, 12, step, 0)

    return unpack


EARLY_HALVES = ((4, 16, 3072), (4, 4, 16, 768))
LATE_HALVES = ((4, 16, 768), (4, 16, 2304))


def attend_back_kernel(
    len_ref, x_ref, o_ref, lse_ref, d_ref, expand_src, shrink_src, small_src,
    g_ref, expand_out, shrink_out, small_out, *refs,
):
    attention, refs = refs[:8], refs[8:]
    pairs, scratch = Reduce.unflatten(refs, 2)
    small_out[...] = small_src[...]
    reduce = Reduce(
        place(), 768, [(source, *pair) for source, pair in zip((expand_src, shrink_src), pairs)],
        lambda p, acc: merge_blocks(p, pairs, acc, early_blocks), early_unpack(expand_out, shrink_out),
        small_out, scratch,
    )
    greet_all(reduce.neighbours())
    reduce.start()
    after = ((1, 0), (5, 1), (6, 2), (7, 3), (8, 4))
    attend_back_body(
        len_ref, x_ref, o_ref, lse_ref, d_ref, g_ref, *attention, q_rows=512, k_rows=512, streams=2,
        after=[(end, functools.partial(reduce.step, number)) for end, number in after],
    )
    reduce.step(5)
    reduce.step(6)
    reduce.finish()


def attend_back(valid, packed, mixed, lse, grad_mixed, expand_term, shrink_term, small, collective_id):
    vmem, anywhere = pl.BlockSpec(memory_space=pltpu.VMEM), pl.BlockSpec(memory_space=pl.ANY)
    return pl.pallas_call(
        attend_back_kernel,
        out_shape=(
            jax.ShapeDtypeStruct((OWNERS, 3, 64, SPAN), bf16),
            jax.ShapeDtypeStruct((192, 3072), f32),
            jax.ShapeDtypeStruct((768, 768), f32),
            jax.ShapeDtypeStruct(small.shape, f32),
        ),
        in_specs=[pl.BlockSpec(memory_space=pltpu.SMEM)] + [vmem] * 4 + [anywhere] * 2 + [vmem],
        out_specs=[vmem] * 4,
        scratch_shapes=[
            pltpu.VMEM((128, LEN), bf16),
            pltpu.VMEM((LEN, 128), bf16),
            pltpu.VMEM((LEN, 128), bf16),
            pltpu.VMEM((64, LEN), bf16),
            pltpu.VMEM((LEN, 128), bf16),
            pltpu.VMEM((128, LEN), bf16),
            pltpu.VMEM((LEN, 128), bf16),
            pltpu.VMEM((64, LEN), f32),
        ] + Reduce.scratch(768, EARLY_HALVES, small.shape[0]),
        compiler_params=pltpu.CompilerParams(
            collective_id=collective_id, has_side_effects=True, vmem_limit_bytes=VMEM_BYTES
        ),
        name="attend_back",
    )(
        valid, packed, mixed, lse, grad_mixed, expand_term.reshape(2, 2, 3, 4, 16, 3072),
        shrink_term.reshape(2, 2, 3, 4, 4, 16, 768), small,
    )


def late_kernel(output_src, attend_src, small_src, output_out, attend_out, small_out, *refs):
    pairs, scratch = Reduce.unflatten(refs, 2)
    small_out[...] = small_src[...]
    reduce = Reduce(
        place(), 384, [(source, *pair) for source, pair in zip((output_src, attend_src), pairs)],
        lambda p, acc: merge_blocks(p, pairs, acc, late_blocks), late_unpack(output_out, attend_out),
        small_out, scratch,
    )
    greet_all(reduce.neighbours())
    reduce.start()
    for number in range(7):
        reduce.step(number)
    reduce.finish()


def late_reduce(output_term, attend_term, small, collective_id):
    vmem, anywhere = pl.BlockSpec(memory_space=pltpu.VMEM), pl.BlockSpec(memory_space=pl.ANY)
    return pl.pallas_call(
        late_kernel,
        out_shape=(
            jax.ShapeDtypeStruct((192, 768), f32),
            jax.ShapeDtypeStruct((192, 2304), f32),
            jax.ShapeDtypeStruct(small.shape, f32),
        ),
        in_specs=[anywhere] * 2 + [vmem],
        out_specs=[vmem] * 3,
        scratch_shapes=Reduce.scratch(384, LATE_HALVES, small.shape[0]),
        compiler_params=pltpu.CompilerParams(
            collective_id=collective_id, has_side_effects=True, vmem_limit_bytes=VMEM_BYTES
        ),
        name="late_reduce",
    )(output_term.reshape(2, 2, 3, 4, 16, 768), attend_term.reshape(2, 2, 3, 4, 16, 2304), small)


def per_device(
    inputs, lengths, attend_weight, query_bias, value_bias, output_weight, output_bias, norm_gain, norm_shift,
    expand_weight, expand_bias, shrink_weight, shrink_bias, final_gain, final_shift, cotangent,
):
    ctx, wt = lax.axis_index("ctx"), lax.axis_index("wt")
    vectors = (
        query_bias, value_bias, output_bias, norm_gain, norm_shift, expand_bias, shrink_bias, final_gain, final_shift,
    )
    attend_full, small_full = first_weights(attend_weight, vectors, 0)
    small_full = small_full.reshape(4, 32, 768).astype(f32)
    query_add, value_add, output_add, gain_one, shift_one, expand_add, shrink_add, gain_two, shift_two = [
        small_full[:, n, : v.shape[0]].reshape(-1) for n, v in enumerate(vectors)
    ]

    seq_count, tok_local, model_width = inputs.shape
    row_count = seq_count * tok_local
    tokens = inputs.reshape(row_count, model_width)
    tokens_low = tokens.astype(bf16)
    column_scale = jnp.concatenate(
        [jnp.full((model_width,), HEAD_DIM ** (-0.5), f32), jnp.ones((2 * model_width,), f32)]
    )
    bias = jnp.concatenate([query_add, jnp.zeros_like(query_add), value_add])
    packed = ((contract(attend_full, tokens_low, 0, 1) + bias[:, None]) * column_scale[:, None]).astype(bf16)
    held = exchange(to_heads_kernel, packed.reshape(3, HEADS, 64, row_count), (OWNERS, 3, 64, SPAN), 1, "to_heads")
    seq, _, holds = head_of(ctx)
    my_length = jnp.where(holds, lengths[seq], 0).astype(jnp.int32).reshape(1)
    mixed_heads, mixed_heads_low, lse, output_full, expand_full, shrink_full = attend(
        my_length, held, (output_weight, expand_weight, shrink_weight), 6
    )
    mixed_low = exchange(
        to_tokens_kernel, mixed_heads_low, (HEADS, 64, row_count), 2, "mixed_to_tokens"
    ).reshape(model_width, row_count)

    attended = contract(mixed_low, output_full, 0, 0) + output_add
    hidden_one = tokens + attended
    normed_one = layer_norm(hidden_one, gain_one, shift_one)
    normed_low = normed_one.astype(bf16)
    raised = dot(normed_low, expand_full) + expand_add
    activated = exact_gelu(raised).astype(bf16)
    branch = dot(activated, shrink_full) + shrink_add
    hidden_two = normed_one + branch
    result = layer_norm(hidden_two, gain_two, shift_two)

    upstream = cotangent.reshape(row_count, model_width)
    grad_two, final_gain_term, final_shift_term = norm_pullback(hidden_two, gain_two, upstream)
    branch_low = grad_two.astype(bf16)
    shrink_bias_term = jnp.sum(branch_low.astype(f32), axis=0)
    shrink_term = contract(activated, branch_low, 0, 0)
    grad_active = contract(branch_low, shrink_full, 1, 1)
    _, gelu_pull = jax.vjp(exact_gelu, raised)
    raised_low = gelu_pull(grad_active)[0].astype(bf16)
    expand_bias_term = jnp.sum(raised_low.astype(f32), axis=0)
    expand_term = contract(normed_low, raised_low, 0, 0)
    grad_normed = grad_two + contract(raised_low, expand_full, 1, 1)
    grad_one, norm_gain_term, norm_shift_term = norm_pullback(hidden_one, gain_one, grad_normed)
    attended_low = grad_one.astype(bf16)
    output_bias_term = jnp.sum(attended_low.astype(f32), axis=0)
    output_term = dot(mixed_low, attended_low)
    grad_mixed = contract(output_full, attended_low, 1, 1).astype(bf16)

    grad_heads = exchange(
        to_heads_kernel, grad_mixed.reshape(HEADS, 64, row_count), (OWNERS, 64, SPAN), 3, "grad_to_heads"
    )
    early = jnp.concatenate(
        [t.reshape(4, -1) for t in (
            output_bias_term, norm_gain_term, norm_shift_term, expand_bias_term, shrink_bias_term,
            final_gain_term, final_shift_term)] + [jnp.zeros((4, 128), f32)], axis=1,
    ).reshape(64, 128)
    grad_held, expand_grad, shrink_grad, early = attend_back(
        my_length, held, mixed_heads, lse, grad_heads, expand_term.astype(bf16), shrink_term.astype(bf16), early, 5
    )
    grad_packed = exchange(
        to_tokens_kernel, grad_held, (3, HEADS, 64, row_count), 4, "grad_to_tokens"
    ).reshape(3 * model_width, row_count)
    attend_term = contract(tokens_low, grad_packed, 0, 1)
    input_grad = grad_one + contract(grad_packed, attend_full, 0, 1)
    query_bias_term = jnp.sum(grad_packed[:model_width].astype(f32), axis=1)
    value_bias_term = jnp.sum(grad_packed[2 * model_width :].astype(f32), axis=1)

    late = jnp.concatenate(
        [t.reshape(4, -1) for t in (query_bias_term, value_bias_term)] + [jnp.zeros((4, 128), f32)], axis=1
    ).reshape(16, 128)
    output_grad, attend_grad, late = late_reduce(output_term.astype(bf16), attend_term.astype(bf16), late, 7)
    early = lax.dynamic_index_in_dim(early.reshape(4, 2048), wt, 0, keepdims=False)
    late = lax.dynamic_index_in_dim(late.reshape(4, 512), wt, 0, keepdims=False)
    n = 192
    return (
        result.reshape(inputs.shape),
        input_grad.reshape(inputs.shape),
        attend_grad,
        late[:n],
        late[n : 2 * n],
        output_grad,
        early[0:n],
        early[n : 2 * n],
        early[2 * n : 3 * n],
        expand_grad,
        early[3 * n : 7 * n],
        shrink_grad,
        early[7 * n : 8 * n],
        early[8 * n : 9 * n],
        early[9 * n : 10 * n],
    )


def solution(mesh):
    wide, rows, flat = P("wt", "ctx", None), P("wt", None), P("wt")
    return jax.shard_map(
        per_device,
        mesh=mesh,
        in_specs=(
            wide, flat, rows, flat, flat, rows, flat, flat, flat, rows, flat, rows, flat, flat, flat, wide,
        ),
        out_specs=(
            wide, wide, rows, flat, flat, rows, flat, flat, flat, rows, flat, rows, flat, flat, flat,
        ),
        check_vma=False,
    )
```

```python
import functools

import jax
import jax.numpy as jnp
from jax import lax
from jax.experimental import pallas as pl
from jax.experimental.pallas import tpu as pltpu
from jax.sharding import PartitionSpec as P

HEADS = 12
HEAD_DIM = 64
LEN = 4096
WIDTH = 768
OWNERS = 32
PAIRS = 24
VMEM_BYTES = 58 << 20
SPAN = 128
MASKED = -1e30
norm_eps = 1e-06
f32 = jnp.float32
bf16 = jnp.bfloat16
MESH = pl.DeviceIdType.MESH


def layer_norm(values, gain_row, shift_row):
    centered = values - jnp.mean(values, axis=-1, keepdims=True)
    variance = jnp.mean(centered * centered, axis=-1, keepdims=True)
    return centered * lax.rsqrt(variance + norm_eps) * gain_row + shift_row


def norm_pullback(values, gain_row, upstream):
    _, pulled = jax.vjp(lambda inside, scaled: layer_norm(inside, scaled, 0.0), values, gain_row)
    grad_values, grad_gain = pulled(upstream)
    return (grad_values, grad_gain, jnp.sum(upstream, axis=0))


def exact_gelu(values):
    return jax.nn.gelu(values, approximate=False)


def dot(left, right):
    return jnp.dot(left, right, preferred_element_type=f32)


def contract(left, right, left_dim, right_dim):
    return lax.dot_general(
        left, right, (((left_dim,), (right_dim,)), ((), ())), preferred_element_type=f32
    )


def head_of(ctx):
    z, y = lax.rem(lax.div(ctx, 4), 4), lax.rem(ctx, 4)
    turn = lax.rem(y + 7 - z, 4)
    return lax.div(ctx, 16), 3 * z + jnp.minimum(turn, 2), turn < 3


def token_slice(ref, ctx, *lead):
    seq, head, _ = head_of(ctx)
    return ref.at[lead + (head, slice(None), pl.ds(pl.multiple_of(seq * SPAN, SPAN), SPAN))]


def wait_bytes(ref, sem):
    pltpu.make_async_copy(ref, ref, sem).wait()


class Exchange:
    def __init__(self, send_sem, recv_sem):
        self.me = lax.axis_index("ctx")
        self.holds = head_of(self.me)[2]
        self.send_sem, self.recv_sem = send_sem, recv_sem

    def copy(self, src, dst, peer, slot):
        pltpu.make_async_remote_copy(
            src, dst, self.send_sem, self.recv_sem.at[slot], device_id={"ctx": peer}, device_id_type=MESH
        ).start()

    def send_heads(self, source, mine, slot):
        def start(s, _):
            n = lax.rem(s + self.me, PAIRS)
            seq, head = lax.div(n, HEADS), lax.rem(n, HEADS)
            z = lax.div(head, 3)
            peer = seq * 16 + z * 4 + lax.rem(z + 1 + lax.rem(head, 3), 4)

            @pl.when(peer != self.me)
            def _():
                self.copy(source(seq, head), mine, peer, slot)

            return 0

        lax.fori_loop(0, PAIRS, start, 0)

        @pl.when(self.holds)
        def _():
            seq, head, _ = head_of(self.me)
            pltpu.make_async_copy(source(seq, head), mine, self.recv_sem.at[slot]).start()

    def sent_heads(self, stand_in):
        @pl.when(self.holds)
        def _():
            wait_bytes(stand_in(PAIRS - 1), self.send_sem)

        @pl.when(jnp.logical_not(self.holds))
        def _():
            wait_bytes(stand_in(PAIRS), self.send_sem)

    def take_heads(self, landed, slot):
        @pl.when(self.holds)
        def _():
            wait_bytes(landed, self.recv_sem.at[slot])

    def send_tokens(self, source, target, peer):
        @pl.when(jnp.logical_and(self.holds, peer == self.me))
        def _():
            pltpu.make_async_copy(source, target, self.recv_sem.at[0]).start()

        @pl.when(jnp.logical_and(self.holds, peer != self.me))
        def _():
            self.copy(source, target, peer, 0)

    def finish_tokens(self, sent, landed):
        @pl.when(self.holds)
        def _():
            wait_bytes(sent, self.send_sem)

        wait_bytes(landed, self.recv_sem.at[0])


def exchange_sems(slots):
    return [pltpu.SemaphoreType.DMA(()), pltpu.SemaphoreType.DMA((slots,))]


def place():
    ctx, wt = lax.axis_index("ctx"), lax.axis_index("wt")
    return dict(
        x_hi=ctx // 16, z=(ctx // 4) % 4, y=ctx % 4, x_lo=wt // 2, core=wt % 2, x=(ctx // 16) * 2 + wt // 2
    )


def device_at(here, **change):
    at = dict(here)
    if "x" in change:
        at["x_hi"], at["x_lo"] = change["x"] // 2, change["x"] % 2
        change = {k: v for k, v in change.items() if k != "x"}
    at.update(change)
    return (at["x_hi"] * 16 + at["z"] * 4 + at["y"], at["x_lo"] * 2 + at["core"])


def greet_all(devices, owners=False):
    barrier = pltpu.get_barrier_semaphore()
    for device in devices:
        pl.semaphore_signal(barrier, 1, device_id=device, device_id_type=MESH)
    count = len(devices)
    if owners:
        me = lax.axis_index("ctx")

        def greet(s, _):
            pl.semaphore_signal(barrier, 1, device_id={"ctx": lax.rem(me + s, OWNERS)}, device_id_type=MESH)
            return 0

        lax.fori_loop(1, OWNERS, greet, 0)
        count += OWNERS - 1
    pl.semaphore_wait(barrier, count)


class WeightGather:
    def __init__(self, here, shards, fulls, send_sem, recv_sem, local_sem):
        self.partner = device_at(here, core=1 - here["core"])
        self.ahead = device_at(here, x=(here["x"] + 1) % 4)
        self.behind = device_at(here, x=(here["x"] + 3) % 4)
        self.mine = here["x_lo"] * 2 + here["core"]
        self.far = (1 - here["x_lo"]) * 2 + here["core"]
        self.shards, self.fulls = shards, fulls
        self.sems = send_sem, recv_sem, local_sem
        self.sent, self.local, self.handed = [], [], []

    def neighbours(self):
        return [self.partner, self.ahead, self.behind]

    def remote(self, src, dst, slot, n, device):
        return pltpu.make_async_remote_copy(
            src, dst, self.sems[0].at[slot, n], self.sems[1].at[slot, n], device_id=device, device_id_type=MESH
        )

    def start(self, first, last):
        for n in range(first, last):
            shard, full = self.shards[n], self.fulls[n]
            rows = shard.shape[0]
            half = rows // 2

            def part(owner, h, full=full, rows=rows, half=half):
                return full.at[pl.ds(pl.multiple_of(owner * rows + h * half, 16), half), :]

            whole = full.at[pl.ds(pl.multiple_of(self.mine * rows, 16), rows), :]
            copies = [
                self.remote(shard.at[pl.ds(0, half), :], part(self.mine, 0), 0, n, self.ahead),
                self.remote(shard.at[pl.ds(half, half), :], part(self.mine, 1), 1, n, self.behind),
                self.remote(shard, whole, 2, n, self.partner),
            ]
            own = pltpu.make_async_copy(shard, whole, self.sems[2].at[n])
            for copy in copies + [own]:
                copy.start()
            self.sent.append(copies)
            self.local.append(own)
            self.handed.append(
                [self.remote(part(self.far, h), part(self.far, h), 3 + h, n, self.partner) for h in (0, 1)]
            )

    def hand_on(self, n):
        for h in (0, 1):
            self.sent[n][h].wait_recv()
            self.handed[n][h].start()

    def ready(self, n):
        self.local[n].wait()
        self.sent[n][2].wait_recv()
        for copy in self.handed[n]:
            copy.wait_recv()

    def finish(self, unready):
        for n, (copies, handed) in enumerate(zip(self.sent, self.handed)):
            if n in unready:
                self.ready(n)
            for copy in copies + handed:
                copy.wait_send()


THIRDS = (1, 2, 0)


def forward_kernel(
    len_ref, tok_ref, weight, v0, v1, v2, v3, v4, v5, v6, v7, v8, w0, w1, w2,
    x_ref, o_ref, lse_ref, mixed, attend_out, small_out, f0, f1, f2,
    low, full, small, small_low, small_full, packed, low_ref, qn, kt, vn, b0, b1, b2,
    send_sem, recv_sem, local_sem, out_sem, ka, kb, va, vb, qa, qb, ma, mb, *, q_rows, k_rows,
):
    valid = len_ref[0]
    me = lax.axis_index("ctx")
    columns = [pl.ds(t * WIDTH, WIDTH) for t in range(3)]
    gather = WeightGather(
        place(),
        [small_low] + [low.at[:, columns[t]] for t in THIRDS] + [b0, b1, b2],
        [small_full] + [full.at[:, columns[t]] for t in THIRDS] + [f0, f1, f2],
        send_sem, recv_sem, local_sem,
    )
    small[...] = jnp.zeros_like(small)
    for n, vector in enumerate((v0, v1, v2, v3, v4, v5, v6, v7, v8)):
        small[n : n + 1, 0 : vector.shape[1]] = vector[...]
    small_low[...] = small[...].astype(bf16)
    low[...] = weight[...].astype(bf16)
    greet_all(gather.neighbours(), owners=True)
    gather.start(0, 4)
    for narrow, wide in ((b0, w0), (b1, w1), (b2, w2)):
        narrow[...] = wide[...].astype(bf16)
    tokens = tok_ref[...].astype(bf16)
    moves = {1: Exchange(ka, kb), 2: Exchange(va, vb), 0: Exchange(qa, qb)}
    pieces = q_rows // SPAN
    steps = LEN // q_rows
    offset = lax.div(me, pieces)

    def source(third):
        return lambda seq, head: packed.at[third, head, :, pl.ds(pl.multiple_of(seq * SPAN, SPAN), SPAN)]

    gather.hand_on(0)
    gather.hand_on(1)
    gather.ready(0)

    def bias(row):
        rows = [small_full[32 * w : 32 * w + 16, 0:192].astype(f32)[row : row + 1] for w in range(4)]
        return jnp.concatenate(rows, axis=1)

    biases = {0: bias(0), 1: None, 2: bias(1)}
    for order, third in enumerate(THIRDS):
        if order < 2:
            gather.hand_on(order + 2)
        gather.ready(order + 1)
        product = dot(tokens, full[:, third * WIDTH : (third + 1) * WIDTH])
        if biases[third] is not None:
            product = product + biases[third]
        if third == 0:
            product = product * HEAD_DIM ** (-0.5)
        packed[third] = product.T.astype(bf16).reshape(HEADS, 64, 2 * SPAN)
        moves[third].send_heads(source(third), x_ref.at[me, third], 0 if third else offset)
    outs = [pltpu.make_async_copy(full, attend_out, out_sem.at[0]), pltpu.make_async_copy(small_full, small_out, out_sem.at[1])]
    for copy in outs:
        copy.start()
    lane = lax.broadcasted_iota(jnp.int32, (64, 128), 1)
    first = lax.broadcasted_iota(jnp.int32, (64, 128), 0) == 0
    zero = jnp.zeros((64, 128), f32)
    one_row = jnp.where(first, 1.0, zero)

    def prepare_keys(c, _):
        here = pl.ds(pl.multiple_of(c * SPAN, SPAN), SPAN)
        kt[0:64, here] = x_ref[c, 1]
        mask = jnp.where(lane + c * SPAN < valid, 0.0, MASKED)
        kt[64:128, here] = jnp.where(first, mask, zero).astype(bf16)
        return 0

    def prepare_values(c, _):
        here = pl.ds(pl.multiple_of(c * SPAN, SPAN), SPAN)
        vn[here, :] = jnp.concatenate([x_ref[c, 2].astype(f32), one_row], 0).T.astype(bf16)
        return 0

    moves[1].take_heads(x_ref.at[:, 1], 0)
    lax.fori_loop(0, OWNERS, prepare_keys, 0)
    moves[2].take_heads(x_ref.at[:, 2], 0)
    gather.start(4, 7)
    lax.fori_loop(0, OWNERS, prepare_values, 0)
    target = token_slice(mixed, me)

    def q_block(turn, _):
        i = lax.rem(turn + offset, steps)
        moves[0].take_heads(x_ref.at[pl.ds(i * pieces, pieces), 0], i)
        for t in range(pieces):
            c = i * pieces + t
            here = pl.ds(pl.multiple_of(c * SPAN, SPAN), SPAN)
            qn[here, :] = jnp.concatenate([x_ref[c, 0].astype(f32), one_row], 0).T.astype(bf16)
        q = qn[pl.ds(pl.multiple_of(i * q_rows, q_rows), q_rows), :]

        def k_block(j, carry):
            peak, acc = carry
            here = pl.ds(pl.multiple_of(j * k_rows, k_rows), k_rows)
            scores = dot(q, kt[:, here])
            folded = scores[:, 0:128]
            for t in range(1, k_rows // 128):
                folded = jnp.maximum(folded, scores[:, t * 128 : (t + 1) * 128])
            peak_new = jnp.maximum(peak, jnp.max(folded, axis=1, keepdims=True))
            weights = jnp.exp(scores - peak_new).astype(bf16)
            return peak_new, acc * jnp.exp(peak - peak_new) + dot(weights, vn[here, :])

        start = (jnp.full((q_rows, 1), -3e38, f32), jnp.zeros((q_rows, 128), f32))
        peak, acc = lax.fori_loop(0, LEN // k_rows, k_block, start)
        total = acc[:, 64:65]
        column = lax.broadcasted_iota(jnp.int32, (q_rows, 128), 1)
        finished = jnp.where(column == 64, peak + jnp.log(total), acc / total).T
        for t in range(pieces):
            c = i * pieces + t
            cols = slice(t * SPAN, (t + 1) * SPAN)
            o_ref[c] = finished[0:64, cols]
            low_ref[c] = finished[0:64, cols].astype(bf16)
            lse_ref[c] = finished[64:72, cols]
            back.send_tokens(low_ref.at[c], target, c)
        return 0

    back = Exchange(ma, mb)
    cuts = (0, steps // 2, steps - 2, steps)
    for n in range(3):
        lax.fori_loop(cuts[n], cuts[n + 1], q_block, 0)
        gather.hand_on(n + 4)
    for third in THIRDS:
        moves[third].sent_heads(lambda n, third=third: x_ref.at[pl.ds(0, n), third])
    for copy in outs:
        copy.wait()
    gather.finish((4, 5, 6))
    back.finish_tokens(low_ref.at[pl.ds(0, OWNERS - 1)], mixed)


def forward(valid, tokens, weight, vectors, shards, collective_id):
    vmem, anywhere = pl.BlockSpec(memory_space=pltpu.VMEM), pl.BlockSpec(memory_space=pl.ANY)
    rows, width = weight.shape
    return pl.pallas_call(
        functools.partial(forward_kernel, q_rows=512, k_rows=1024),
        out_shape=(
            jax.ShapeDtypeStruct((OWNERS, 3, 64, SPAN), bf16),
            jax.ShapeDtypeStruct((OWNERS, 64, SPAN), f32),
            jax.ShapeDtypeStruct((OWNERS, 8, SPAN), f32),
            jax.ShapeDtypeStruct((HEADS, 64, 2 * SPAN), bf16),
            jax.ShapeDtypeStruct((4 * rows, width), bf16),
            jax.ShapeDtypeStruct((128, 768), bf16),
        ) + tuple(jax.ShapeDtypeStruct((4 * s.shape[0], s.shape[1]), bf16) for s in shards),
        in_specs=[pl.BlockSpec(memory_space=pltpu.SMEM)] + [vmem] * 14,
        out_specs=[vmem] * 4 + [anywhere] * 5,
        scratch_shapes=[
            pltpu.VMEM((rows, width), bf16),
            pltpu.VMEM((4 * rows, width), bf16),
            pltpu.VMEM((32, 768), f32),
            pltpu.VMEM((32, 768), bf16),
            pltpu.VMEM((128, 768), bf16),
            pltpu.VMEM((3, HEADS, 64, 2 * SPAN), bf16),
            pltpu.VMEM((OWNERS, 64, SPAN), bf16),
            pltpu.VMEM((LEN, 128), bf16),
            pltpu.VMEM((128, LEN), bf16),
            pltpu.VMEM((LEN, 128), bf16),
        ] + [pltpu.VMEM(s.shape, bf16) for s in shards] + [
            pltpu.SemaphoreType.DMA((5, 7)), pltpu.SemaphoreType.DMA((5, 7)), pltpu.SemaphoreType.DMA((7,)),
            pltpu.SemaphoreType.DMA((2,)),
        ] + exchange_sems(1) * 2 + exchange_sems(LEN // 512) + exchange_sems(1),
        compiler_params=pltpu.CompilerParams(
            collective_id=collective_id, has_side_effects=True, vmem_limit_bytes=VMEM_BYTES
        ),
        name="forward",
    )(valid, tokens, weight, *[v.reshape(1, -1) for v in vectors], *shards)


def split_terms(values):
    high = values.astype(bf16).astype(f32)
    rest = values - high
    middle = rest.astype(bf16).astype(f32)
    return high, middle, rest - middle


def attend_back_body(
    len_ref, x_ref, o_ref, lse_ref, grad_ref, grads, d_ref, g_ref, qt, qn, kn, kt, vn, dt, dn, dq, sems,
    *, q_rows, k_rows, streams, after,
):
    valid = len_ref[0]
    me = lax.axis_index("ctx")
    lane = lax.broadcasted_iota(jnp.int32, (64, 128), 1)
    row = lax.broadcasted_iota(jnp.int32, (64, 128), 0)
    zero = jnp.zeros((64, 128), f32)
    incoming, keys_back, query_back = [Exchange(*sems[2 * n : 2 * n + 2]) for n in range(3)]

    def source(seq, head):
        return grad_ref.at[head, :, pl.ds(pl.multiple_of(seq * SPAN, SPAN), SPAN)]

    incoming.send_heads(source, d_ref.at[me], 0)
    yield

    def prepare(c, _):
        here = pl.ds(pl.multiple_of(c * SPAN, SPAN), SPAN)
        q = x_ref[c, 0].astype(f32)
        k = x_ref[c, 1].astype(f32)
        v = x_ref[c, 2].astype(f32)
        high, middle, rest = split_terms(-lse_ref[c][0:1])
        q_extra = jnp.where(
            row == 0, 1.0, jnp.where(row == 1, high, jnp.where(row == 2, middle, jnp.where(row == 3, rest, 0.0)))
        )
        mask = jnp.where(lane + c * SPAN < valid, 0.0, MASKED)
        k_extra = jnp.where(row == 0, mask, jnp.where(row < 4, 1.0, 0.0))
        qt[:, here] = jnp.concatenate([q, q_extra], 0).astype(bf16)
        qn[here, :] = jnp.concatenate([q, zero], 0).T.astype(bf16)
        kn[here, :] = jnp.concatenate([k, k_extra], 0).T.astype(bf16)
        kt[:, here] = k.astype(bf16)
        v_extra = jnp.where(row < 3, 1.0, zero)
        vn[here, :] = jnp.concatenate([v, v_extra], 0).T.astype(bf16)
        return 0

    def prepare_grads(c, _):
        here = pl.ds(pl.multiple_of(c * SPAN, SPAN), SPAN)
        do = d_ref[c].astype(f32)
        delta = jnp.sum(do * o_ref[c], axis=0, keepdims=True)
        high, middle, rest = split_terms(-delta)
        d_extra = jnp.where(row == 0, high, jnp.where(row == 1, middle, jnp.where(row == 2, rest, 0.0)))
        dt[:, here] = jnp.concatenate([do, d_extra], 0).astype(bf16)
        dn[here, :] = jnp.concatenate([do, zero], 0).T.astype(bf16)
        return 0

    lax.fori_loop(0, OWNERS, prepare, 0)
    dq[...] = jnp.zeros_like(dq)
    incoming.take_heads(d_ref, 0)
    lax.fori_loop(0, OWNERS, prepare_grads, 0)
    pieces = k_rows // SPAN
    steps = LEN // k_rows
    offset = lax.div(me, pieces)

    def keys_target(c):
        seq, head, _ = head_of(c)
        return grads.at[pl.ds(1, 2), head, :, pl.ds(pl.multiple_of(seq * SPAN, SPAN), SPAN)]

    def k_block(turn, middle):
        j = lax.rem(turn + offset, steps)
        here = pl.ds(pl.multiple_of(j * k_rows, k_rows), k_rows)
        k, v, k_flat = kn[here, :], vn[here, :], kt[:, here]

        def q_block(i, carry):
            dk, dv = carry
            for s in range(streams):
                cols = pl.ds(pl.multiple_of(i * (q_rows * streams) + s * q_rows, q_rows), q_rows)
                weights = jnp.exp(dot(k, qt[:, cols]))
                ds = (weights * dot(v, dt[:, cols])).astype(bf16)
                dv = dv + dot(weights.astype(bf16), dn[cols, :])
                dk = dk + dot(ds, qn[cols, :])
                dq[:, cols] += dot(k_flat, ds)
            return dk, dv

        start = jnp.zeros((k_rows, 128), f32)
        count = LEN // (q_rows * streams)
        if middle is None:
            dk, dv = lax.fori_loop(0, count, q_block, (start, start))
        else:
            carry = lax.fori_loop(0, count // 2, q_block, (start, start))
            middle()
            dk, dv = lax.fori_loop(count // 2, count, q_block, carry)
        for t in range(pieces):
            rows = slice(t * SPAN, (t + 1) * SPAN)
            c = j * pieces + t
            g_ref[c, 1] = dk[rows].T[0:64].astype(bf16)
            g_ref[c, 2] = dv[rows].T[0:64].astype(bf16)
            keys_back.send_tokens(g_ref.at[c, pl.ds(1, 2)], keys_target(me), c)

    def whole_block(turn, _):
        k_block(turn, None)
        return 0

    begin = 0
    for end, event in after:
        if end == int(end):
            if int(end) > begin:
                lax.fori_loop(begin, int(end), whole_block, 0)
            event()
            begin = int(end)
        else:
            k_block(begin, event)
            begin += 1

    def finish(s, _):
        c = lax.rem(me + s, OWNERS)
        rounded = dq[:, pl.ds(pl.multiple_of(c * SPAN, SPAN), SPAN)].astype(bf16)
        g_ref[c, 0] = (rounded.astype(f32) * HEAD_DIM ** (-0.5)).astype(bf16)
        query_back.send_tokens(g_ref.at[c, 0], token_slice(grads, me, 0), c)
        return 0

    lax.fori_loop(0, OWNERS, finish, 0)
    yield
    incoming.sent_heads(lambda n: d_ref.at[pl.ds(0, n)])
    keys_back.finish_tokens(g_ref.at[pl.ds(0, OWNERS - 1), pl.ds(1, 2)], grads.at[pl.ds(1, 2)])
    query_back.finish_tokens(g_ref.at[pl.ds(0, OWNERS - 1), 0], grads.at[0])


ORDERS = (("y", "z", "x"), ("z", "x", "y"), ("x", "y", "z"))
LEAD = ("x", "z", "y")
STAGES = ("y", "z", "x")


def axes_after(p, count):
    return [a for a in LEAD if a not in ORDERS[p][:count]]


def shape_after(p, count, width):
    shape = []
    for name in axes_after(p, count):
        shape += [2, 2] if name == "x" else [4]
    return tuple(shape) + (16, width)


def total_shape(width):
    return (2, 4, 4, 48, width)


class Reduce:
    def __init__(self, here, width, halves, merge, unpack, small, scratch):
        self.here, self.width, self.merge, self.unpack, self.small = here, width, merge, unpack, small
        self.halves = halves
        (self.acc, self.out, self.sums, self.landing, self.hall,
         self.core_send, self.core_recv, self.own_sem, self.send_sem, self.recv_sem,
         self.back_send, self.back_recv, self.small_send, self.small_recv) = scratch
        self.partner = device_at(here, core=1 - here["core"])
        self.peers = {
            axis: [device_at(here, **{axis: (here[axis] + d) % 4}) for d in (1, 2, 3)] for axis in STAGES
        }
        self.waits = []
        self.flying = [[], [], []]

    @staticmethod
    def scratch(width, halves, small_rows):
        shapes = []
        for shape in halves:
            shapes += [pltpu.VMEM((3, 2) + shape, bf16)] * 2
        shapes += [pltpu.VMEM(shape_after(p, 0, width), bf16) for p in range(3)]
        shapes.append(pltpu.VMEM(total_shape(width), bf16))
        for count in (1, 2):
            shapes += [pltpu.VMEM(shape_after(p, count, width), bf16) for p in range(3)]
        for count in (1, 2, 3):
            shapes += [pltpu.VMEM((3,) + shape_after(p, count, width), bf16) for p in range(3)]
        shapes.append(pltpu.VMEM((4, 4, small_rows, 128), f32))
        count = 3 * 2 * len(halves)
        shapes += [pltpu.SemaphoreType.DMA((count,))] * 3
        shapes += [pltpu.SemaphoreType.DMA((27,))] * 4
        shapes += [pltpu.SemaphoreType.DMA((12,))] * 2
        return shapes

    @staticmethod
    def unflatten(refs, tensors):
        refs = list(refs)
        pairs = [(refs[2 * n], refs[2 * n + 1]) for n in range(tensors)]
        refs = refs[2 * tensors :]
        acc, out, refs = refs[:3], refs[3], refs[4:]
        sums = [refs[0:3], refs[3:6]]
        landing = [refs[6:9], refs[9:12], refs[12:15]]
        return pairs, [acc, out, sums, landing] + refs[15:]

    def neighbours(self):
        return [self.partner] + [device for axis in STAGES for device in self.peers[axis]]

    def remote(self, src, dst, sems, slot, device):
        copy = pltpu.make_async_remote_copy(
            src, dst, sems[0].at[slot], sems[1].at[slot], device_id=device, device_id_type=MESH
        )
        copy.start()
        self.waits.append(copy)
        return copy

    def start(self):
        core = self.here["core"]
        self.core_copies = [[], [], []]
        slot = 0
        for p in range(3):
            for source, own, other in self.halves:
                for lo in range(2):
                    moved = self.remote(
                        source.at[lo, 1 - core, p], other.at[p, lo], (self.core_send, self.core_recv), slot,
                        self.partner,
                    )
                    kept = pltpu.make_async_copy(source.at[lo, core, p], own.at[p, lo], self.own_sem.at[slot])
                    kept.start()
                    self.core_copies[p].append((moved, kept))
                    slot += 1
        self.small_stage(0, self.small[...])

    def small_stage(self, stage, value):
        axis = STAGES[stage] if stage < 3 else "core"
        mine = self.hall.at[stage, self.here[axis]]
        mine[...] = value
        devices = self.peers[axis] if stage < 3 else [self.partner]
        self.small_flying = [
            self.remote(mine, mine, (self.small_send, self.small_recv), 3 * stage + d, device)
            for d, device in enumerate(devices)
        ]

    def small_sum(self, stage):
        for copy in self.small_flying:
            copy.wait_recv()
        value = self.hall[stage, 0]
        for n in range(1, 4 if stage < 3 else 2):
            value = value + self.hall[stage, n]
        return value

    def index(self, axes, axis, value):
        index = []
        for name in axes:
            if name == "x":
                index += [value % 2, value // 2] if axis == "x" else [slice(None), slice(None)]
            else:
                index.append(value if axis == name else slice(None))
        return tuple(index)

    def scatter(self, p, stage, source):
        axis, axes = ORDERS[p][stage], axes_after(p, stage)
        self.flying[p] = [
            self.remote(
                source.at[self.index(axes, axis, (self.here[axis] + d) % 4)], self.landing[stage][p].at[d - 1],
                (self.send_sem, self.recv_sem), (p * 3 + stage) * 3 + d - 1, self.peers[axis][d - 1],
            )
            for d in (1, 2, 3)
        ]

    def begin(self, p):
        for moved, kept in self.core_copies[p]:
            moved.wait_recv()
            kept.wait()
        self.merge(p, self.acc[p])
        self.scatter(p, 0, self.acc[p])

    def advance(self, p, stage):
        axis, axes = ORDERS[p][stage], axes_after(p, stage)
        source = self.acc[p] if stage == 0 else self.sums[stage - 1][p]
        kept = source.at[self.index(axes, axis, self.here[axis])]
        landing = self.landing[stage][p]
        for copy in self.flying[p]:
            copy.wait_recv()
        if stage < 2:
            target = self.sums[stage][p]
        else:
            target = self.out.at[self.here["x_hi"], self.here["z"], self.here["y"], pl.ds(16 * p, 16), :]
        lead = target.shape[:-2]
        total = 1
        for size in lead:
            total *= size

        def step(n, _):
            index, left = [], n
            for size in reversed(lead):
                index.insert(0, left % size)
                left = left // size
            index = tuple(index)
            value = kept[index].astype(f32)
            for d in range(3):
                value = value + landing[(d,) + index].astype(f32)
            target[index] = value.astype(bf16)
            return 0

        if lead:
            lax.fori_loop(0, total, step, 0)
            self.scatter(p, stage + 1, target)
        else:
            value = kept[...].astype(f32)
            for d in range(3):
                value = value + landing[d].astype(f32)
            target[...] = value.astype(bf16)
            self.spread(p, 0)

    def spread(self, p, stage):
        if stage:
            for copy in self.flying[p]:
                copy.wait_recv()
        if stage == 3:
            return
        axis = ORDERS[p][2 - stage]
        done = [ORDERS[p][2 - k] for k in range(stage)]
        index = tuple(
            slice(None) if name in done else self.here["x_hi" if name == "x" else name] for name in LEAD
        )
        piece = self.out.at[index + (pl.ds(16 * p, 16), slice(None))]
        devices = [device_at(self.here, x_hi=1 - self.here["x_hi"])] if axis == "x" else self.peers[axis]
        self.flying[p] = [
            self.remote(piece, piece, (self.back_send, self.back_recv), (p * 3 + stage) * 3 + d, device)
            for d, device in enumerate(devices)
        ]

    def step(self, number):
        for p in range(3):
            if number == 0:
                self.begin(p)
            elif number <= 3:
                self.advance(p, number - 1)
            else:
                self.spread(p, number - 3)
        if 1 <= number <= 3:
            self.small_stage(number, self.small_sum(number - 1))
        elif number == 4:
            self.small[...] = self.small_sum(3)

    def finish(self):
        self.unpack(self.out)
        for copy in self.waits:
            copy.wait_send()


def merge_blocks(p, pairs, acc, blocks):
    def step(n, _):
        lo, z = n // 4, n % 4

        def load(tensor, index):
            own, other = pairs[tensor]
            index = (p, lo, z) + index
            return own[index].astype(f32) + other[index].astype(f32)

        for (hi, y, left), value in blocks(load):
            acc[lo, hi, z, y, :, left : left + value.shape[1]] = value.astype(bf16)
        return 0

    lax.fori_loop(0, 8, step, 0)


def cut(value):
    return [value[:, n * 384 : (n + 1) * 384] for n in range(value.shape[1] // 384)]


def early_blocks(load):
    wide = cut(load(0, ()))
    found = [((n // 4, n % 4, 0), value) for n, value in enumerate(wide)]
    for y in range(4):
        found += [((hi, y, 384), value) for hi, value in enumerate(cut(load(1, (y,))))]
    return found


def late_blocks(load):
    pieces = cut(load(0, ())) + cut(load(1, ()))
    return [((n // 4, n % 4, 0), value) for n, value in enumerate(pieces)]


def early_unpack(expand_out, shrink_out):
    def unpack(out):
        def step(n, _):
            p, z = n // 4, n % 4
            band = pl.ds(pl.multiple_of(p * 16, 16), 16)
            rows = pl.ds(pl.multiple_of(n * 16, 16), 16)
            for hi in range(2):
                for y in range(4):
                    value = out[hi, z, y, band, :]
                    left = hi * 1536 + y * 384
                    expand_out[rows, left : left + 384] = value[:, 0:384]
                    below = pl.ds(pl.multiple_of(n * 64 + y * 16, 16), 16)
                    shrink_out[below, hi * 384 : hi * 384 + 384] = value[:, 384:768]
            return 0

        lax.fori_loop(0, 12, step, 0)

    return unpack


def late_unpack(output_out, attend_out):
    def unpack(out):
        def step(n, _):
            p, z = n // 4, n % 4
            band = pl.ds(pl.multiple_of(p * 16, 16), 16)
            rows = pl.ds(pl.multiple_of(n * 16, 16), 16)
            for m in range(8):
                value = out[m // 4, z, m % 4, band, :]
                if m < 2:
                    output_out[rows, m * 384 : m * 384 + 384] = value
                else:
                    attend_out[rows, (m - 2) * 384 : (m - 1) * 384] = value
            return 0

        lax.fori_loop(0, 12, step, 0)

    return unpack


REDUCE_STEPS = ((1, 0), (4, 1), (5, 2), (5.5, 3), (6, 4), (6.5, 5), (8, 6))
EARLY_HALVES = ((4, 16, 3072), (4, 4, 16, 768))
LATE_HALVES = ((4, 16, 768), (4, 16, 2304))


def attend_back_kernel(
    len_ref, x_ref, o_ref, lse_ref, grad_ref, expand_src, shrink_src, small_src,
    grads, expand_out, shrink_out, small_out, *refs,
):
    attention, sems, refs = refs[:10], refs[10:16], refs[16:]
    pairs, scratch = Reduce.unflatten(refs, 2)
    small_out[...] = small_src[...]
    reduce = Reduce(
        place(), 768, [(source, *pair) for source, pair in zip((expand_src, shrink_src), pairs)],
        lambda p, acc: merge_blocks(p, pairs, acc, early_blocks), early_unpack(expand_out, shrink_out),
        small_out, scratch,
    )
    greet_all(reduce.neighbours(), owners=True)
    body = attend_back_body(
        len_ref, x_ref, o_ref, lse_ref, grad_ref, grads, *attention, sems, q_rows=512, k_rows=512, streams=2,
        after=[(end, functools.partial(reduce.step, number)) for end, number in REDUCE_STEPS],
    )
    next(body)
    reduce.start()
    next(body)
    reduce.finish()
    for _ in body:
        pass


def attend_back(valid, packed, mixed, lse, grad_mixed, expand_term, shrink_term, small, collective_id):
    vmem, anywhere = pl.BlockSpec(memory_space=pltpu.VMEM), pl.BlockSpec(memory_space=pl.ANY)
    return pl.pallas_call(
        attend_back_kernel,
        out_shape=(
            jax.ShapeDtypeStruct((3, HEADS, 64, 2 * SPAN), bf16),
            jax.ShapeDtypeStruct((192, 3072), bf16),
            jax.ShapeDtypeStruct((768, 768), bf16),
            jax.ShapeDtypeStruct(small.shape, f32),
        ),
        in_specs=[pl.BlockSpec(memory_space=pltpu.SMEM)] + [vmem] * 4 + [anywhere] * 2 + [vmem],
        out_specs=[vmem] * 4,
        scratch_shapes=[
            pltpu.VMEM((OWNERS, 64, SPAN), bf16),
            pltpu.VMEM((OWNERS, 3, 64, SPAN), bf16),
            pltpu.VMEM((128, LEN), bf16),
            pltpu.VMEM((LEN, 128), bf16),
            pltpu.VMEM((LEN, 128), bf16),
            pltpu.VMEM((64, LEN), bf16),
            pltpu.VMEM((LEN, 128), bf16),
            pltpu.VMEM((128, LEN), bf16),
            pltpu.VMEM((LEN, 128), bf16),
            pltpu.VMEM((64, LEN), f32),
        ] + exchange_sems(1) * 3 + Reduce.scratch(768, EARLY_HALVES, small.shape[0]),
        compiler_params=pltpu.CompilerParams(
            collective_id=collective_id, has_side_effects=True, vmem_limit_bytes=VMEM_BYTES
        ),
        name="attend_back",
    )(
        valid, packed, mixed, lse, grad_mixed, expand_term.reshape(2, 2, 3, 4, 16, 3072),
        shrink_term.reshape(2, 2, 3, 4, 4, 16, 768), small,
    )


def late_kernel(output_src, attend_src, small_src, output_out, attend_out, small_out, *refs):
    pairs, scratch = Reduce.unflatten(refs, 2)
    small_out[...] = small_src[...]
    reduce = Reduce(
        place(), 384, [(source, *pair) for source, pair in zip((output_src, attend_src), pairs)],
        lambda p, acc: merge_blocks(p, pairs, acc, late_blocks), late_unpack(output_out, attend_out),
        small_out, scratch,
    )
    greet_all(reduce.neighbours())
    reduce.start()
    for number in range(7):
        reduce.step(number)
    reduce.finish()


def late_reduce(output_term, attend_term, small, collective_id):
    vmem, anywhere = pl.BlockSpec(memory_space=pltpu.VMEM), pl.BlockSpec(memory_space=pl.ANY)
    return pl.pallas_call(
        late_kernel,
        out_shape=(
            jax.ShapeDtypeStruct((192, 768), bf16),
            jax.ShapeDtypeStruct((192, 2304), bf16),
            jax.ShapeDtypeStruct(small.shape, f32),
        ),
        in_specs=[anywhere] * 2 + [vmem],
        out_specs=[vmem] * 3,
        scratch_shapes=Reduce.scratch(384, LATE_HALVES, small.shape[0]),
        compiler_params=pltpu.CompilerParams(
            collective_id=collective_id, has_side_effects=True, vmem_limit_bytes=VMEM_BYTES
        ),
        name="late_reduce",
    )(output_term.reshape(2, 2, 3, 4, 16, 768), attend_term.reshape(2, 2, 3, 4, 16, 2304), small)


def per_device(
    inputs, lengths, attend_weight, query_bias, value_bias, output_weight, output_bias, norm_gain, norm_shift,
    expand_weight, expand_bias, shrink_weight, shrink_bias, final_gain, final_shift, cotangent,
):
    ctx, wt = lax.axis_index("ctx"), lax.axis_index("wt")
    vectors = (
        query_bias, value_bias, output_bias, norm_gain, norm_shift, expand_bias, shrink_bias, final_gain, final_shift,
    )
    seq_count, tok_local, model_width = inputs.shape
    row_count = seq_count * tok_local
    tokens = inputs.reshape(row_count, model_width)
    tokens_low = tokens.astype(bf16)
    seq, _, holds = head_of(ctx)
    my_length = jnp.where(holds, lengths[seq], 0).astype(jnp.int32).reshape(1)
    held, mixed_heads, lse, mixed, attend_full, small_full, output_full, expand_full, shrink_full = forward(
        my_length, tokens, attend_weight, vectors, (output_weight, expand_weight, shrink_weight), 0
    )
    mixed_low = mixed.reshape(model_width, row_count)
    small_full = small_full.reshape(4, 32, 768).astype(f32)
    _, _, output_add, gain_one, shift_one, expand_add, shrink_add, gain_two, shift_two = [
        small_full[:, n, : v.shape[0]].reshape(-1) for n, v in enumerate(vectors)
    ]

    attended = contract(mixed_low, output_full, 0, 0) + output_add
    hidden_one = tokens + attended
    normed_one = layer_norm(hidden_one, gain_one, shift_one)
    normed_low = normed_one.astype(bf16)
    raised = dot(normed_low, expand_full) + expand_add
    activated = exact_gelu(raised).astype(bf16)
    branch = dot(activated, shrink_full) + shrink_add
    hidden_two = normed_one + branch
    result = layer_norm(hidden_two, gain_two, shift_two)

    upstream = cotangent.reshape(row_count, model_width)
    grad_two, final_gain_term, final_shift_term = norm_pullback(hidden_two, gain_two, upstream)
    branch_low = grad_two.astype(bf16)
    shrink_bias_term = jnp.sum(branch_low.astype(f32), axis=0)
    shrink_term = contract(activated, branch_low, 0, 0)
    grad_active = contract(branch_low, shrink_full, 1, 1)
    _, gelu_pull = jax.vjp(exact_gelu, raised)
    raised_low = gelu_pull(grad_active)[0].astype(bf16)
    expand_bias_term = jnp.sum(raised_low.astype(f32), axis=0)
    expand_term = contract(normed_low, raised_low, 0, 0)
    grad_normed = grad_two + contract(raised_low, expand_full, 1, 1)
    grad_one, norm_gain_term, norm_shift_term = norm_pullback(hidden_one, gain_one, grad_normed)
    attended_low = grad_one.astype(bf16)
    output_bias_term = jnp.sum(attended_low.astype(f32), axis=0)
    output_term = dot(mixed_low, attended_low)
    grad_mixed = contract(output_full, attended_low, 1, 1).astype(bf16)

    early = jnp.concatenate(
        [t.reshape(4, -1) for t in (
            output_bias_term, norm_gain_term, norm_shift_term, expand_bias_term, shrink_bias_term,
            final_gain_term, final_shift_term)] + [jnp.zeros((4, 128), f32)], axis=1,
    ).reshape(64, 128)
    grad_packed, expand_grad, shrink_grad, early = attend_back(
        my_length, held, mixed_heads, lse, grad_mixed.reshape(HEADS, 64, row_count), expand_term.astype(bf16), shrink_term.astype(bf16), early, 1
    )
    grad_packed = grad_packed.reshape(3 * model_width, row_count)
    attend_term = contract(tokens_low, grad_packed, 0, 1)
    input_grad = grad_one + contract(grad_packed, attend_full, 0, 1)
    query_bias_term = jnp.sum(grad_packed[:model_width].astype(f32), axis=1)
    value_bias_term = jnp.sum(grad_packed[2 * model_width :].astype(f32), axis=1)

    late = jnp.concatenate(
        [t.reshape(4, -1) for t in (query_bias_term, value_bias_term)] + [jnp.zeros((4, 128), f32)], axis=1
    ).reshape(16, 128)
    output_grad, attend_grad, late = late_reduce(output_term.astype(bf16), attend_term.astype(bf16), late, 2)
    early = lax.dynamic_index_in_dim(early.reshape(4, 2048), wt, 0, keepdims=False)
    late = lax.dynamic_index_in_dim(late.reshape(4, 512), wt, 0, keepdims=False)
    n = 192
    return (
        result.reshape(inputs.shape),
        input_grad.reshape(inputs.shape),
        attend_grad.astype(f32),
        late[:n],
        late[n : 2 * n],
        output_grad.astype(f32),
        early[0:n],
        early[n : 2 * n],
        early[2 * n : 3 * n],
        expand_grad.astype(f32),
        early[3 * n : 7 * n],
        shrink_grad.astype(f32),
        early[7 * n : 8 * n],
        early[8 * n : 9 * n],
        early[9 * n : 10 * n],
    )


def solution(mesh):
    wide, rows, flat = P("wt", "ctx", None), P("wt", None), P("wt")
    return jax.shard_map(
        per_device,
        mesh=mesh,
        in_specs=(
            wide, flat, rows, flat, flat, rows, flat, flat, flat, rows, flat, rows, flat, flat, flat, wide,
        ),
        out_specs=(
            wide, wide, rows, flat, flat, rows, flat, flat, flat, rows, flat, rows, flat, flat, flat,
        ),
        check_vma=False,
    )
```

```python
import functools

import jax
import jax.numpy as jnp
from jax import lax
from jax.experimental import pallas as pl
from jax.experimental.pallas import tpu as pltpu
from jax.sharding import PartitionSpec as P

HEADS = 12
HEAD_DIM = 64
LEN = 4096
WIDTH = 768
OWNERS = 32
PAIRS = 24
VMEM_BYTES = 58 << 20
SPAN = 128
MASKED = -1e30
norm_eps = 1e-06
f32 = jnp.float32
bf16 = jnp.bfloat16
MESH = pl.DeviceIdType.MESH


def layer_norm(values, gain_row, shift_row):
    centered = values - jnp.mean(values, axis=-1, keepdims=True)
    variance = jnp.mean(centered * centered, axis=-1, keepdims=True)
    return centered * lax.rsqrt(variance + norm_eps) * gain_row + shift_row


def norm_pullback(values, gain_row, upstream):
    _, pulled = jax.vjp(lambda inside, scaled: layer_norm(inside, scaled, 0.0), values, gain_row)
    grad_values, grad_gain = pulled(upstream)
    return (grad_values, grad_gain, jnp.sum(upstream, axis=0))


def exact_gelu(values):
    return jax.nn.gelu(values, approximate=False)


def dot(left, right):
    return jnp.dot(left, right, preferred_element_type=f32)


def contract(left, right, left_dim, right_dim):
    return lax.dot_general(
        left, right, (((left_dim,), (right_dim,)), ((), ())), preferred_element_type=f32
    )


def head_of(ctx):
    z, y = lax.rem(lax.div(ctx, 4), 4), lax.rem(ctx, 4)
    turn = lax.rem(y + 7 - z, 4)
    return lax.div(ctx, 16), 3 * z + jnp.minimum(turn, 2), turn < 3


def token_slice(ref, ctx, *lead):
    seq, head, _ = head_of(ctx)
    return ref.at[lead + (head, slice(None), pl.ds(pl.multiple_of(seq * SPAN, SPAN), SPAN))]


def wait_bytes(ref, sem):
    pltpu.make_async_copy(ref, ref, sem).wait()


class Exchange:
    def __init__(self, send_sem, recv_sem):
        self.me = lax.axis_index("ctx")
        self.holds = head_of(self.me)[2]
        self.send_sem, self.recv_sem = send_sem, recv_sem

    def copy(self, src, dst, peer, slot):
        pltpu.make_async_remote_copy(
            src, dst, self.send_sem, self.recv_sem.at[slot], device_id={"ctx": peer}, device_id_type=MESH
        ).start()

    def send_heads(self, source, mine, slot):
        def start(s, _):
            n = lax.rem(s + self.me, PAIRS)
            seq, head = lax.div(n, HEADS), lax.rem(n, HEADS)
            z = lax.div(head, 3)
            peer = seq * 16 + z * 4 + lax.rem(z + 1 + lax.rem(head, 3), 4)

            @pl.when(peer != self.me)
            def _():
                self.copy(source(seq, head), mine, peer, slot)

            return 0

        lax.fori_loop(0, PAIRS, start, 0)

        @pl.when(self.holds)
        def _():
            seq, head, _ = head_of(self.me)
            pltpu.make_async_copy(source(seq, head), mine, self.recv_sem.at[slot]).start()

    def sent_heads(self, stand_in):
        @pl.when(self.holds)
        def _():
            wait_bytes(stand_in(PAIRS - 1), self.send_sem)

        @pl.when(jnp.logical_not(self.holds))
        def _():
            wait_bytes(stand_in(PAIRS), self.send_sem)

    def take_heads(self, landed, slot):
        @pl.when(self.holds)
        def _():
            wait_bytes(landed, self.recv_sem.at[slot])

    def send_tokens(self, source, target, peer):
        @pl.when(jnp.logical_and(self.holds, peer == self.me))
        def _():
            pltpu.make_async_copy(source, target, self.recv_sem.at[0]).start()

        @pl.when(jnp.logical_and(self.holds, peer != self.me))
        def _():
            self.copy(source, target, peer, 0)

    def finish_tokens(self, sent, landed):
        @pl.when(self.holds)
        def _():
            wait_bytes(sent, self.send_sem)

        wait_bytes(landed, self.recv_sem.at[0])


def exchange_sems(slots):
    return [pltpu.SemaphoreType.DMA(()), pltpu.SemaphoreType.DMA((slots,))]


def place():
    ctx, wt = lax.axis_index("ctx"), lax.axis_index("wt")
    return dict(
        x_hi=ctx // 16, z=(ctx // 4) % 4, y=ctx % 4, x_lo=wt // 2, core=wt % 2, x=(ctx // 16) * 2 + wt // 2
    )


def device_at(here, **change):
    at = dict(here)
    if "x" in change:
        at["x_hi"], at["x_lo"] = change["x"] // 2, change["x"] % 2
        change = {k: v for k, v in change.items() if k != "x"}
    at.update(change)
    return (at["x_hi"] * 16 + at["z"] * 4 + at["y"], at["x_lo"] * 2 + at["core"])


def greet_all(devices, owners=False):
    barrier = pltpu.get_barrier_semaphore()
    for device in devices:
        pl.semaphore_signal(barrier, 1, device_id=device, device_id_type=MESH)
    count = len(devices)
    if owners:
        me = lax.axis_index("ctx")

        def greet(s, _):
            pl.semaphore_signal(barrier, 1, device_id={"ctx": lax.rem(me + s, OWNERS)}, device_id_type=MESH)
            return 0

        lax.fori_loop(1, OWNERS, greet, 0)
        count += OWNERS - 1
    pl.semaphore_wait(barrier, count)


class WeightGather:
    def __init__(self, here, shards, fulls, send_sem, recv_sem, local_sem):
        self.partner = device_at(here, core=1 - here["core"])
        self.ahead = device_at(here, x=(here["x"] + 1) % 4)
        self.behind = device_at(here, x=(here["x"] + 3) % 4)
        self.mine = here["x_lo"] * 2 + here["core"]
        self.far = (1 - here["x_lo"]) * 2 + here["core"]
        self.shards, self.fulls = shards, fulls
        self.sems = send_sem, recv_sem, local_sem
        self.sent, self.local, self.handed = [], [], []

    def neighbours(self):
        return [self.partner, self.ahead, self.behind]

    def remote(self, src, dst, slot, n, device):
        return pltpu.make_async_remote_copy(
            src, dst, self.sems[0].at[slot, n], self.sems[1].at[slot, n], device_id=device, device_id_type=MESH
        )

    def start(self, first, last):
        for n in range(first, last):
            shard, full = self.shards[n], self.fulls[n]
            rows = shard.shape[0]
            half = rows // 2

            def part(owner, h, full=full, rows=rows, half=half):
                return full.at[pl.ds(pl.multiple_of(owner * rows + h * half, 16), half), :]

            whole = full.at[pl.ds(pl.multiple_of(self.mine * rows, 16), rows), :]
            copies = [
                self.remote(shard.at[pl.ds(0, half), :], part(self.mine, 0), 0, n, self.ahead),
                self.remote(shard.at[pl.ds(half, half), :], part(self.mine, 1), 1, n, self.behind),
                self.remote(shard, whole, 2, n, self.partner),
            ]
            own = pltpu.make_async_copy(shard, whole, self.sems[2].at[n])
            for copy in copies + [own]:
                copy.start()
            self.sent.append(copies)
            self.local.append(own)
            self.handed.append(
                [self.remote(part(self.far, h), part(self.far, h), 3 + h, n, self.partner) for h in (0, 1)]
            )

    def hand_on(self, n):
        for h in (0, 1):
            self.sent[n][h].wait_recv()
            self.handed[n][h].start()

    def ready(self, n):
        self.local[n].wait()
        self.sent[n][2].wait_recv()
        for copy in self.handed[n]:
            copy.wait_recv()

    def finish(self, unready):
        for n, (copies, handed) in enumerate(zip(self.sent, self.handed)):
            if n in unready:
                self.ready(n)
            for copy in copies + handed:
                copy.wait_send()


THIRDS = (1, 2, 0)


def forward_kernel(
    len_ref, tok_ref, weight, v0, v1, v2, v3, v4, v5, v6, v7, v8, w0, w1, w2,
    x_ref, o_ref, lse_ref, mixed, attend_out, small_out, f0, f1, f2,
    low, full, small, small_low, small_full, packed, low_ref, qn, kt, vn, b0, b1, b2,
    send_sem, recv_sem, local_sem, out_sem, ka, kb, va, vb, qa, qb, ma, mb, *, q_rows, k_rows,
):
    valid = len_ref[0]
    me = lax.axis_index("ctx")
    columns = [pl.ds(t * WIDTH, WIDTH) for t in range(3)]
    gather = WeightGather(
        place(),
        [small_low] + [low.at[:, columns[t]] for t in THIRDS] + [b0, b1, b2],
        [small_full] + [full.at[:, columns[t]] for t in THIRDS] + [f0, f1, f2],
        send_sem, recv_sem, local_sem,
    )
    small[...] = jnp.zeros_like(small)
    for n, vector in enumerate((v0, v1, v2, v3, v4, v5, v6, v7, v8)):
        small[n : n + 1, 0 : vector.shape[1]] = vector[...]
    small_low[...] = small[...].astype(bf16)
    low[...] = weight[...].astype(bf16)
    greet_all(gather.neighbours(), owners=True)
    gather.start(0, 4)
    for narrow, wide in ((b0, w0), (b1, w1), (b2, w2)):
        narrow[...] = wide[...].astype(bf16)
    tokens = tok_ref[...].astype(bf16)
    moves = {1: Exchange(ka, kb), 2: Exchange(va, vb), 0: Exchange(qa, qb)}
    pieces = q_rows // SPAN
    steps = LEN // q_rows
    offset = lax.div(me, pieces)

    def source(third):
        return lambda seq, head: packed.at[third, head, :, pl.ds(pl.multiple_of(seq * SPAN, SPAN), SPAN)]

    gather.hand_on(0)
    gather.hand_on(1)
    gather.ready(0)

    def bias(row):
        rows = [small_full[32 * w : 32 * w + 16, 0:192].astype(f32)[row : row + 1] for w in range(4)]
        return jnp.concatenate(rows, axis=1)

    biases = {0: bias(0), 1: None, 2: bias(1)}
    for order, third in enumerate(THIRDS):
        if order < 2:
            gather.hand_on(order + 2)
        gather.ready(order + 1)
        product = dot(tokens, full[:, third * WIDTH : (third + 1) * WIDTH])
        if biases[third] is not None:
            product = product + biases[third]
        if third == 0:
            product = product * HEAD_DIM ** (-0.5)
        packed[third] = product.T.astype(bf16).reshape(HEADS, 64, 2 * SPAN)
        moves[third].send_heads(source(third), x_ref.at[me, third], 0 if third else offset)
    outs = [pltpu.make_async_copy(full, attend_out, out_sem.at[0]), pltpu.make_async_copy(small_full, small_out, out_sem.at[1])]
    for copy in outs:
        copy.start()
    lane = lax.broadcasted_iota(jnp.int32, (64, 128), 1)
    first = lax.broadcasted_iota(jnp.int32, (64, 128), 0) == 0
    zero = jnp.zeros((64, 128), f32)
    one_row = jnp.where(first, 1.0, zero)

    def prepare_keys(c, _):
        here = pl.ds(pl.multiple_of(c * SPAN, SPAN), SPAN)
        kt[0:64, here] = x_ref[c, 1]
        mask = jnp.where(lane + c * SPAN < valid, 0.0, MASKED)
        kt[64:128, here] = jnp.where(first, mask, zero).astype(bf16)
        return 0

    def prepare_values(c, _):
        here = pl.ds(pl.multiple_of(c * SPAN, SPAN), SPAN)
        vn[here, :] = jnp.concatenate([x_ref[c, 2].astype(f32), one_row], 0).T.astype(bf16)
        return 0

    moves[1].take_heads(x_ref.at[:, 1], 0)
    lax.fori_loop(0, OWNERS, prepare_keys, 0)
    moves[2].take_heads(x_ref.at[:, 2], 0)
    gather.start(4, 7)
    lax.fori_loop(0, OWNERS, prepare_values, 0)
    target = token_slice(mixed, me)

    def q_block(turn, _):
        i = lax.rem(turn + offset, steps)
        moves[0].take_heads(x_ref.at[pl.ds(i * pieces, pieces), 0], i)
        for t in range(pieces):
            c = i * pieces + t
            here = pl.ds(pl.multiple_of(c * SPAN, SPAN), SPAN)
            qn[here, :] = jnp.concatenate([x_ref[c, 0].astype(f32), one_row], 0).T.astype(bf16)
        q = qn[pl.ds(pl.multiple_of(i * q_rows, q_rows), q_rows), :]

        def k_block(j, carry):
            peak, acc = carry
            here = pl.ds(pl.multiple_of(j * k_rows, k_rows), k_rows)
            scores = dot(q, kt[:, here])
            folded = scores[:, 0:128]
            for t in range(1, k_rows // 128):
                folded = jnp.maximum(folded, scores[:, t * 128 : (t + 1) * 128])
            peak_new = jnp.maximum(peak, jnp.max(folded, axis=1, keepdims=True))
            weights = jnp.exp(scores - peak_new).astype(bf16)
            return peak_new, acc * jnp.exp(peak - peak_new) + dot(weights, vn[here, :])

        start = (jnp.full((q_rows, 1), -3e38, f32), jnp.zeros((q_rows, 128), f32))
        peak, acc = lax.fori_loop(0, LEN // k_rows, k_block, start)
        total = acc[:, 64:65]
        column = lax.broadcasted_iota(jnp.int32, (q_rows, 128), 1)
        finished = jnp.where(column == 64, peak + jnp.log(total), acc / total).T
        for t in range(pieces):
            c = i * pieces + t
            cols = slice(t * SPAN, (t + 1) * SPAN)
            o_ref[c] = finished[0:64, cols]
            low_ref[c] = finished[0:64, cols].astype(bf16)
            lse_ref[c] = finished[64:72, cols]
            back.send_tokens(low_ref.at[c], target, c)
        return 0

    back = Exchange(ma, mb)
    cuts = (0, steps // 2, steps - 2, steps - 1)
    for n in range(3):
        lax.fori_loop(cuts[n], cuts[n + 1], q_block, 0)
        gather.hand_on(n + 4)
    lax.fori_loop(steps - 1, steps, q_block, 0)
    for third in THIRDS:
        moves[third].sent_heads(lambda n, third=third: x_ref.at[pl.ds(0, n), third])
    for copy in outs:
        copy.wait()
    gather.finish((4, 5, 6))
    back.finish_tokens(low_ref.at[pl.ds(0, OWNERS - 1)], mixed)


def forward(valid, tokens, weight, vectors, shards, collective_id):
    vmem, anywhere = pl.BlockSpec(memory_space=pltpu.VMEM), pl.BlockSpec(memory_space=pl.ANY)
    rows, width = weight.shape
    return pl.pallas_call(
        functools.partial(forward_kernel, q_rows=512, k_rows=1024),
        out_shape=(
            jax.ShapeDtypeStruct((OWNERS, 3, 64, SPAN), bf16),
            jax.ShapeDtypeStruct((OWNERS, 64, SPAN), f32),
            jax.ShapeDtypeStruct((OWNERS, 8, SPAN), f32),
            jax.ShapeDtypeStruct((HEADS, 64, 2 * SPAN), bf16),
            jax.ShapeDtypeStruct((4 * rows, width), bf16),
            jax.ShapeDtypeStruct((128, 768), bf16),
        ) + tuple(jax.ShapeDtypeStruct((4 * s.shape[0], s.shape[1]), bf16) for s in shards),
        in_specs=[pl.BlockSpec(memory_space=pltpu.SMEM)] + [vmem] * 14,
        out_specs=[vmem] * 4 + [anywhere] * 5,
        scratch_shapes=[
            pltpu.VMEM((rows, width), bf16),
            pltpu.VMEM((4 * rows, width), bf16),
            pltpu.VMEM((32, 768), f32),
            pltpu.VMEM((32, 768), bf16),
            pltpu.VMEM((128, 768), bf16),
            pltpu.VMEM((3, HEADS, 64, 2 * SPAN), bf16),
            pltpu.VMEM((OWNERS, 64, SPAN), bf16),
            pltpu.VMEM((LEN, 128), bf16),
            pltpu.VMEM((128, LEN), bf16),
            pltpu.VMEM((LEN, 128), bf16),
        ] + [pltpu.VMEM(s.shape, bf16) for s in shards] + [
            pltpu.SemaphoreType.DMA((5, 7)), pltpu.SemaphoreType.DMA((5, 7)), pltpu.SemaphoreType.DMA((7,)),
            pltpu.SemaphoreType.DMA((2,)),
        ] + exchange_sems(1) * 2 + exchange_sems(LEN // 512) + exchange_sems(1),
        compiler_params=pltpu.CompilerParams(
            collective_id=collective_id, has_side_effects=True, vmem_limit_bytes=VMEM_BYTES
        ),
        name="forward",
    )(valid, tokens, weight, *[v.reshape(1, -1) for v in vectors], *shards)


def split_terms(values):
    high = values.astype(bf16).astype(f32)
    rest = values - high
    middle = rest.astype(bf16).astype(f32)
    return high, middle, rest - middle


def attend_back_body(
    len_ref, x_ref, o_ref, lse_ref, grad_ref, grads, d_ref, g_ref, qt, qn, kn, kt, vn, dt, dn, dq, sems,
    *, q_rows, k_rows, streams, after,
):
    valid = len_ref[0]
    me = lax.axis_index("ctx")
    lane = lax.broadcasted_iota(jnp.int32, (64, 128), 1)
    row = lax.broadcasted_iota(jnp.int32, (64, 128), 0)
    zero = jnp.zeros((64, 128), f32)
    incoming, keys_back, query_back = [Exchange(*sems[2 * n : 2 * n + 2]) for n in range(3)]

    def source(seq, head):
        return grad_ref.at[head, :, pl.ds(pl.multiple_of(seq * SPAN, SPAN), SPAN)]

    incoming.send_heads(source, d_ref.at[me], 0)
    yield

    def prepare(c, _):
        here = pl.ds(pl.multiple_of(c * SPAN, SPAN), SPAN)
        q = x_ref[c, 0].astype(f32)
        k = x_ref[c, 1].astype(f32)
        v = x_ref[c, 2].astype(f32)
        high, middle, rest = split_terms(-lse_ref[c][0:1])
        q_extra = jnp.where(
            row == 0, 1.0, jnp.where(row == 1, high, jnp.where(row == 2, middle, jnp.where(row == 3, rest, 0.0)))
        )
        mask = jnp.where(lane + c * SPAN < valid, 0.0, MASKED)
        k_extra = jnp.where(row == 0, mask, jnp.where(row < 4, 1.0, 0.0))
        qt[:, here] = jnp.concatenate([q, q_extra], 0).astype(bf16)
        qn[here, :] = jnp.concatenate([q, zero], 0).T.astype(bf16)
        kn[here, :] = jnp.concatenate([k, k_extra], 0).T.astype(bf16)
        kt[:, here] = k.astype(bf16)
        v_extra = jnp.where(row < 3, 1.0, zero)
        vn[here, :] = jnp.concatenate([v, v_extra], 0).T.astype(bf16)
        return 0

    def prepare_grads(c, _):
        here = pl.ds(pl.multiple_of(c * SPAN, SPAN), SPAN)
        do = d_ref[c].astype(f32)
        delta = jnp.sum(do * o_ref[c], axis=0, keepdims=True)
        high, middle, rest = split_terms(-delta)
        d_extra = jnp.where(row == 0, high, jnp.where(row == 1, middle, jnp.where(row == 2, rest, 0.0)))
        dt[:, here] = jnp.concatenate([do, d_extra], 0).astype(bf16)
        dn[here, :] = jnp.concatenate([do, zero], 0).T.astype(bf16)
        return 0

    lax.fori_loop(0, OWNERS, prepare, 0)
    dq[...] = jnp.zeros_like(dq)
    incoming.take_heads(d_ref, 0)
    lax.fori_loop(0, OWNERS, prepare_grads, 0)
    pieces = k_rows // SPAN
    steps = LEN // k_rows
    offset = lax.div(me, pieces)

    def keys_target(c):
        seq, head, _ = head_of(c)
        return grads.at[pl.ds(1, 2), head, :, pl.ds(pl.multiple_of(seq * SPAN, SPAN), SPAN)]

    def k_block(turn, middle):
        j = lax.rem(turn + offset, steps)
        here = pl.ds(pl.multiple_of(j * k_rows, k_rows), k_rows)
        k, v, k_flat = kn[here, :], vn[here, :], kt[:, here]

        def q_block(i, carry):
            dk, dv = carry
            for s in range(streams):
                cols = pl.ds(pl.multiple_of(i * (q_rows * streams) + s * q_rows, q_rows), q_rows)
                weights = jnp.exp(dot(k, qt[:, cols]))
                ds = (weights * dot(v, dt[:, cols])).astype(bf16)
                dv = dv + dot(weights.astype(bf16), dn[cols, :])
                dk = dk + dot(ds, qn[cols, :])
                dq[:, cols] += dot(k_flat, ds)
            return dk, dv

        start = jnp.zeros((k_rows, 128), f32)
        count = LEN // (q_rows * streams)
        if middle is None:
            dk, dv = lax.fori_loop(0, count, q_block, (start, start))
        else:
            carry = lax.fori_loop(0, count // 2, q_block, (start, start))
            middle()
            dk, dv = lax.fori_loop(count // 2, count, q_block, carry)
        for t in range(pieces):
            rows = slice(t * SPAN, (t + 1) * SPAN)
            c = j * pieces + t
            g_ref[c, 1] = dk[rows].T[0:64].astype(bf16)
            g_ref[c, 2] = dv[rows].T[0:64].astype(bf16)
            keys_back.send_tokens(g_ref.at[c, pl.ds(1, 2)], keys_target(me), c)

    def whole_block(turn, _):
        k_block(turn, None)
        return 0

    begin = 0
    for end, event in after:
        if end == int(end):
            if int(end) > begin:
                lax.fori_loop(begin, int(end), whole_block, 0)
            event()
            begin = int(end)
        else:
            k_block(begin, event)
            begin += 1

    def finish(s, _):
        c = lax.rem(me + s, OWNERS)
        rounded = dq[:, pl.ds(pl.multiple_of(c * SPAN, SPAN), SPAN)].astype(bf16)
        g_ref[c, 0] = (rounded.astype(f32) * HEAD_DIM ** (-0.5)).astype(bf16)
        query_back.send_tokens(g_ref.at[c, 0], token_slice(grads, me, 0), c)
        return 0

    lax.fori_loop(0, OWNERS, finish, 0)
    yield
    incoming.sent_heads(lambda n: d_ref.at[pl.ds(0, n)])
    keys_back.finish_tokens(g_ref.at[pl.ds(0, OWNERS - 1), pl.ds(1, 2)], grads.at[pl.ds(1, 2)])
    query_back.finish_tokens(g_ref.at[pl.ds(0, OWNERS - 1), 0], grads.at[0])


ORDERS = (("y", "z", "x"), ("z", "x", "y"), ("x", "y", "z"))
LEAD = ("x", "z", "y")
STAGES = ("y", "z", "x")


def axes_after(p, count):
    return [a for a in LEAD if a not in ORDERS[p][:count]]


def shape_after(p, count, width):
    shape = []
    for name in axes_after(p, count):
        shape += [2, 2] if name == "x" else [4]
    return tuple(shape) + (16, width)


def total_shape(width):
    return (2, 4, 4, 48, width)


class Reduce:
    def __init__(self, here, width, halves, merge, unpack, small, scratch):
        self.here, self.width, self.merge, self.unpack, self.small = here, width, merge, unpack, small
        self.halves = halves
        (self.acc, self.out, self.sums, self.landing, self.hall,
         self.core_send, self.core_recv, self.own_sem, self.send_sem, self.recv_sem,
         self.back_send, self.back_recv, self.small_send, self.small_recv) = scratch
        self.partner = device_at(here, core=1 - here["core"])
        self.peers = {
            axis: [device_at(here, **{axis: (here[axis] + d) % 4}) for d in (1, 2, 3)] for axis in STAGES
        }
        self.waits = []
        self.flying = [[], [], []]

    @staticmethod
    def scratch(width, halves, small_rows):
        shapes = []
        for shape in halves:
            shapes += [pltpu.VMEM((3, 2) + shape, bf16)] * 2
        shapes += [pltpu.VMEM(shape_after(p, 0, width), bf16) for p in range(3)]
        shapes.append(pltpu.VMEM(total_shape(width), bf16))
        for count in (1, 2):
            shapes += [pltpu.VMEM(shape_after(p, count, width), bf16) for p in range(3)]
        for count in (1, 2, 3):
            shapes += [pltpu.VMEM((3,) + shape_after(p, count, width), bf16) for p in range(3)]
        shapes.append(pltpu.VMEM((4, 4, small_rows, 128), f32))
        count = 3 * 2 * len(halves)
        shapes += [pltpu.SemaphoreType.DMA((count,))] * 3
        shapes += [pltpu.SemaphoreType.DMA((27,))] * 4
        shapes += [pltpu.SemaphoreType.DMA((12,))] * 2
        return shapes

    @staticmethod
    def unflatten(refs, tensors):
        refs = list(refs)
        pairs = [(refs[2 * n], refs[2 * n + 1]) for n in range(tensors)]
        refs = refs[2 * tensors :]
        acc, out, refs = refs[:3], refs[3], refs[4:]
        sums = [refs[0:3], refs[3:6]]
        landing = [refs[6:9], refs[9:12], refs[12:15]]
        return pairs, [acc, out, sums, landing] + refs[15:]

    def neighbours(self):
        return [self.partner] + [device for axis in STAGES for device in self.peers[axis]]

    def remote(self, src, dst, sems, slot, device):
        copy = pltpu.make_async_remote_copy(
            src, dst, sems[0].at[slot], sems[1].at[slot], device_id=device, device_id_type=MESH
        )
        copy.start()
        self.waits.append(copy)
        return copy

    def start(self):
        core = self.here["core"]
        self.core_copies = [[], [], []]
        slot = 0
        for p in range(3):
            for source, own, other in self.halves:
                for lo in range(2):
                    moved = self.remote(
                        source.at[lo, 1 - core, p], other.at[p, lo], (self.core_send, self.core_recv), slot,
                        self.partner,
                    )
                    kept = pltpu.make_async_copy(source.at[lo, core, p], own.at[p, lo], self.own_sem.at[slot])
                    kept.start()
                    self.core_copies[p].append((moved, kept))
                    slot += 1
        self.small_stage(0, self.small[...])

    def small_stage(self, stage, value):
        axis = STAGES[stage] if stage < 3 else "core"
        mine = self.hall.at[stage, self.here[axis]]
        mine[...] = value
        devices = self.peers[axis] if stage < 3 else [self.partner]
        self.small_flying = [
            self.remote(mine, mine, (self.small_send, self.small_recv), 3 * stage + d, device)
            for d, device in enumerate(devices)
        ]

    def small_sum(self, stage):
        for copy in self.small_flying:
            copy.wait_recv()
        value = self.hall[stage, 0]
        for n in range(1, 4 if stage < 3 else 2):
            value = value + self.hall[stage, n]
        return value

    def index(self, axes, axis, value):
        index = []
        for name in axes:
            if name == "x":
                index += [value % 2, value // 2] if axis == "x" else [slice(None), slice(None)]
            else:
                index.append(value if axis == name else slice(None))
        return tuple(index)

    def scatter(self, p, stage, source):
        axis, axes = ORDERS[p][stage], axes_after(p, stage)
        self.flying[p] = [
            self.remote(
                source.at[self.index(axes, axis, (self.here[axis] + d) % 4)], self.landing[stage][p].at[d - 1],
                (self.send_sem, self.recv_sem), (p * 3 + stage) * 3 + d - 1, self.peers[axis][d - 1],
            )
            for d in (1, 2, 3)
        ]

    def begin(self, p):
        for moved, kept in self.core_copies[p]:
            moved.wait_recv()
            kept.wait()
        self.merge(p, self.acc[p])
        self.scatter(p, 0, self.acc[p])

    def advance(self, p, stage):
        axis, axes = ORDERS[p][stage], axes_after(p, stage)
        source = self.acc[p] if stage == 0 else self.sums[stage - 1][p]
        kept = source.at[self.index(axes, axis, self.here[axis])]
        landing = self.landing[stage][p]
        for copy in self.flying[p]:
            copy.wait_recv()
        if stage < 2:
            target = self.sums[stage][p]
        else:
            target = self.out.at[self.here["x_hi"], self.here["z"], self.here["y"], pl.ds(16 * p, 16), :]
        lead = target.shape[:-2]
        total = 1
        for size in lead:
            total *= size

        def step(n, _):
            index, left = [], n
            for size in reversed(lead):
                index.insert(0, left % size)
                left = left // size
            index = tuple(index)
            value = kept[index].astype(f32)
            for d in range(3):
                value = value + landing[(d,) + index].astype(f32)
            target[index] = value.astype(bf16)
            return 0

        if lead:
            lax.fori_loop(0, total, step, 0)
            self.scatter(p, stage + 1, target)
        else:
            value = kept[...].astype(f32)
            for d in range(3):
                value = value + landing[d].astype(f32)
            target[...] = value.astype(bf16)
            self.spread(p, 0)

    def spread(self, p, stage):
        if stage:
            for copy in self.flying[p]:
                copy.wait_recv()
        if stage == 3:
            return
        axis = ORDERS[p][2 - stage]
        done = [ORDERS[p][2 - k] for k in range(stage)]
        index = tuple(
            slice(None) if name in done else self.here["x_hi" if name == "x" else name] for name in LEAD
        )
        piece = self.out.at[index + (pl.ds(16 * p, 16), slice(None))]
        devices = [device_at(self.here, x_hi=1 - self.here["x_hi"])] if axis == "x" else self.peers[axis]
        self.flying[p] = [
            self.remote(piece, piece, (self.back_send, self.back_recv), (p * 3 + stage) * 3 + d, device)
            for d, device in enumerate(devices)
        ]

    def step(self, number):
        for p in range(3):
            if number == 0:
                self.begin(p)
            elif number <= 3:
                self.advance(p, number - 1)
            else:
                self.spread(p, number - 3)
        if 1 <= number <= 3:
            self.small_stage(number, self.small_sum(number - 1))
        elif number == 4:
            self.small[...] = self.small_sum(3)

    def finish(self):
        self.unpack(self.out)
        for copy in self.waits:
            copy.wait_send()


def merge_blocks(p, pairs, acc, blocks):
    def step(n, _):
        lo, z = n // 4, n % 4

        def load(tensor, index):
            own, other = pairs[tensor]
            index = (p, lo, z) + index
            return own[index].astype(f32) + other[index].astype(f32)

        for (hi, y, left), value in blocks(load):
            acc[lo, hi, z, y, :, left : left + value.shape[1]] = value.astype(bf16)
        return 0

    lax.fori_loop(0, 8, step, 0)


def cut(value):
    return [value[:, n * 384 : (n + 1) * 384] for n in range(value.shape[1] // 384)]


def early_blocks(load):
    wide = cut(load(0, ()))
    found = [((n // 4, n % 4, 0), value) for n, value in enumerate(wide)]
    for y in range(4):
        found += [((hi, y, 384), value) for hi, value in enumerate(cut(load(1, (y,))))]
    return found


def late_blocks(load):
    pieces = cut(load(0, ())) + cut(load(1, ()))
    return [((n // 4, n % 4, 0), value) for n, value in enumerate(pieces)]


def early_unpack(expand_out, shrink_out):
    def unpack(out):
        def step(n, _):
            p, z = n // 4, n % 4
            band = pl.ds(pl.multiple_of(p * 16, 16), 16)
            rows = pl.ds(pl.multiple_of(n * 16, 16), 16)
            for hi in range(2):
                for y in range(4):
                    value = out[hi, z, y, band, :]
                    left = hi * 1536 + y * 384
                    expand_out[rows, left : left + 384] = value[:, 0:384]
                    below = pl.ds(pl.multiple_of(n * 64 + y * 16, 16), 16)
                    shrink_out[below, hi * 384 : hi * 384 + 384] = value[:, 384:768]
            return 0

        lax.fori_loop(0, 12, step, 0)

    return unpack


def late_unpack(output_out, attend_out):
    def unpack(out):
        def step(n, _):
            p, z = n // 4, n % 4
            band = pl.ds(pl.multiple_of(p * 16, 16), 16)
            rows = pl.ds(pl.multiple_of(n * 16, 16), 16)
            for m in range(8):
                value = out[m // 4, z, m % 4, band, :]
                if m < 2:
                    output_out[rows, m * 384 : m * 384 + 384] = value
                else:
                    attend_out[rows, (m - 2) * 384 : (m - 1) * 384] = value
            return 0

        lax.fori_loop(0, 12, step, 0)

    return unpack


REDUCE_STEPS = ((1, 0), (4, 1), (5, 2), (5.5, 3), (6, 4), (6.5, 5), (8, None))
EARLY_HALVES = ((4, 16, 3072), (4, 4, 16, 768))
LATE_HALVES = ((4, 16, 768), (4, 16, 2304))


def attend_back_kernel(
    len_ref, x_ref, o_ref, lse_ref, grad_ref, expand_src, shrink_src, small_src,
    grads, expand_out, shrink_out, small_out, *refs,
):
    attention, sems, refs = refs[:10], refs[10:16], refs[16:]
    pairs, scratch = Reduce.unflatten(refs, 2)
    small_out[...] = small_src[...]
    reduce = Reduce(
        place(), 768, [(source, *pair) for source, pair in zip((expand_src, shrink_src), pairs)],
        lambda p, acc: merge_blocks(p, pairs, acc, early_blocks), early_unpack(expand_out, shrink_out),
        small_out, scratch,
    )
    greet_all(reduce.neighbours(), owners=True)
    body = attend_back_body(
        len_ref, x_ref, o_ref, lse_ref, grad_ref, grads, *attention, sems, q_rows=512, k_rows=512, streams=2,
        after=[
            (end, (lambda: None) if number is None else functools.partial(reduce.step, number))
            for end, number in REDUCE_STEPS
        ],
    )
    next(body)
    reduce.start()
    next(body)
    reduce.step(6)
    reduce.finish()
    for _ in body:
        pass


def attend_back(valid, packed, mixed, lse, grad_mixed, expand_term, shrink_term, small, collective_id):
    vmem, anywhere = pl.BlockSpec(memory_space=pltpu.VMEM), pl.BlockSpec(memory_space=pl.ANY)
    return pl.pallas_call(
        attend_back_kernel,
        out_shape=(
            jax.ShapeDtypeStruct((3, HEADS, 64, 2 * SPAN), bf16),
            jax.ShapeDtypeStruct((192, 3072), bf16),
            jax.ShapeDtypeStruct((768, 768), bf16),
            jax.ShapeDtypeStruct(small.shape, f32),
        ),
        in_specs=[pl.BlockSpec(memory_space=pltpu.SMEM)] + [vmem] * 4 + [anywhere] * 2 + [vmem],
        out_specs=[vmem] * 4,
        scratch_shapes=[
            pltpu.VMEM((OWNERS, 64, SPAN), bf16),
            pltpu.VMEM((OWNERS, 3, 64, SPAN), bf16),
            pltpu.VMEM((128, LEN), bf16),
            pltpu.VMEM((LEN, 128), bf16),
            pltpu.VMEM((LEN, 128), bf16),
            pltpu.VMEM((64, LEN), bf16),
            pltpu.VMEM((LEN, 128), bf16),
            pltpu.VMEM((128, LEN), bf16),
            pltpu.VMEM((LEN, 128), bf16),
            pltpu.VMEM((64, LEN), f32),
        ] + exchange_sems(1) * 3 + Reduce.scratch(768, EARLY_HALVES, small.shape[0]),
        compiler_params=pltpu.CompilerParams(
            collective_id=collective_id, has_side_effects=True, vmem_limit_bytes=VMEM_BYTES
        ),
        name="attend_back",
    )(
        valid, packed, mixed, lse, grad_mixed, expand_term.reshape(2, 2, 3, 4, 16, 3072),
        shrink_term.reshape(2, 2, 3, 4, 4, 16, 768), small,
    )


def late_kernel(output_src, attend_src, small_src, output_out, attend_out, small_out, *refs):
    pairs, scratch = Reduce.unflatten(refs, 2)
    small_out[...] = small_src[...]
    reduce = Reduce(
        place(), 384, [(source, *pair) for source, pair in zip((output_src, attend_src), pairs)],
        lambda p, acc: merge_blocks(p, pairs, acc, late_blocks), late_unpack(output_out, attend_out),
        small_out, scratch,
    )
    greet_all(reduce.neighbours())
    reduce.start()
    for number in range(7):
        reduce.step(number)
    reduce.finish()


def late_reduce(output_term, attend_term, small, collective_id):
    vmem, anywhere = pl.BlockSpec(memory_space=pltpu.VMEM), pl.BlockSpec(memory_space=pl.ANY)
    return pl.pallas_call(
        late_kernel,
        out_shape=(
            jax.ShapeDtypeStruct((192, 768), bf16),
            jax.ShapeDtypeStruct((192, 2304), bf16),
            jax.ShapeDtypeStruct(small.shape, f32),
        ),
        in_specs=[anywhere] * 2 + [vmem],
        out_specs=[vmem] * 3,
        scratch_shapes=Reduce.scratch(384, LATE_HALVES, small.shape[0]),
        compiler_params=pltpu.CompilerParams(
            collective_id=collective_id, has_side_effects=True, vmem_limit_bytes=VMEM_BYTES
        ),
        name="late_reduce",
    )(output_term.reshape(2, 2, 3, 4, 16, 768), attend_term.reshape(2, 2, 3, 4, 16, 2304), small)


def per_device(
    inputs, lengths, attend_weight, query_bias, value_bias, output_weight, output_bias, norm_gain, norm_shift,
    expand_weight, expand_bias, shrink_weight, shrink_bias, final_gain, final_shift, cotangent,
):
    ctx, wt = lax.axis_index("ctx"), lax.axis_index("wt")
    vectors = (
        query_bias, value_bias, output_bias, norm_gain, norm_shift, expand_bias, shrink_bias, final_gain, final_shift,
    )
    seq_count, tok_local, model_width = inputs.shape
    row_count = seq_count * tok_local
    tokens = inputs.reshape(row_count, model_width)
    tokens_low = tokens.astype(bf16)
    seq, _, holds = head_of(ctx)
    my_length = jnp.where(holds, lengths[seq], 0).astype(jnp.int32).reshape(1)
    held, mixed_heads, lse, mixed, attend_full, small_full, output_full, expand_full, shrink_full = forward(
        my_length, tokens, attend_weight, vectors, (output_weight, expand_weight, shrink_weight), 0
    )
    mixed_low = mixed.reshape(model_width, row_count)
    small_full = small_full.reshape(4, 32, 768).astype(f32)
    _, _, output_add, gain_one, shift_one, expand_add, shrink_add, gain_two, shift_two = [
        small_full[:, n, : v.shape[0]].reshape(-1) for n, v in enumerate(vectors)
    ]

    attended = contract(mixed_low, output_full, 0, 0) + output_add
    hidden_one = tokens + attended
    normed_one = layer_norm(hidden_one, gain_one, shift_one)
    normed_low = normed_one.astype(bf16)
    raised = dot(normed_low, expand_full) + expand_add
    activated = exact_gelu(raised).astype(bf16)
    branch = dot(activated, shrink_full) + shrink_add
    hidden_two = normed_one + branch
    result = layer_norm(hidden_two, gain_two, shift_two)

    upstream = cotangent.reshape(row_count, model_width)
    grad_two, final_gain_term, final_shift_term = norm_pullback(hidden_two, gain_two, upstream)
    branch_low = grad_two.astype(bf16)
    shrink_bias_term = jnp.sum(branch_low.astype(f32), axis=0)
    shrink_term = contract(activated, branch_low, 0, 0)
    grad_active = contract(branch_low, shrink_full, 1, 1)
    _, gelu_pull = jax.vjp(exact_gelu, raised)
    raised_low = gelu_pull(grad_active)[0].astype(bf16)
    expand_bias_term = jnp.sum(raised_low.astype(f32), axis=0)
    expand_term = contract(normed_low, raised_low, 0, 0)
    grad_normed = grad_two + contract(raised_low, expand_full, 1, 1)
    grad_one, norm_gain_term, norm_shift_term = norm_pullback(hidden_one, gain_one, grad_normed)
    attended_low = grad_one.astype(bf16)
    output_bias_term = jnp.sum(attended_low.astype(f32), axis=0)
    output_term = dot(mixed_low, attended_low)
    grad_mixed = contract(output_full, attended_low, 1, 1).astype(bf16)

    early = jnp.concatenate(
        [t.reshape(4, -1) for t in (
            output_bias_term, norm_gain_term, norm_shift_term, expand_bias_term, shrink_bias_term,
            final_gain_term, final_shift_term)] + [jnp.zeros((4, 128), f32)], axis=1,
    ).reshape(64, 128)
    grad_packed, expand_grad, shrink_grad, early = attend_back(
        my_length, held, mixed_heads, lse, grad_mixed.reshape(HEADS, 64, row_count), expand_term.astype(bf16), shrink_term.astype(bf16), early, 1
    )
    grad_packed = grad_packed.reshape(3 * model_width, row_count)
    attend_term = contract(tokens_low, grad_packed, 0, 1)
    input_grad = grad_one + contract(grad_packed, attend_full, 0, 1)
    query_bias_term = jnp.sum(grad_packed[:model_width].astype(f32), axis=1)
    value_bias_term = jnp.sum(grad_packed[2 * model_width :].astype(f32), axis=1)

    late = jnp.concatenate(
        [t.reshape(4, -1) for t in (query_bias_term, value_bias_term)] + [jnp.zeros((4, 128), f32)], axis=1
    ).reshape(16, 128)
    output_grad, attend_grad, late = late_reduce(output_term.astype(bf16), attend_term.astype(bf16), late, 2)
    early = lax.dynamic_index_in_dim(early.reshape(4, 2048), wt, 0, keepdims=False)
    late = lax.dynamic_index_in_dim(late.reshape(4, 512), wt, 0, keepdims=False)
    n = 192
    return (
        result.reshape(inputs.shape),
        input_grad.reshape(inputs.shape),
        attend_grad.astype(f32),
        late[:n],
        late[n : 2 * n],
        output_grad.astype(f32),
        early[0:n],
        early[n : 2 * n],
        early[2 * n : 3 * n],
        expand_grad.astype(f32),
        early[3 * n : 7 * n],
        shrink_grad.astype(f32),
        early[7 * n : 8 * n],
        early[8 * n : 9 * n],
        early[9 * n : 10 * n],
    )


def solution(mesh):
    wide, rows, flat = P("wt", "ctx", None), P("wt", None), P("wt")
    return jax.shard_map(
        per_device,
        mesh=mesh,
        in_specs=(
            wide, flat, rows, flat, flat, rows, flat, flat, flat, rows, flat, rows, flat, flat, flat, wide,
        ),
        out_specs=(
            wide, wide, rows, flat, flat, rows, flat, flat, flat, rows, flat, rows, flat, flat, flat,
        ),
        check_vma=False,
    )
```

```python
import functools

import jax
import jax.numpy as jnp
from jax import lax
from jax.experimental import pallas as pl
from jax.experimental.pallas import tpu as pltpu
from jax.sharding import PartitionSpec as P

HEADS = 12
HEAD_DIM = 64
LEN = 4096
WIDTH = 768
OWNERS = 32
PAIRS = 24
VMEM_BYTES = 58 << 20
SPAN = 128
MASKED = -1e30
norm_eps = 1e-06
f32 = jnp.float32
bf16 = jnp.bfloat16
MESH = pl.DeviceIdType.MESH


def layer_norm(values, gain_row, shift_row):
    centered = values - jnp.mean(values, axis=-1, keepdims=True)
    variance = jnp.mean(centered * centered, axis=-1, keepdims=True)
    return centered * lax.rsqrt(variance + norm_eps) * gain_row + shift_row


def norm_pullback(values, gain_row, upstream):
    _, pulled = jax.vjp(lambda inside, scaled: layer_norm(inside, scaled, 0.0), values, gain_row)
    grad_values, grad_gain = pulled(upstream)
    return (grad_values, grad_gain, jnp.sum(upstream, axis=0))


def exact_gelu(values):
    return 0.5 * values * (1.0 + lax.erf(values * 0.5**0.5))


def dot(left, right):
    return jnp.dot(left, right, preferred_element_type=f32)


def contract(left, right, left_dim, right_dim):
    return lax.dot_general(
        left, right, (((left_dim,), (right_dim,)), ((), ())), preferred_element_type=f32
    )


def head_of(ctx):
    z, y = lax.rem(lax.div(ctx, 4), 4), lax.rem(ctx, 4)
    turn = lax.rem(y + 7 - z, 4)
    return lax.div(ctx, 16), 3 * z + jnp.minimum(turn, 2), turn < 3


def token_slice(ref, ctx, *lead):
    seq, head, _ = head_of(ctx)
    return ref.at[lead + (head, slice(None), pl.ds(pl.multiple_of(seq * SPAN, SPAN), SPAN))]


def wait_bytes(ref, sem):
    pltpu.make_async_copy(ref, ref, sem).wait()


class Exchange:
    def __init__(self, send_sem, recv_sem):
        self.me = lax.axis_index("ctx")
        self.holds = head_of(self.me)[2]
        self.send_sem, self.recv_sem = send_sem, recv_sem

    def copy(self, src, dst, peer, slot):
        pltpu.make_async_remote_copy(
            src, dst, self.send_sem, self.recv_sem.at[slot], device_id={"ctx": peer}, device_id_type=MESH
        ).start()

    def send_heads(self, source, mine, slot):
        def start(s, _):
            n = lax.rem(s + self.me, PAIRS)
            seq, head = lax.div(n, HEADS), lax.rem(n, HEADS)
            z = lax.div(head, 3)
            peer = seq * 16 + z * 4 + lax.rem(z + 1 + lax.rem(head, 3), 4)

            @pl.when(peer != self.me)
            def _():
                self.copy(source(seq, head), mine, peer, slot)

            return 0

        lax.fori_loop(0, PAIRS, start, 0)

        @pl.when(self.holds)
        def _():
            seq, head, _ = head_of(self.me)
            pltpu.make_async_copy(source(seq, head), mine, self.recv_sem.at[slot]).start()

    def sent_heads(self, stand_in):
        @pl.when(self.holds)
        def _():
            wait_bytes(stand_in(PAIRS - 1), self.send_sem)

        @pl.when(jnp.logical_not(self.holds))
        def _():
            wait_bytes(stand_in(PAIRS), self.send_sem)

    def take_heads(self, landed, slot):
        @pl.when(self.holds)
        def _():
            wait_bytes(landed, self.recv_sem.at[slot])

    def send_tokens(self, source, target, peer):
        @pl.when(jnp.logical_and(self.holds, peer == self.me))
        def _():
            pltpu.make_async_copy(source, target, self.recv_sem.at[0]).start()

        @pl.when(jnp.logical_and(self.holds, peer != self.me))
        def _():
            self.copy(source, target, peer, 0)

    def finish_tokens(self, sent, landed):
        @pl.when(self.holds)
        def _():
            wait_bytes(sent, self.send_sem)

        wait_bytes(landed, self.recv_sem.at[0])


def exchange_sems(slots):
    return [pltpu.SemaphoreType.DMA(()), pltpu.SemaphoreType.DMA((slots,))]


def place():
    ctx, wt = lax.axis_index("ctx"), lax.axis_index("wt")
    return dict(
        x_hi=ctx // 16, z=(ctx // 4) % 4, y=ctx % 4, x_lo=wt // 2, core=wt % 2, x=(ctx // 16) * 2 + wt // 2
    )


def device_at(here, **change):
    at = dict(here)
    if "x" in change:
        at["x_hi"], at["x_lo"] = change["x"] // 2, change["x"] % 2
        change = {k: v for k, v in change.items() if k != "x"}
    at.update(change)
    return (at["x_hi"] * 16 + at["z"] * 4 + at["y"], at["x_lo"] * 2 + at["core"])


def greet_all(devices, owners=False):
    barrier = pltpu.get_barrier_semaphore()
    for device in devices:
        pl.semaphore_signal(barrier, 1, device_id=device, device_id_type=MESH)
    count = len(devices)
    if owners:
        me = lax.axis_index("ctx")

        def greet(s, _):
            pl.semaphore_signal(barrier, 1, device_id={"ctx": lax.rem(me + s, OWNERS)}, device_id_type=MESH)
            return 0

        lax.fori_loop(1, OWNERS, greet, 0)
        count += OWNERS - 1
    pl.semaphore_wait(barrier, count)


class WeightGather:
    def __init__(self, here, shards, fulls, send_sem, recv_sem, local_sem):
        self.partner = device_at(here, core=1 - here["core"])
        self.ahead = device_at(here, x=(here["x"] + 1) % 4)
        self.behind = device_at(here, x=(here["x"] + 3) % 4)
        self.mine = here["x_lo"] * 2 + here["core"]
        self.far = (1 - here["x_lo"]) * 2 + here["core"]
        self.shards, self.fulls = shards, fulls
        self.sems = send_sem, recv_sem, local_sem
        self.sent, self.local, self.handed = [], [], []

    def neighbours(self):
        return [self.partner, self.ahead, self.behind]

    def remote(self, src, dst, slot, n, device):
        return pltpu.make_async_remote_copy(
            src, dst, self.sems[0].at[slot, n], self.sems[1].at[slot, n], device_id=device, device_id_type=MESH
        )

    def start(self, first, last):
        for n in range(first, last):
            shard, full = self.shards[n], self.fulls[n]
            rows = shard.shape[0]
            half = rows // 2

            def part(owner, h, full=full, rows=rows, half=half):
                return full.at[pl.ds(pl.multiple_of(owner * rows + h * half, 16), half), :]

            whole = full.at[pl.ds(pl.multiple_of(self.mine * rows, 16), rows), :]
            copies = [
                self.remote(shard.at[pl.ds(0, half), :], part(self.mine, 0), 0, n, self.ahead),
                self.remote(shard.at[pl.ds(half, half), :], part(self.mine, 1), 1, n, self.behind),
                self.remote(shard, whole, 2, n, self.partner),
            ]
            own = pltpu.make_async_copy(shard, whole, self.sems[2].at[n])
            for copy in copies + [own]:
                copy.start()
            self.sent.append(copies)
            self.local.append(own)
            self.handed.append(
                [self.remote(part(self.far, h), part(self.far, h), 3 + h, n, self.partner) for h in (0, 1)]
            )

    def hand_on(self, n):
        for h in (0, 1):
            self.sent[n][h].wait_recv()
            self.handed[n][h].start()

    def ready(self, n):
        self.local[n].wait()
        self.sent[n][2].wait_recv()
        for copy in self.handed[n]:
            copy.wait_recv()

    def finish(self, unready):
        for n, (copies, handed) in enumerate(zip(self.sent, self.handed)):
            if n in unready:
                self.ready(n)
            for copy in copies + handed:
                copy.wait_send()


THIRDS = (1, 2, 0)


def forward_kernel(
    len_ref, tok_ref, weight, v0, v1, v2, v3, v4, v5, v6, v7, v8, w0, w1, w2,
    x_ref, o_ref, lse_ref, mixed, attend_out, small_out, f0, f1, f2,
    low, full, small, small_low, small_full, packed, low_ref, qn, kt, vn, b0, b1, b2,
    send_sem, recv_sem, local_sem, out_sem, ka, kb, va, vb, qa, qb, ma, mb, *, q_rows, k_rows,
):
    valid = len_ref[0]
    me = lax.axis_index("ctx")
    columns = [pl.ds(t * WIDTH, WIDTH) for t in range(3)]
    gather = WeightGather(
        place(),
        [small_low] + [low.at[:, columns[t]] for t in THIRDS] + [b0, b1, b2],
        [small_full] + [full.at[:, columns[t]] for t in THIRDS] + [f0, f1, f2],
        send_sem, recv_sem, local_sem,
    )
    small[...] = jnp.zeros_like(small)
    for n, vector in enumerate((v0, v1, v2, v3, v4, v5, v6, v7, v8)):
        small[n : n + 1, 0 : vector.shape[1]] = vector[...]
    small_low[...] = small[...].astype(bf16)
    low[...] = weight[...].astype(bf16)
    greet_all(gather.neighbours(), owners=True)
    gather.start(0, 4)
    for narrow, wide in ((b0, w0), (b1, w1), (b2, w2)):
        narrow[...] = wide[...].astype(bf16)
    tokens = tok_ref[...].astype(bf16)
    moves = {1: Exchange(ka, kb), 2: Exchange(va, vb), 0: Exchange(qa, qb)}
    pieces = q_rows // SPAN
    steps = LEN // q_rows
    offset = lax.div(me, pieces)

    def source(third):
        return lambda seq, head: packed.at[third, head, :, pl.ds(pl.multiple_of(seq * SPAN, SPAN), SPAN)]

    gather.hand_on(0)
    gather.hand_on(1)
    gather.ready(0)

    def bias(row):
        rows = [small_full[32 * w : 32 * w + 16, 0:192].astype(f32)[row : row + 1] for w in range(4)]
        return jnp.concatenate(rows, axis=1)

    biases = {0: bias(0), 1: None, 2: bias(1)}
    for order, third in enumerate(THIRDS):
        if order < 2:
            gather.hand_on(order + 2)
        gather.ready(order + 1)
        product = dot(tokens, full[:, third * WIDTH : (third + 1) * WIDTH])
        if biases[third] is not None:
            product = product + biases[third]
        if third == 0:
            product = product * HEAD_DIM ** (-0.5)
        packed[third] = product.T.astype(bf16).reshape(HEADS, 64, 2 * SPAN)
        moves[third].send_heads(source(third), x_ref.at[me, third], 0 if third else offset)
    outs = [pltpu.make_async_copy(full, attend_out, out_sem.at[0]), pltpu.make_async_copy(small_full, small_out, out_sem.at[1])]
    for copy in outs:
        copy.start()
    lane = lax.broadcasted_iota(jnp.int32, (64, 128), 1)
    first = lax.broadcasted_iota(jnp.int32, (64, 128), 0) == 0
    zero = jnp.zeros((64, 128), f32)
    one_row = jnp.where(first, 1.0, zero)

    def prepare_keys(c, _):
        here = pl.ds(pl.multiple_of(c * SPAN, SPAN), SPAN)
        kt[0:64, here] = x_ref[c, 1]
        mask = jnp.where(lane + c * SPAN < valid, 0.0, MASKED)
        kt[64:128, here] = jnp.where(first, mask, zero).astype(bf16)
        return 0

    def prepare_values(c, _):
        here = pl.ds(pl.multiple_of(c * SPAN, SPAN), SPAN)
        vn[here, :] = jnp.concatenate([x_ref[c, 2].astype(f32), one_row], 0).T.astype(bf16)
        return 0

    moves[1].take_heads(x_ref.at[:, 1], 0)
    lax.fori_loop(0, OWNERS, prepare_keys, 0)
    moves[2].take_heads(x_ref.at[:, 2], 0)
    gather.start(4, 7)
    lax.fori_loop(0, OWNERS, prepare_values, 0)
    target = token_slice(mixed, me)

    def q_block(turn, _):
        i = lax.rem(turn + offset, steps)
        moves[0].take_heads(x_ref.at[pl.ds(i * pieces, pieces), 0], i)
        for t in range(pieces):
            c = i * pieces + t
            here = pl.ds(pl.multiple_of(c * SPAN, SPAN), SPAN)
            qn[here, :] = jnp.concatenate([x_ref[c, 0].astype(f32), one_row], 0).T.astype(bf16)
        q = qn[pl.ds(pl.multiple_of(i * q_rows, q_rows), q_rows), :]

        def k_block(j, carry):
            peak, acc = carry
            here = pl.ds(pl.multiple_of(j * k_rows, k_rows), k_rows)
            scores = dot(q, kt[:, here])
            folded = scores[:, 0:128]
            for t in range(1, k_rows // 128):
                folded = jnp.maximum(folded, scores[:, t * 128 : (t + 1) * 128])
            peak_new = jnp.maximum(peak, jnp.max(folded, axis=1, keepdims=True))
            weights = jnp.exp(scores - peak_new).astype(bf16)
            return peak_new, acc * jnp.exp(peak - peak_new) + dot(weights, vn[here, :])

        start = (jnp.full((q_rows, 1), -3e38, f32), jnp.zeros((q_rows, 128), f32))
        peak, acc = lax.fori_loop(0, LEN // k_rows, k_block, start)
        total = acc[:, 64:65]
        column = lax.broadcasted_iota(jnp.int32, (q_rows, 128), 1)
        finished = jnp.where(column == 64, peak + jnp.log(total), acc / total).T
        for t in range(pieces):
            c = i * pieces + t
            cols = slice(t * SPAN, (t + 1) * SPAN)
            o_ref[c] = finished[0:64, cols]
            low_ref[c] = finished[0:64, cols].astype(bf16)
            lse_ref[c] = finished[64:72, cols]
            back.send_tokens(low_ref.at[c], target, c)
        return 0

    back = Exchange(ma, mb)
    cuts = (0, steps // 2, steps - 2, steps - 1)
    for n in range(3):
        lax.fori_loop(cuts[n], cuts[n + 1], q_block, 0)
        gather.hand_on(n + 4)
    lax.fori_loop(steps - 1, steps, q_block, 0)
    for third in THIRDS:
        moves[third].sent_heads(lambda n, third=third: x_ref.at[pl.ds(0, n), third])
    for copy in outs:
        copy.wait()
    gather.finish((4, 5, 6))
    back.finish_tokens(low_ref.at[pl.ds(0, OWNERS - 1)], mixed)


def forward(valid, tokens, weight, vectors, shards, collective_id):
    vmem, anywhere = pl.BlockSpec(memory_space=pltpu.VMEM), pl.BlockSpec(memory_space=pl.ANY)
    rows, width = weight.shape
    return pl.pallas_call(
        functools.partial(forward_kernel, q_rows=512, k_rows=1024),
        out_shape=(
            jax.ShapeDtypeStruct((OWNERS, 3, 64, SPAN), bf16),
            jax.ShapeDtypeStruct((OWNERS, 64, SPAN), f32),
            jax.ShapeDtypeStruct((OWNERS, 8, SPAN), f32),
            jax.ShapeDtypeStruct((HEADS, 64, 2 * SPAN), bf16),
            jax.ShapeDtypeStruct((4 * rows, width), bf16),
            jax.ShapeDtypeStruct((128, 768), bf16),
        ) + tuple(jax.ShapeDtypeStruct((4 * s.shape[0], s.shape[1]), bf16) for s in shards),
        in_specs=[pl.BlockSpec(memory_space=pltpu.SMEM)] + [vmem] * 14,
        out_specs=[vmem] * 4 + [anywhere] * 5,
        scratch_shapes=[
            pltpu.VMEM((rows, width), bf16),
            pltpu.VMEM((4 * rows, width), bf16),
            pltpu.VMEM((32, 768), f32),
            pltpu.VMEM((32, 768), bf16),
            pltpu.VMEM((128, 768), bf16),
            pltpu.VMEM((3, HEADS, 64, 2 * SPAN), bf16),
            pltpu.VMEM((OWNERS, 64, SPAN), bf16),
            pltpu.VMEM((LEN, 128), bf16),
            pltpu.VMEM((128, LEN), bf16),
            pltpu.VMEM((LEN, 128), bf16),
        ] + [pltpu.VMEM(s.shape, bf16) for s in shards] + [
            pltpu.SemaphoreType.DMA((5, 7)), pltpu.SemaphoreType.DMA((5, 7)), pltpu.SemaphoreType.DMA((7,)),
            pltpu.SemaphoreType.DMA((2,)),
        ] + exchange_sems(1) * 2 + exchange_sems(LEN // 512) + exchange_sems(1),
        compiler_params=pltpu.CompilerParams(
            collective_id=collective_id, has_side_effects=True, vmem_limit_bytes=VMEM_BYTES
        ),
        name="forward",
    )(valid, tokens, weight, *[v.reshape(1, -1) for v in vectors], *shards)


def split_terms(values):
    high = values.astype(bf16).astype(f32)
    rest = values - high
    middle = rest.astype(bf16).astype(f32)
    return high, middle, rest - middle


def attend_back_body(
    len_ref, x_ref, o_ref, lse_ref, grad_ref, grads, d_ref, g_ref, qt, qn, kn, kt, vn, dt, dn, dq, sems,
    *, q_rows, k_rows, streams, after,
):
    valid = len_ref[0]
    me = lax.axis_index("ctx")
    lane = lax.broadcasted_iota(jnp.int32, (64, 128), 1)
    row = lax.broadcasted_iota(jnp.int32, (64, 128), 0)
    zero = jnp.zeros((64, 128), f32)
    incoming, keys_back, query_back = [Exchange(*sems[2 * n : 2 * n + 2]) for n in range(3)]

    def source(seq, head):
        return grad_ref.at[head, :, pl.ds(pl.multiple_of(seq * SPAN, SPAN), SPAN)]

    incoming.send_heads(source, d_ref.at[me], 0)
    yield

    def prepare(c, _):
        here = pl.ds(pl.multiple_of(c * SPAN, SPAN), SPAN)
        q = x_ref[c, 0].astype(f32)
        k = x_ref[c, 1].astype(f32)
        v = x_ref[c, 2].astype(f32)
        high, middle, rest = split_terms(-lse_ref[c][0:1])
        q_extra = jnp.where(
            row == 0, 1.0, jnp.where(row == 1, high, jnp.where(row == 2, middle, jnp.where(row == 3, rest, 0.0)))
        )
        mask = jnp.where(lane + c * SPAN < valid, 0.0, MASKED)
        k_extra = jnp.where(row == 0, mask, jnp.where(row < 4, 1.0, 0.0))
        qt[:, here] = jnp.concatenate([q, q_extra], 0).astype(bf16)
        qn[here, :] = jnp.concatenate([q, zero], 0).T.astype(bf16)
        kn[here, :] = jnp.concatenate([k, k_extra], 0).T.astype(bf16)
        kt[:, here] = k.astype(bf16)
        v_extra = jnp.where(row < 3, 1.0, zero)
        vn[here, :] = jnp.concatenate([v, v_extra], 0).T.astype(bf16)
        return 0

    def prepare_grads(c, _):
        here = pl.ds(pl.multiple_of(c * SPAN, SPAN), SPAN)
        do = d_ref[c].astype(f32)
        delta = jnp.sum(do * o_ref[c], axis=0, keepdims=True)
        high, middle, rest = split_terms(-delta)
        d_extra = jnp.where(row == 0, high, jnp.where(row == 1, middle, jnp.where(row == 2, rest, 0.0)))
        dt[:, here] = jnp.concatenate([do, d_extra], 0).astype(bf16)
        dn[here, :] = jnp.concatenate([do, zero], 0).T.astype(bf16)
        return 0

    lax.fori_loop(0, OWNERS, prepare, 0)
    dq[...] = jnp.zeros_like(dq)
    incoming.take_heads(d_ref, 0)
    lax.fori_loop(0, OWNERS, prepare_grads, 0)
    pieces = k_rows // SPAN
    steps = LEN // k_rows
    offset = lax.div(me, pieces)

    def keys_target(c):
        seq, head, _ = head_of(c)
        return grads.at[pl.ds(1, 2), head, :, pl.ds(pl.multiple_of(seq * SPAN, SPAN), SPAN)]

    def k_block(turn, middle):
        j = lax.rem(turn + offset, steps)
        here = pl.ds(pl.multiple_of(j * k_rows, k_rows), k_rows)
        k, v, k_flat = kn[here, :], vn[here, :], kt[:, here]

        def q_block(i, carry):
            dk, dv = carry
            for s in range(streams):
                cols = pl.ds(pl.multiple_of(i * (q_rows * streams) + s * q_rows, q_rows), q_rows)
                weights = jnp.exp(dot(k, qt[:, cols]))
                ds = (weights * dot(v, dt[:, cols])).astype(bf16)
                dv = dv + dot(weights.astype(bf16), dn[cols, :])
                dk = dk + dot(ds, qn[cols, :])
                dq[:, cols] += dot(k_flat, ds)
            return dk, dv

        start = jnp.zeros((k_rows, 128), f32)
        count = LEN // (q_rows * streams)
        if middle is None:
            dk, dv = lax.fori_loop(0, count, q_block, (start, start))
        else:
            carry = lax.fori_loop(0, count // 2, q_block, (start, start))
            middle()
            dk, dv = lax.fori_loop(count // 2, count, q_block, carry)
        for t in range(pieces):
            rows = slice(t * SPAN, (t + 1) * SPAN)
            c = j * pieces + t
            g_ref[c, 1] = dk[rows].T[0:64].astype(bf16)
            g_ref[c, 2] = dv[rows].T[0:64].astype(bf16)
            keys_back.send_tokens(g_ref.at[c, pl.ds(1, 2)], keys_target(me), c)

    def whole_block(turn, _):
        k_block(turn, None)
        return 0

    begin = 0
    for end, event in after:
        if end == int(end):
            if int(end) > begin:
                lax.fori_loop(begin, int(end), whole_block, 0)
            event()
            begin = int(end)
        else:
            k_block(begin, event)
            begin += 1

    def finish(s, _):
        c = lax.rem(me + s, OWNERS)
        rounded = dq[:, pl.ds(pl.multiple_of(c * SPAN, SPAN), SPAN)].astype(bf16)
        g_ref[c, 0] = (rounded.astype(f32) * HEAD_DIM ** (-0.5)).astype(bf16)
        query_back.send_tokens(g_ref.at[c, 0], token_slice(grads, me, 0), c)
        return 0

    lax.fori_loop(0, OWNERS, finish, 0)
    yield
    incoming.sent_heads(lambda n: d_ref.at[pl.ds(0, n)])
    keys_back.finish_tokens(g_ref.at[pl.ds(0, OWNERS - 1), pl.ds(1, 2)], grads.at[pl.ds(1, 2)])
    query_back.finish_tokens(g_ref.at[pl.ds(0, OWNERS - 1), 0], grads.at[0])


ORDERS = (("y", "z", "x"), ("z", "x", "y"), ("x", "y", "z"))
LEAD = ("x", "z", "y")
STAGES = ("y", "z", "x")


def axes_after(p, count):
    return [a for a in LEAD if a not in ORDERS[p][:count]]


def shape_after(p, count, width):
    shape = []
    for name in axes_after(p, count):
        shape += [2, 2] if name == "x" else [4]
    return tuple(shape) + (16, width)


def total_shape(width):
    return (2, 4, 4, 48, width)


class Reduce:
    def __init__(self, here, width, halves, merge, unpack, small, scratch):
        self.here, self.width, self.merge, self.unpack, self.small = here, width, merge, unpack, small
        self.halves = halves
        (self.acc, self.out, self.sums, self.landing, self.hall,
         self.core_send, self.core_recv, self.own_sem, self.send_sem, self.recv_sem,
         self.back_send, self.back_recv, self.small_send, self.small_recv) = scratch
        self.partner = device_at(here, core=1 - here["core"])
        self.peers = {
            axis: [device_at(here, **{axis: (here[axis] + d) % 4}) for d in (1, 2, 3)] for axis in STAGES
        }
        self.waits = []
        self.flying = [[], [], []]

    @staticmethod
    def scratch(width, halves, small_rows):
        shapes = []
        for shape in halves:
            shapes += [pltpu.VMEM((3, 2) + shape, bf16)] * 2
        shapes += [pltpu.VMEM(shape_after(p, 0, width), bf16) for p in range(3)]
        shapes.append(pltpu.VMEM(total_shape(width), bf16))
        for count in (1, 2):
            shapes += [pltpu.VMEM(shape_after(p, count, width), bf16) for p in range(3)]
        for count in (1, 2, 3):
            shapes += [pltpu.VMEM((3,) + shape_after(p, count, width), bf16) for p in range(3)]
        shapes.append(pltpu.VMEM((4, 4, small_rows, 128), f32))
        count = 3 * 2 * len(halves)
        shapes += [pltpu.SemaphoreType.DMA((count,))] * 3
        shapes += [pltpu.SemaphoreType.DMA((27,))] * 4
        shapes += [pltpu.SemaphoreType.DMA((12,))] * 2
        return shapes

    @staticmethod
    def unflatten(refs, tensors):
        refs = list(refs)
        pairs = [(refs[2 * n], refs[2 * n + 1]) for n in range(tensors)]
        refs = refs[2 * tensors :]
        acc, out, refs = refs[:3], refs[3], refs[4:]
        sums = [refs[0:3], refs[3:6]]
        landing = [refs[6:9], refs[9:12], refs[12:15]]
        return pairs, [acc, out, sums, landing] + refs[15:]

    def neighbours(self):
        return [self.partner] + [device for axis in STAGES for device in self.peers[axis]]

    def remote(self, src, dst, sems, slot, device):
        copy = pltpu.make_async_remote_copy(
            src, dst, sems[0].at[slot], sems[1].at[slot], device_id=device, device_id_type=MESH
        )
        copy.start()
        self.waits.append(copy)
        return copy

    def start(self):
        core = self.here["core"]
        self.core_copies = [[], [], []]
        slot = 0
        for p in range(3):
            for source, own, other in self.halves:
                for lo in range(2):
                    moved = self.remote(
                        source.at[lo, 1 - core, p], other.at[p, lo], (self.core_send, self.core_recv), slot,
                        self.partner,
                    )
                    kept = pltpu.make_async_copy(source.at[lo, core, p], own.at[p, lo], self.own_sem.at[slot])
                    kept.start()
                    self.core_copies[p].append((moved, kept))
                    slot += 1
        self.small_stage(0, self.small[...])

    def small_stage(self, stage, value):
        axis = STAGES[stage] if stage < 3 else "core"
        mine = self.hall.at[stage, self.here[axis]]
        mine[...] = value
        devices = self.peers[axis] if stage < 3 else [self.partner]
        self.small_flying = [
            self.remote(mine, mine, (self.small_send, self.small_recv), 3 * stage + d, device)
            for d, device in enumerate(devices)
        ]

    def small_sum(self, stage):
        for copy in self.small_flying:
            copy.wait_recv()
        value = self.hall[stage, 0]
        for n in range(1, 4 if stage < 3 else 2):
            value = value + self.hall[stage, n]
        return value

    def index(self, axes, axis, value):
        index = []
        for name in axes:
            if name == "x":
                index += [value % 2, value // 2] if axis == "x" else [slice(None), slice(None)]
            else:
                index.append(value if axis == name else slice(None))
        return tuple(index)

    def scatter(self, p, stage, source):
        axis, axes = ORDERS[p][stage], axes_after(p, stage)
        self.flying[p] = [
            self.remote(
                source.at[self.index(axes, axis, (self.here[axis] + d) % 4)], self.landing[stage][p].at[d - 1],
                (self.send_sem, self.recv_sem), (p * 3 + stage) * 3 + d - 1, self.peers[axis][d - 1],
            )
            for d in (1, 2, 3)
        ]

    def begin(self, p):
        for moved, kept in self.core_copies[p]:
            moved.wait_recv()
            kept.wait()
        self.merge(p, self.acc[p])
        self.scatter(p, 0, self.acc[p])

    def advance(self, p, stage):
        axis, axes = ORDERS[p][stage], axes_after(p, stage)
        source = self.acc[p] if stage == 0 else self.sums[stage - 1][p]
        kept = source.at[self.index(axes, axis, self.here[axis])]
        landing = self.landing[stage][p]
        for copy in self.flying[p]:
            copy.wait_recv()
        if stage < 2:
            target = self.sums[stage][p]
        else:
            target = self.out.at[self.here["x_hi"], self.here["z"], self.here["y"], pl.ds(16 * p, 16), :]
        lead = target.shape[:-2]
        total = 1
        for size in lead:
            total *= size

        def step(n, _):
            index, left = [], n
            for size in reversed(lead):
                index.insert(0, left % size)
                left = left // size
            index = tuple(index)
            value = kept[index].astype(f32)
            for d in range(3):
                value = value + landing[(d,) + index].astype(f32)
            target[index] = value.astype(bf16)
            return 0

        if lead:
            lax.fori_loop(0, total, step, 0)
            self.scatter(p, stage + 1, target)
        else:
            value = kept[...].astype(f32)
            for d in range(3):
                value = value + landing[d].astype(f32)
            target[...] = value.astype(bf16)
            self.spread(p, 0)

    def spread(self, p, stage):
        if stage:
            for copy in self.flying[p]:
                copy.wait_recv()
        if stage == 3:
            return
        axis = ORDERS[p][2 - stage]
        done = [ORDERS[p][2 - k] for k in range(stage)]
        index = tuple(
            slice(None) if name in done else self.here["x_hi" if name == "x" else name] for name in LEAD
        )
        piece = self.out.at[index + (pl.ds(16 * p, 16), slice(None))]
        devices = [device_at(self.here, x_hi=1 - self.here["x_hi"])] if axis == "x" else self.peers[axis]
        self.flying[p] = [
            self.remote(piece, piece, (self.back_send, self.back_recv), (p * 3 + stage) * 3 + d, device)
            for d, device in enumerate(devices)
        ]

    def step(self, number):
        for p in range(3):
            if number == 0:
                self.begin(p)
            elif number <= 3:
                self.advance(p, number - 1)
            else:
                self.spread(p, number - 3)
        if 1 <= number <= 3:
            self.small_stage(number, self.small_sum(number - 1))
        elif number == 4:
            self.small[...] = self.small_sum(3)

    def finish(self):
        self.unpack(self.out)
        for copy in self.waits:
            copy.wait_send()


def merge_blocks(p, pairs, acc, blocks):
    def step(n, _):
        lo, z = n // 4, n % 4

        def load(tensor, index):
            own, other = pairs[tensor]
            index = (p, lo, z) + index
            return own[index].astype(f32) + other[index].astype(f32)

        for (hi, y, left), value in blocks(load):
            acc[lo, hi, z, y, :, left : left + value.shape[1]] = value.astype(bf16)
        return 0

    lax.fori_loop(0, 8, step, 0)


def cut(value):
    return [value[:, n * 384 : (n + 1) * 384] for n in range(value.shape[1] // 384)]


def early_blocks(load):
    wide = cut(load(0, ()))
    found = [((n // 4, n % 4, 0), value) for n, value in enumerate(wide)]
    for y in range(4):
        found += [((hi, y, 384), value) for hi, value in enumerate(cut(load(1, (y,))))]
    return found


def late_blocks(load):
    pieces = cut(load(0, ())) + cut(load(1, ()))
    return [((n // 4, n % 4, 0), value) for n, value in enumerate(pieces)]


def early_unpack(expand_out, shrink_out):
    def unpack(out):
        def step(n, _):
            p, z = n // 4, n % 4
            band = pl.ds(pl.multiple_of(p * 16, 16), 16)
            rows = pl.ds(pl.multiple_of(n * 16, 16), 16)
            for hi in range(2):
                for y in range(4):
                    value = out[hi, z, y, band, :]
                    left = hi * 1536 + y * 384
                    expand_out[rows, left : left + 384] = value[:, 0:384]
                    below = pl.ds(pl.multiple_of(n * 64 + y * 16, 16), 16)
                    shrink_out[below, hi * 384 : hi * 384 + 384] = value[:, 384:768]
            return 0

        lax.fori_loop(0, 12, step, 0)

    return unpack


def late_unpack(output_out, attend_out):
    def unpack(out):
        def step(n, _):
            p, z = n // 4, n % 4
            band = pl.ds(pl.multiple_of(p * 16, 16), 16)
            rows = pl.ds(pl.multiple_of(n * 16, 16), 16)
            for m in range(8):
                value = out[m // 4, z, m % 4, band, :]
                if m < 2:
                    output_out[rows, m * 384 : m * 384 + 384] = value
                else:
                    attend_out[rows, (m - 2) * 384 : (m - 1) * 384] = value
            return 0

        lax.fori_loop(0, 12, step, 0)

    return unpack


REDUCE_STEPS = ((1, 0), (4, 1), (5, 2), (5.5, 3), (6, 4), (6.5, 5), (8, None))
EARLY_HALVES = ((4, 16, 3072), (4, 4, 16, 768))
LATE_HALVES = ((4, 16, 768), (4, 16, 2304))


def attend_back_kernel(
    len_ref, x_ref, o_ref, lse_ref, grad_ref, expand_src, shrink_src, small_src,
    grads, expand_out, shrink_out, small_out, *refs,
):
    attention, sems, refs = refs[:10], refs[10:16], refs[16:]
    pairs, scratch = Reduce.unflatten(refs, 2)
    small_out[...] = small_src[...]
    reduce = Reduce(
        place(), 768, [(source, *pair) for source, pair in zip((expand_src, shrink_src), pairs)],
        lambda p, acc: merge_blocks(p, pairs, acc, early_blocks), early_unpack(expand_out, shrink_out),
        small_out, scratch,
    )
    greet_all(reduce.neighbours(), owners=True)
    body = attend_back_body(
        len_ref, x_ref, o_ref, lse_ref, grad_ref, grads, *attention, sems, q_rows=512, k_rows=512, streams=2,
        after=[
            (end, (lambda: None) if number is None else functools.partial(reduce.step, number))
            for end, number in REDUCE_STEPS
        ],
    )
    next(body)
    reduce.start()
    next(body)
    reduce.step(6)
    reduce.finish()
    for _ in body:
        pass


def attend_back(valid, packed, mixed, lse, grad_mixed, expand_term, shrink_term, small, collective_id):
    vmem, anywhere = pl.BlockSpec(memory_space=pltpu.VMEM), pl.BlockSpec(memory_space=pl.ANY)
    return pl.pallas_call(
        attend_back_kernel,
        out_shape=(
            jax.ShapeDtypeStruct((3, HEADS, 64, 2 * SPAN), bf16),
            jax.ShapeDtypeStruct((192, 3072), bf16),
            jax.ShapeDtypeStruct((768, 768), bf16),
            jax.ShapeDtypeStruct(small.shape, f32),
        ),
        in_specs=[pl.BlockSpec(memory_space=pltpu.SMEM)] + [vmem] * 4 + [anywhere] * 2 + [vmem],
        out_specs=[vmem] * 4,
        scratch_shapes=[
            pltpu.VMEM((OWNERS, 64, SPAN), bf16),
            pltpu.VMEM((OWNERS, 3, 64, SPAN), bf16),
            pltpu.VMEM((128, LEN), bf16),
            pltpu.VMEM((LEN, 128), bf16),
            pltpu.VMEM((LEN, 128), bf16),
            pltpu.VMEM((64, LEN), bf16),
            pltpu.VMEM((LEN, 128), bf16),
            pltpu.VMEM((128, LEN), bf16),
            pltpu.VMEM((LEN, 128), bf16),
            pltpu.VMEM((64, LEN), f32),
        ] + exchange_sems(1) * 3 + Reduce.scratch(768, EARLY_HALVES, small.shape[0]),
        compiler_params=pltpu.CompilerParams(
            collective_id=collective_id, has_side_effects=True, vmem_limit_bytes=VMEM_BYTES
        ),
        name="attend_back",
    )(
        valid, packed, mixed, lse, grad_mixed, expand_term.reshape(2, 2, 3, 4, 16, 3072),
        shrink_term.reshape(2, 2, 3, 4, 4, 16, 768), small,
    )


def late_kernel(output_src, attend_src, small_src, output_out, attend_out, small_out, *refs):
    pairs, scratch = Reduce.unflatten(refs, 2)
    small_out[...] = small_src[...]
    reduce = Reduce(
        place(), 384, [(source, *pair) for source, pair in zip((output_src, attend_src), pairs)],
        lambda p, acc: merge_blocks(p, pairs, acc, late_blocks), late_unpack(output_out, attend_out),
        small_out, scratch,
    )
    greet_all(reduce.neighbours())
    reduce.start()
    for number in range(7):
        reduce.step(number)
    reduce.finish()


def late_reduce(output_term, attend_term, small, collective_id):
    vmem, anywhere = pl.BlockSpec(memory_space=pltpu.VMEM), pl.BlockSpec(memory_space=pl.ANY)
    return pl.pallas_call(
        late_kernel,
        out_shape=(
            jax.ShapeDtypeStruct((192, 768), bf16),
            jax.ShapeDtypeStruct((192, 2304), bf16),
            jax.ShapeDtypeStruct(small.shape, f32),
        ),
        in_specs=[anywhere] * 2 + [vmem],
        out_specs=[vmem] * 3,
        scratch_shapes=Reduce.scratch(384, LATE_HALVES, small.shape[0]),
        compiler_params=pltpu.CompilerParams(
            collective_id=collective_id, has_side_effects=True, vmem_limit_bytes=VMEM_BYTES
        ),
        name="late_reduce",
    )(output_term.reshape(2, 2, 3, 4, 16, 768), attend_term.reshape(2, 2, 3, 4, 16, 2304), small)


def per_device(
    inputs, lengths, attend_weight, query_bias, value_bias, output_weight, output_bias, norm_gain, norm_shift,
    expand_weight, expand_bias, shrink_weight, shrink_bias, final_gain, final_shift, cotangent,
):
    ctx, wt = lax.axis_index("ctx"), lax.axis_index("wt")
    vectors = (
        query_bias, value_bias, output_bias, norm_gain, norm_shift, expand_bias, shrink_bias, final_gain, final_shift,
    )
    seq_count, tok_local, model_width = inputs.shape
    row_count = seq_count * tok_local
    tokens = inputs.reshape(row_count, model_width)
    tokens_low = tokens.astype(bf16)
    seq, _, holds = head_of(ctx)
    my_length = jnp.where(holds, lengths[seq], 0).astype(jnp.int32).reshape(1)
    held, mixed_heads, lse, mixed, attend_full, small_full, output_full, expand_full, shrink_full = forward(
        my_length, tokens, attend_weight, vectors, (output_weight, expand_weight, shrink_weight), 0
    )
    mixed_low = mixed.reshape(model_width, row_count)
    small_full = small_full.reshape(4, 32, 768).astype(f32)
    _, _, output_add, gain_one, shift_one, expand_add, shrink_add, gain_two, shift_two = [
        small_full[:, n, : v.shape[0]].reshape(-1) for n, v in enumerate(vectors)
    ]

    attended = contract(mixed_low, output_full, 0, 0) + output_add
    hidden_one = tokens + attended
    normed_one = layer_norm(hidden_one, gain_one, shift_one)
    normed_low = normed_one.astype(bf16)
    raised = dot(normed_low, expand_full) + expand_add
    activated = exact_gelu(raised).astype(bf16)
    branch = dot(activated, shrink_full) + shrink_add
    hidden_two = normed_one + branch
    result = layer_norm(hidden_two, gain_two, shift_two)

    upstream = cotangent.reshape(row_count, model_width)
    grad_two, final_gain_term, final_shift_term = norm_pullback(hidden_two, gain_two, upstream)
    branch_low = grad_two.astype(bf16)
    shrink_bias_term = jnp.sum(branch_low.astype(f32), axis=0)
    shrink_term = contract(activated, branch_low, 0, 0)
    grad_active = contract(branch_low, shrink_full, 1, 1)
    _, gelu_pull = jax.vjp(exact_gelu, raised)
    raised_low = gelu_pull(grad_active)[0].astype(bf16)
    expand_bias_term = jnp.sum(raised_low.astype(f32), axis=0)
    expand_term = contract(normed_low, raised_low, 0, 0)
    grad_normed = grad_two + contract(raised_low, expand_full, 1, 1)
    grad_one, norm_gain_term, norm_shift_term = norm_pullback(hidden_one, gain_one, grad_normed)
    attended_low = grad_one.astype(bf16)
    output_bias_term = jnp.sum(attended_low.astype(f32), axis=0)
    output_term = dot(mixed_low, attended_low)
    grad_mixed = contract(output_full, attended_low, 1, 1).astype(bf16)

    early = jnp.concatenate(
        [t.reshape(4, -1) for t in (
            output_bias_term, norm_gain_term, norm_shift_term, expand_bias_term, shrink_bias_term,
            final_gain_term, final_shift_term)] + [jnp.zeros((4, 128), f32)], axis=1,
    ).reshape(64, 128)
    grad_packed, expand_grad, shrink_grad, early = attend_back(
        my_length, held, mixed_heads, lse, grad_mixed.reshape(HEADS, 64, row_count), expand_term.astype(bf16), shrink_term.astype(bf16), early, 1
    )
    grad_packed = grad_packed.reshape(3 * model_width, row_count)
    attend_term = contract(tokens_low, grad_packed, 0, 1)
    input_grad = grad_one + contract(grad_packed, attend_full, 0, 1)
    query_bias_term = jnp.sum(grad_packed[:model_width].astype(f32), axis=1)
    value_bias_term = jnp.sum(grad_packed[2 * model_width :].astype(f32), axis=1)

    late = jnp.concatenate(
        [t.reshape(4, -1) for t in (query_bias_term, value_bias_term)] + [jnp.zeros((4, 128), f32)], axis=1
    ).reshape(16, 128)
    output_grad, attend_grad, late = late_reduce(output_term.astype(bf16), attend_term.astype(bf16), late, 2)
    early = lax.dynamic_index_in_dim(early.reshape(4, 2048), wt, 0, keepdims=False)
    late = lax.dynamic_index_in_dim(late.reshape(4, 512), wt, 0, keepdims=False)
    n = 192
    return (
        result.reshape(inputs.shape),
        input_grad.reshape(inputs.shape),
        attend_grad.astype(f32),
        late[:n],
        late[n : 2 * n],
        output_grad.astype(f32),
        early[0:n],
        early[n : 2 * n],
        early[2 * n : 3 * n],
        expand_grad.astype(f32),
        early[3 * n : 7 * n],
        shrink_grad.astype(f32),
        early[7 * n : 8 * n],
        early[8 * n : 9 * n],
        early[9 * n : 10 * n],
    )


def solution(mesh):
    wide, rows, flat = P("wt", "ctx", None), P("wt", None), P("wt")
    return jax.shard_map(
        per_device,
        mesh=mesh,
        in_specs=(
            wide, flat, rows, flat, flat, rows, flat, flat, flat, rows, flat, rows, flat, flat, flat, wide,
        ),
        out_specs=(
            wide, wide, rows, flat, flat, rows, flat, flat, flat, rows, flat, rows, flat, flat, flat,
        ),
        check_vma=False,
    )
```
